32 devices in a mesh: mod: 8 (over z, y), rep: 4 (over x, core).
Axes of the slice: x: 2, y: 2, z: 4, core: 2. Of those that a mesh axis runs over, the one named last changes fastest.
Arguments:
- raw_rows: bfloat16 [64, 384, 768], P('mod', 'rep'), may hold values from -6 to 6
- recv_counts: int32 [8, 32], P('mod', 'rep'), may hold values from 0 to 96, as said below
- slot_groups: int32 [8, 3072], P('mod', 'rep'), may hold values from 0 to 4, as said below
- read_counts: int32 [8, 4], P('mod', 'rep'), may hold values from 1 to 4, as said below
- patch_convolution_weight: bfloat16 [768, 768], replicated, may hold values from -0.21875 to 0.21875
- patch_stem_bias_vector: float32 [768], replicated, may hold values from -3 to 3
- language_projection_weight: bfloat16 [768, 768], replicated, may hold values from -0.21875 to 0.21875
- language_bias_vector: float32 [768], replicated, may hold values from -3 to 3
- readout_table: float32 [8, 768], replicated, may hold values from -6 to 6
- attn_gain: float32 [768], replicated, may hold values from 0.5 to 1.5
- attn_bias: float32 [768], replicated, may hold values from -2 to 2
- qkv_weight: bfloat16 [768, 2304], P('mod'), may hold values from -0.21875 to 0.21875
- out_weight: bfloat16 [768, 768], P('mod'), may hold values from -0.875 to 0.875
- mlp_gain: float32 [768], replicated, may hold values from 0.5 to 1.5
- mlp_bias: float32 [768], replicated, may hold values from -2 to 2
- up_weight: bfloat16 [768, 3072], P('mod'), may hold values from -0.21875 to 0.21875
- up_bias: float32 [3072], replicated, may hold values from -2 to 2
- down_weight: bfloat16 [3072, 768], P('mod'), may hold values from -0.109375 to 0.109375
- down_bias: float32 [768], replicated, may hold values from -2 to 2
- out_cotangent: bfloat16 [8, 3104, 768], P('mod', 'rep'), may hold values from -6 to 6
Outputs:
- layer_out: bfloat16 [8, 3104, 768], P('mod', 'rep')
- raw_grad: float32 [64, 384, 768], P('mod', 'rep')
- patch_weight_grad: float32 [768, 768], replicated
- patch_bias_grad: float32 [768], replicated
- lang_weight_grad: float32 [768, 768], replicated
- lang_bias_grad: float32 [768], replicated
- readout_grad: float32 [8, 768], replicated
- attn_gain_grad: float32 [768], replicated
- attn_bias_grad: float32 [768], replicated
- qkv_weight_grad: float32 [768, 2304], P('mod')
- out_weight_grad: float32 [768, 768], P('mod')
- mlp_gain_grad: float32 [768], replicated
- mlp_bias_grad: float32 [768], replicated
- up_weight_grad: float32 [768, 3072], P('mod')
- up_bias_grad: float32 [3072], replicated
- down_weight_grad: float32 [3072, 768], P('mod')
- down_bias_grad: float32 [768], replicated
The draws below stay inside these ranges and needn't reach their ends.
Inputs may be any that keep to these rules, and one draw needn't show every extreme that they name: `recv_counts`: every sequence receives a full block of 96 live rows from device 0 of mod. `slot_groups`: even values: 0 for language tokens, 2 (t + 1) for observation tokens of time step t. `read_counts`: some sequence has 4.
All inputs are finite; a program needn't handle non-finite values.
Results may differ from the reference program's by a relative error of at most 0.017.
Values may be sent and summed in bfloat16 or wider, within the bound.
No kernel may reach another device: no remote copies, remote signals or barrier semaphores. Data moves between devices by JAX's collectives and lax.ppermute only.
A program may use at most 192 MiB of HBM per device.

```python
import jax
import jax.numpy as jnp
from jax import lax

D = 768
HEADS = 12
HD = 64
FF = 3072
RAW = 768
TIME = 2
RPS = 4
CAP = 768
RD = 8
BLK = 96
SEQ = 776
N_MOD = 8
N_REP = 4


def draw_recv_counts(key, part):
    key = jax.random.fold_in(key, 11)
    subkeys = jax.random.split(key, 3)
    primary = jax.random.randint(subkeys[0], (N_MOD, N_REP, N_MOD), BLK // 2, BLK + 1)
    wrist_on = jax.random.randint(subkeys[1], (N_MOD, N_REP, 1), 0, 2)
    language = jax.random.randint(subkeys[2], (N_MOD, N_REP, N_MOD), 1, BLK + 1)
    source = jnp.arange(N_MOD)[None, None, :]
    counts = jnp.where(source < N_MOD // 2, primary, jnp.where(source < 3 * N_MOD // 4, primary * wrist_on, language))
    counts = jnp.where(source == 0, BLK, counts)
    return counts.reshape(N_MOD, N_REP * N_MOD).astype(jnp.int32)


def draw_slot_groups(key, part):
    key = jax.random.fold_in(key, 12)
    time_step = jax.random.randint(key, (N_MOD, N_REP, N_MOD, BLK), 0, TIME)
    source = jnp.arange(N_MOD)[None, None, :, None]
    groups = jnp.where(source < 3 * N_MOD // 4, 2 * (time_step + 1), 0)
    return groups.reshape(N_MOD, N_REP * CAP).astype(jnp.int32)


def draw_read_counts(key, part):
    key = jax.random.fold_in(key, 13)
    drawn = jax.random.randint(key, (N_MOD, N_REP), 1, RPS + 1)
    first = (jnp.arange(N_MOD)[:, None] == 0) & (jnp.arange(N_REP)[None, :] == 0)
    return jnp.where(first, RPS, drawn).astype(jnp.int32)


def levels(stream_key, extent, cuts, smallest, high):
    level, own = 1.0, jax.random.fold_in(stream_key, 6)
    for position, parts in cuts:
        steps = jnp.exp(jax.random.uniform(jax.random.fold_in(own, position), (parts,), jnp.float32, smallest / len(cuts), high / len(cuts)))
        level = level * jnp.repeat(steps, extent[position] // parts).reshape([-1 if axis == position else 1 for axis in range(len(extent))])
    return level


def normal_values(own_key, dims, spread, bound, cuts=(), kind=jnp.bfloat16):
    array = jax.random.normal(own_key, dims, jnp.float32) * spread
    if len(cuts) > 0:
        array = levels(own_key, dims, cuts, -0.22, 0.18) * array
    return jnp.clip(array, min=-bound, max=bound).astype(kind)


def setup_inputs(seed: int = 0) -> dict:
    splits = jax.random.split(jax.random.key(seed), 21)
    raw_rows = normal_values(splits[0], (N_MOD * N_MOD, N_REP * BLK, RAW), 1.0, 6.0, ((0, 8), (1, 4)))
    recv_counts = draw_recv_counts(jax.random.fold_in(splits[20], 71), 0)
    slot_groups = draw_slot_groups(jax.random.fold_in(splits[20], 71), 0)
    read_counts = draw_read_counts(jax.random.fold_in(splits[20], 71), 0)
    patch_convolution_weight = normal_values(splits[4], (RAW, D), RAW ** -0.5, 0.21875)
    patch_stem_bias_vector = normal_values(splits[5], (D,), 0.5, 3.0, (), jnp.float32)
    language_projection_weight = normal_values(splits[6], (RAW, D), RAW ** -0.5, 0.21875)
    language_bias_vector = normal_values(splits[7], (D,), 0.5, 3.0, (), jnp.float32)
    readout_table = normal_values(splits[8], (RD, D), 1.0, 6.0, (), jnp.float32)
    attn_gain = jnp.clip(1.0 + 0.1 * jax.random.normal(splits[9], (D,), jnp.float32), 0.5, 1.5)
    attn_bias = normal_values(splits[10], (D,), 0.3, 2.0, (), jnp.float32)
    qkv_weight = normal_values(splits[11], (D, 3 * D), D ** -0.5, 0.21875, ((0, 8),))
    out_weight = normal_values(splits[12], (D, D), (D // 16) ** -0.5, 0.875, ((0, 8),))
    mlp_gain = jnp.clip(1.0 + 0.1 * jax.random.normal(splits[13], (D,), jnp.float32), 0.5, 1.5)
    mlp_bias = normal_values(splits[14], (D,), 0.3, 2.0, (), jnp.float32)
    up_weight = normal_values(splits[15], (D, FF), D ** -0.5, 0.21875, ((0, 8),))
    up_bias = normal_values(splits[16], (FF,), 0.3, 2.0, (), jnp.float32)
    down_weight = normal_values(splits[17], (FF, D), FF ** -0.5, 0.109375, ((0, 8),))
    down_bias = normal_values(splits[18], (D,), 0.3, 2.0, (), jnp.float32)
    out_cotangent = normal_values(splits[19], (N_MOD, N_REP * SEQ, D), 1.0, 6.0, ((0, 8), (1, 4)))
    return {"raw_rows": raw_rows, "recv_counts": recv_counts, "slot_groups": slot_groups, "read_counts": read_counts, "patch_convolution_weight": patch_convolution_weight, "patch_stem_bias_vector": patch_stem_bias_vector, "language_projection_weight": language_projection_weight, "language_bias_vector": language_bias_vector, "readout_table": readout_table, "attn_gain": attn_gain, "attn_bias": attn_bias, "qkv_weight": qkv_weight, "out_weight": out_weight, "mlp_gain": mlp_gain, "mlp_bias": mlp_bias, "up_weight": up_weight, "up_bias": up_bias, "down_weight": down_weight, "down_bias": down_bias, "out_cotangent": out_cotangent}


@jax.custom_vjp
def low(v):
    return lax.optimization_barrier(v.astype(jnp.bfloat16)).astype(jnp.float32)

@jax.custom_vjp
def low_back(v):
    return v

def low_keep(v):
    return (low(v), None)

def low_pass(kept, grad):
    return (grad,)

def back_keep(v):
    return (v, None)

def back_low(kept, grad):
    return (low(grad),)
low.defvjp(low_keep, low_pass)
low_back.defvjp(back_keep, back_low)
layer_eps = 1e-06
highest_precision_mode = lax.Precision.HIGHEST

def layer_norm(stream, norm_gain, norm_bias):
    row_mean = lax.optimization_barrier(jnp.mean(stream, axis=-1, keepdims=True))
    centred = stream - row_mean
    row_var = lax.optimization_barrier(jnp.mean(centred * centred, axis=-1, keepdims=True))
    return centred * lax.rsqrt(row_var + layer_eps) * norm_gain + norm_bias

def visibility(group_id, live_slot):
    key_group = group_id[None, :]
    query_group = group_id[:, None]
    visible = live_slot[None, :] & (key_group <= query_group) & ((key_group % 2 == 0) | (key_group == query_group))
    return visible | jnp.eye(group_id.shape[0], dtype=jnp.bool_)

def sequence_forward(params, unprocessed_block, counts, groups, read_count):
    patch_convolution_weight, patch_stem_bias_vector, language_projection_weight, language_bias_vector, readout_table, attn_gain, attn_bias, qkv_weight, out_weight, mlp_gain, mlp_bias, up_weight, up_bias, down_weight, down_bias = params
    is_image = (jnp.arange(N_MOD).astype(jnp.int32) < 3 * N_MOD // 4)[:, None, None]
    patch_embedding = jnp.einsum('xzu,ul->xzl', unprocessed_block, patch_convolution_weight, precision=highest_precision_mode) + patch_stem_bias_vector
    language_embedding = jnp.einsum('xzu,ul->xzl', unprocessed_block, language_projection_weight, precision=highest_precision_mode) + language_bias_vector
    embedded = low_back(low(jnp.where(is_image, patch_embedding, language_embedding))).reshape(CAP, D)
    stream = jnp.concatenate([embedded, readout_table], axis=0)
    slot_index = jnp.arange(CAP).astype(jnp.int32)
    live_recv = slot_index % BLK < counts[slot_index // BLK]
    readout_slot = jnp.arange(RD).astype(jnp.int32)
    live_read = readout_slot % RPS < read_count
    live_slot = jnp.concatenate([live_recv, live_read])
    read_group = (2 * (readout_slot // RPS + 1) + 1).astype(jnp.int32)
    group_id = jnp.concatenate([groups.astype(jnp.int32), read_group])
    visible = visibility(group_id, live_slot)
    normed = low(layer_norm(stream, attn_gain, attn_bias))
    qkv_rows = low_back(low(jnp.dot(normed, qkv_weight, precision=highest_precision_mode)))
    queries = qkv_rows[:, :D].reshape(SEQ, HEADS, HD)
    key_rows = qkv_rows[:, D:2 * D].reshape(SEQ, HEADS, HD)
    values = qkv_rows[:, 2 * D:].reshape(SEQ, HEADS, HD)
    scores = low_back(jnp.einsum('qhe,khe->hqk', queries, key_rows, precision=highest_precision_mode) * HD ** (-0.5))
    scores = jnp.where(visible[None], scores, -1e+30)
    row_peak = lax.optimization_barrier(jnp.max(scores, axis=-1, keepdims=True))
    exponent = jnp.exp(scores - row_peak)
    attn_probs = low(exponent / lax.optimization_barrier(jnp.sum(exponent, axis=-1, keepdims=True)))
    mixed_rows = jnp.einsum('hqk,khe->qhe', attn_probs, values, precision=highest_precision_mode).reshape(SEQ, D)
    mixed_rows = low_back(low(mixed_rows))
    attn_branch = low_back(jnp.dot(mixed_rows, out_weight, precision=highest_precision_mode))
    after_attn = stream + attn_branch
    normed2 = low(layer_norm(after_attn, mlp_gain, mlp_bias))
    hidden_pre = low_back(jnp.dot(normed2, up_weight, precision=highest_precision_mode) + up_bias)
    activated = low(jax.nn.gelu(hidden_pre))
    branch = low_back(jnp.dot(activated, down_weight, precision=highest_precision_mode) + down_bias)
    return (after_attn + branch) * live_slot.astype(jnp.float32)[:, None]

def reference(raw_rows, recv_counts, slot_groups, read_counts, patch_convolution_weight, patch_stem_bias_vector, language_projection_weight, language_bias_vector, readout_table, attn_gain, attn_bias, qkv_weight, out_weight, mlp_gain, mlp_bias, up_weight, up_bias, down_weight, down_bias, out_cotangent):
    seq_count = N_MOD * N_REP
    raw_seq = raw_rows.astype(jnp.float32).reshape(N_MOD, N_MOD, N_REP, BLK, RAW)
    raw_seq = raw_seq.transpose(1, 2, 0, 3, 4).reshape(seq_count, N_MOD, BLK, RAW)
    counts_all = recv_counts.reshape(seq_count, N_MOD)
    groups_all = slot_groups.reshape(seq_count, CAP)
    reads_all = read_counts.reshape(seq_count)
    cotangent = out_cotangent.astype(jnp.float32).reshape(seq_count, SEQ, D)
    params = tuple((item.astype(jnp.float32) for item in (patch_convolution_weight, patch_stem_bias_vector, language_projection_weight, language_bias_vector, readout_table, attn_gain, attn_bias, qkv_weight, out_weight, mlp_gain, mlp_bias, up_weight, up_bias, down_weight, down_bias)))
    checkpointed = jax.checkpoint(sequence_forward)

    def forward(weights, raw_all):

        def step(carry, inputs):
            unprocessed_block, counts, groups, read_count = inputs
            return (carry, checkpointed(weights, unprocessed_block, counts, groups, read_count))
        _, outputs = lax.scan(step, jnp.zeros((), jnp.float32), (raw_all, counts_all, groups_all, reads_all))
        return outputs
    outputs, pullback = jax.vjp(forward, params, raw_seq)
    param_grads, raw_grads = pullback(cotangent)
    layer_out = outputs.reshape(N_MOD, N_REP * SEQ, D).astype(jnp.bfloat16)
    raw_grad = raw_grads.reshape(N_MOD, N_REP, N_MOD, BLK, RAW).transpose(2, 0, 1, 3, 4)
    raw_grad = raw_grad.reshape(N_MOD * N_MOD, N_REP * BLK, RAW)
    patch_weight_grad, patch_bias_grad, lang_weight_grad, lang_bias_grad, readout_grad, attn_gain_grad, attn_bias_grad, qkv_weight_grad, out_weight_grad, mlp_gain_grad, mlp_bias_grad, up_weight_grad, up_bias_grad, down_weight_grad, down_bias_grad = param_grads
    return (layer_out, raw_grad, patch_weight_grad, patch_bias_grad, lang_weight_grad, lang_bias_grad, readout_grad, attn_gain_grad, attn_bias_grad, qkv_weight_grad, out_weight_grad, mlp_gain_grad, mlp_bias_grad, up_weight_grad, up_bias_grad, down_weight_grad, down_bias_grad)
```

```python
import functools

import jax
import jax.numpy as jnp
from jax import lax
from jax.experimental import pallas as pl
from jax.experimental.pallas import tpu as pltpu
from jax.sharding import PartitionSpec as P

D = 768
HEADS = 12
HD = 64
RPS = 4
RD = 8
PAD = 16
LANES = 128
CHUNK = 256
FB = 256
EPS = 1e-6
NEG = -1e30
F32 = jnp.float32
BF16 = jnp.bfloat16
AXES = ("mod", "rep")
SCALE = HD ** (-0.5)
VMEM = pl.BlockSpec(memory_space=pltpu.VMEM)
SMEM = pl.BlockSpec(memory_space=pltpu.SMEM)


def nn(left, right):
    return lax.dot_general(left, right, (((1,), (0,)), ((), ())), preferred_element_type=F32)


def nt(left, right):
    return lax.dot_general(left, right, (((1,), (1,)), ((), ())), preferred_element_type=F32)


def tn(left, right):
    return lax.dot_general(left, right, (((0,), (0,)), ((), ())), preferred_element_type=F32)


def chunks(rows):
    count = rows // CHUNK
    return [
        (i * CHUNK, (rows - i * CHUNK) if i == count - 1 else CHUNK) for i in range(count)
    ]


def normalise(rows):
    mean = jnp.mean(rows, axis=-1, keepdims=True)
    centred = rows - mean
    var = jnp.mean(centred * centred, axis=-1, keepdims=True)
    rstd = lax.rsqrt(var + EPS)
    return centred * rstd, rstd


def norm_input_grad(xhat, rstd, gain, upstream):
    scaled = upstream * gain
    first = jnp.mean(scaled, axis=-1, keepdims=True)
    second = jnp.mean(scaled * xhat, axis=-1, keepdims=True)
    return rstd * (scaled - first - xhat * second)


def call(kernel, out_shape, **kw):
    limit = kw.pop("vmem", 56)
    cost = kw.pop("cost", None)
    return pl.pallas_call(
        kernel,
        out_shape=out_shape,
        cost_estimate=cost,
        compiler_params=pltpu.CompilerParams(vmem_limit_bytes=limit * 1024 * 1024),
        **kw,
    )


def cost(flops, nbytes):
    return pl.CostEstimate(flops=int(flops), bytes_accessed=int(nbytes), transcendentals=0)


def struct(shape, dtype):
    return jax.ShapeDtypeStruct(shape, dtype)


def live_of(index, counts, read, block_rows):
    groups_n = counts.shape[1]
    capacity = groups_n * block_rows
    live = index < 0
    for s in range(groups_n):
        live = live | ((index >= s * block_rows) & (index < s * block_rows + counts[0, s]))
    slot = index - capacity
    return live | ((slot >= 0) & (slot < RD) & (slot % RPS < read[0, 0]))


def stem_kernel(cut, raw, wp, bp, wl, bl, table, gain, bias, stream, normed):
    capacity = raw.shape[0]
    step = capacity // 4
    for start in range(0, capacity, step):
        weight, shift = (wp, bp) if start < cut else (wl, bl)
        rows = pl.ds(start, step)
        embedded = (nn(raw[rows, :], weight[...]) + shift[...]).astype(BF16).astype(F32)
        stream[rows, :] = embedded
        xhat, _ = normalise(embedded)
        normed[rows, :] = (xhat * gain[...] + bias[...]).astype(BF16)
    tail = jnp.concatenate([table[...], jnp.zeros((PAD - RD, D), F32)], axis=0)
    stream[pl.ds(capacity, PAD), :] = tail
    xhat, _ = normalise(tail)
    normed[pl.ds(capacity, PAD), :] = (xhat * gain[...] + bias[...]).astype(BF16)


def stems(raw, wp, bp, wl, bl, table, gain, bias):
    capacity = raw.shape[0]
    total = capacity + PAD
    return call(
        functools.partial(stem_kernel, 3 * capacity // 4),
        (struct((total, D), F32), struct((total, D), BF16)),
        in_specs=[VMEM] * 8,
        out_specs=(VMEM, VMEM),
        cost=cost(2 * capacity * D * D, 8 * capacity * D),
    )(raw, wp, bp, wl, bl, table, gain, bias)


def qkv_kernel(rows, weight, out):
    for start, size in chunks(rows.shape[0]):
        out[0, pl.ds(start, size), :] = nn(rows[pl.ds(start, size), :], weight[0]).astype(BF16)


def project_qkv(normed, weights):
    total = normed.shape[0]
    return call(
        qkv_kernel,
        struct((3, total, D), BF16),
        grid=(3,),
        in_specs=[
            pl.BlockSpec((total, D), lambda r: (0, 0)),
            pl.BlockSpec((1, D, D), lambda r: (r, 0, 0)),
        ],
        out_specs=pl.BlockSpec((1, total, D), lambda r: (r, 0, 0)),
        cost=cost(6 * total * D * D, 6 * D * D + 8 * total * D),
    )(normed, weights)


def visible_readout(group_row, live_row):
    capacity = group_row.shape[1]
    query = lax.broadcasted_iota(jnp.int32, (RD, capacity), 0)
    group = 2 * (query // RPS + 1) + 1
    keys = group_row[...]
    seen = live_row & (keys <= group) & ((keys % 2 == 0) | (keys == group))
    return jnp.where(seen, 0.0, NEG)


def visible_between(read):
    query = lax.broadcasted_iota(jnp.int32, (RD, PAD), 0)
    key = lax.broadcasted_iota(jnp.int32, (RD, PAD), 1)
    live = (key < RD) & (key % RPS < read[0, 0])
    seen = (query == key) | (live & (query // RPS == key // RPS))
    return jnp.where(seen, 0.0, NEG)


def tiled(rows):
    return jnp.concatenate([rows] * HEADS, axis=0)


def own_head():
    row = lax.broadcasted_iota(jnp.int32, (HEADS * RD, D), 0) // RD
    lane = lax.broadcasted_iota(jnp.int32, (HEADS * RD, D), 1) // HD
    return row == lane


def fold_heads(stack, mine):
    kept = jnp.where(mine, stack, 0.0)
    total = kept[:RD]
    for head in range(1, HEADS):
        total = total + kept[head * RD : (head + 1) * RD]
    return jnp.concatenate([total, jnp.zeros((PAD - RD, D), F32)], axis=0)


def attend_kernel(
    block_rows, qkv, counts, read, group_row, group_col, mixed, lse, lse_read, mask, lse_cols, tail
):
    step = pl.program_id(0)
    capacity = group_row.shape[1]

    @pl.when(step == 0)
    def _():
        slot_row = lax.broadcasted_iota(jnp.int32, (1, capacity), 1)
        live_row = live_of(slot_row, counts, read, block_rows)
        keys = group_row[...]
        for start in range(0, capacity, CHUNK):
            query = lax.broadcasted_iota(jnp.int32, (CHUNK, capacity), 0) + start
            group = group_col[pl.ds(start, CHUNK), :]
            seen = live_row & (keys <= group) & ((keys % 2 == 0) | (keys == group))
            seen = seen | (query == slot_row)
            mask[pl.ds(start, CHUNK), :] = jnp.where(seen, 0.0, NEG)
        lse_cols[...] = jnp.zeros_like(lse_cols)
        mine = own_head()
        tail_rows = pl.ds(capacity, PAD)
        head_rows = pl.ds(0, capacity)
        query = qkv[0, tail_rows, :].astype(F32)[:RD] * SCALE
        query = jnp.where(mine, tiled(query), 0.0).astype(BF16)
        far = nt(query, qkv[1, head_rows, :]) + tiled(visible_readout(group_row, live_row))
        near = nt(query, qkv[1, tail_rows, :]) + tiled(visible_between(read))
        peak = jnp.maximum(
            jnp.max(far, axis=1, keepdims=True), jnp.max(near, axis=1, keepdims=True)
        )
        far = jnp.exp(far - peak)
        near = jnp.exp(near - peak)
        total = jnp.sum(far, axis=1, keepdims=True) + jnp.sum(near, axis=1, keepdims=True)
        out = nn(far.astype(BF16), qkv[2, head_rows, :]) + nn(
            near.astype(BF16), qkv[2, tail_rows, :]
        )
        tail[...] = fold_heads(out / total, mine)
        lse_read[...] = jnp.broadcast_to(peak + jnp.log(total), lse_read.shape)

    lane = lax.broadcasted_iota(jnp.int32, (1, LANES), 1)
    columns = pl.ds(pl.multiple_of(step * LANES, LANES), LANES)
    keys = qkv[1, pl.ds(0, capacity), columns]
    values = qkv[2, pl.ds(0, capacity), columns]
    for start in range(0, capacity, CHUNK):
        rows = pl.ds(start, CHUNK)
        query = qkv[0, rows, columns] * SCALE
        outs = []
        logs = lse_cols[rows, :]
        for head in range(2):
            chosen = jnp.where(lane // HD == head, query, jnp.zeros_like(query))
            scores = nt(chosen.astype(BF16), keys) + mask[rows, :]
            peak = jnp.max(scores, axis=1, keepdims=True)
            weight = jnp.exp(scores - peak)
            total = jnp.sum(weight, axis=1, keepdims=True)
            outs.append(nn(weight.astype(BF16), values) / total)
            logs = jnp.where(lane == 2 * step + head, peak + jnp.log(total), logs)
        mixed[rows, :] = jnp.where(lane < HD, outs[0], outs[1]).astype(BF16)
        lse_cols[rows, :] = logs
    mixed[pl.ds(capacity, PAD), :] = tail[:, columns].astype(BF16)

    @pl.when(step == pl.num_programs(0) - 1)
    def _():
        lse[...] = lse_cols[...].T[: lse.shape[0], :]


def attend(qkv, counts, read, group_row, group_col, block_rows):
    total = qkv.shape[1]
    capacity = total - PAD
    pairs = HEADS // 2
    return call(
        functools.partial(attend_kernel, block_rows),
        (
            struct((total, D), BF16),
            struct((16, capacity), F32),
            struct((HEADS * RD, LANES), F32),
        ),
        grid=(pairs,),
        in_specs=[VMEM, SMEM, SMEM, VMEM, VMEM],
        out_specs=(pl.BlockSpec((total, LANES), lambda j: (0, j)), VMEM, VMEM),
        scratch_shapes=[
            pltpu.VMEM((capacity, capacity), F32),
            pltpu.VMEM((capacity, LANES), F32),
            pltpu.VMEM((PAD, D), F32),
        ],
        cost=cost(4 * HEADS * capacity * capacity * 256, 8 * total * D),
    )(qkv, counts, read, group_row, group_col)


def attend_back_kernel(
    block_rows,
    qkv,
    mixed,
    grad,
    lse,
    lse_read,
    counts,
    read,
    group_row,
    group_col,
    out,
    mask,
    delta,
    key_more,
    value_more,
    tails,
):
    step = pl.program_id(0)
    capacity = group_row.shape[1]
    tail_rows = pl.ds(capacity, PAD)
    head_rows = pl.ds(0, capacity)

    @pl.when(step == 0)
    def _():
        slot_row = lax.broadcasted_iota(jnp.int32, (1, capacity), 1)
        group = group_row[...]
        for start in range(0, capacity, CHUNK):
            slot = lax.broadcasted_iota(jnp.int32, (CHUNK, 1), 0) + start
            live = live_of(slot, counts, read, block_rows)
            keys = group_col[pl.ds(start, CHUNK), :]
            seen = live & (keys <= group) & ((keys % 2 == 0) | (keys == group))
            seen = seen | (slot == slot_row)
            mask[pl.ds(start, CHUNK), :] = jnp.where(seen, 0.0, NEG)
        head = lax.broadcasted_iota(jnp.int32, (16, D), 0)
        column = lax.broadcasted_iota(jnp.int32, (16, D), 1)
        select = jnp.where(column // HD == head, 1.0, 0.0).astype(BF16)
        for start in range(0, capacity, CHUNK):
            rows = pl.ds(start, CHUNK)
            product = grad[rows, :].astype(F32) * mixed[rows, :].astype(F32)
            high = product.astype(BF16)
            low = (product - high.astype(F32)).astype(BF16)
            delta[:, rows] = nt(select, high) + nt(select, low)

        live_row = live_of(slot_row, counts, read, block_rows)
        mine = own_head()
        query = qkv[0, tail_rows, :].astype(F32)[:RD] * SCALE
        query = jnp.where(mine, tiled(query), 0.0).astype(BF16)
        upper = grad[tail_rows, :].astype(F32)[:RD]
        upper = jnp.where(mine, tiled(upper), 0.0)
        result = tiled(mixed[tail_rows, :].astype(F32)[:RD])
        row_delta = jnp.sum(upper * result, axis=1, keepdims=True)
        upper = upper.astype(BF16)
        logs = lse_read[:, 0:1]
        far = nt(query, qkv[1, head_rows, :]) + tiled(visible_readout(group_row, live_row))
        near = nt(query, qkv[1, tail_rows, :]) + tiled(visible_between(read))
        far = jnp.exp(far - logs)
        near = jnp.exp(near - logs)
        far_grad = (far * (nt(upper, qkv[2, head_rows, :]) - row_delta)).astype(BF16)
        near_grad = (near * (nt(upper, qkv[2, tail_rows, :]) - row_delta)).astype(BF16)
        query_grad = nn(far_grad, qkv[1, head_rows, :]) + nn(near_grad, qkv[1, tail_rows, :])
        tails[0] = fold_heads(query_grad, mine) * SCALE
        tails[1] = tn(near_grad, query)
        tails[2] = tn(near.astype(BF16), upper)
        key_more[...] = tn(far_grad, query)
        value_more[...] = tn(far.astype(BF16), upper)

    lane = lax.broadcasted_iota(jnp.int32, (1, LANES), 1)
    columns = pl.ds(pl.multiple_of(step * LANES, LANES), LANES)
    query = (qkv[0, head_rows, columns] * SCALE).astype(BF16)
    upper = grad[head_rows, columns]
    query_grad = jnp.zeros((capacity, LANES), F32)
    for start in range(0, capacity, CHUNK):
        rows = pl.ds(start, CHUNK)
        all_keys = qkv[1, rows, columns]
        all_values = qkv[2, rows, columns]
        key_parts = []
        value_parts = []
        for head in range(2):
            own = lane // HD == head
            keys = jnp.where(own, all_keys, jnp.zeros_like(all_keys))
            values = jnp.where(own, all_values, jnp.zeros_like(all_values))
            logs = lse[pl.ds(2 * step + head, 1), :]
            row_delta = delta[pl.ds(2 * step + head, 1), :]
            probs = jnp.exp(nt(keys, query) + mask[rows, :] - logs)
            score_grad = (probs * (nt(values, upper) - row_delta)).astype(BF16)
            value_parts.append(nn(probs.astype(BF16), upper))
            key_parts.append(nn(score_grad, query))
            query_grad = query_grad + tn(score_grad, keys)
        key_grad = jnp.where(lane < HD, key_parts[0], key_parts[1]) + key_more[rows, columns]
        value_grad = jnp.where(lane < HD, value_parts[0], value_parts[1]) + value_more[rows, columns]
        out[1, rows, :] = key_grad.astype(BF16)
        out[2, rows, :] = value_grad.astype(BF16)
    out[0, head_rows, :] = (query_grad * SCALE).astype(BF16)
    for part in range(3):
        out[part, tail_rows, :] = tails[part, :, columns].astype(BF16)


def attend_back(qkv, mixed, grad, lse, lse_read, counts, read, group_row, group_col, block_rows):
    total = qkv.shape[1]
    capacity = total - PAD
    pairs = HEADS // 2
    return call(
        functools.partial(attend_back_kernel, block_rows),
        struct((3, total, D), BF16),
        grid=(pairs,),
        in_specs=[VMEM, VMEM, VMEM, VMEM, VMEM, SMEM, SMEM, VMEM, VMEM],
        out_specs=pl.BlockSpec((3, total, LANES), lambda j: (0, 0, j)),
        scratch_shapes=[
            pltpu.VMEM((capacity, capacity), F32),
            pltpu.VMEM((16, capacity), F32),
            pltpu.VMEM((capacity, D), F32),
            pltpu.VMEM((capacity, D), F32),
            pltpu.VMEM((3, PAD, D), F32),
        ],
        cost=cost(10 * HEADS * capacity * capacity * 256, 16 * total * D),
    )(qkv, mixed, grad, lse, lse_read, counts, read, group_row, group_col)


def out_kernel(mixed, weight, stream, gain, bias, after, normed):
    for start, size in chunks(mixed.shape[0]):
        rows = pl.ds(start, size)
        value = stream[rows, :] + nn(mixed[rows, :], weight[0])
        after[rows, :] = value
        xhat, _ = normalise(value)
        normed[rows, :] = (xhat * gain[...] + bias[...]).astype(BF16)


def out_project(mixed, weights, stream, gain, bias):
    total = mixed.shape[0]
    whole = pl.BlockSpec((total, D), lambda i: (0, 0))
    vector = pl.BlockSpec((1, D), lambda i: (0, 0))
    return call(
        out_kernel,
        (struct((total, D), F32), struct((total, D), BF16)),
        grid=(1,),
        in_specs=[whole, pl.BlockSpec((1, D, D), lambda i: (3, 0, 0)), whole, vector, vector],
        out_specs=(whole, whole),
        cost=cost(2 * total * D * D, 12 * total * D),
    )(mixed, weights, stream, gain, bias)


def out_back_kernel(inner, after, branch, gain, weight, grad, grad_low, mixed_grad, gains, biases):
    gain_sum = jnp.zeros((1, D), F32)
    bias_sum = jnp.zeros((1, D), F32)
    for start, size in chunks(inner.shape[0]):
        rows = pl.ds(start, size)
        upstream = inner[rows, :]
        xhat, rstd = normalise(after[rows, :])
        gain_sum = gain_sum + jnp.sum(upstream * xhat, axis=0, keepdims=True)
        bias_sum = bias_sum + jnp.sum(upstream, axis=0, keepdims=True)
        total = branch[rows, :].astype(F32) + norm_input_grad(xhat, rstd, gain[...], upstream)
        grad[rows, :] = total
        low = total.astype(BF16)
        grad_low[rows, :] = low
        mixed_grad[rows, :] = nt(low, weight[0]).astype(BF16)
    gains[...] = gain_sum
    biases[...] = bias_sum


def out_back(inner, after, branch, gain, weights):
    total = inner.shape[0]
    whole = pl.BlockSpec((total, D), lambda i: (0, 0))
    vector = pl.BlockSpec((1, D), lambda i: (0, 0))
    return call(
        out_back_kernel,
        (
            struct((total, D), F32),
            struct((total, D), BF16),
            struct((total, D), BF16),
            struct((1, D), F32),
            struct((1, D), F32),
        ),
        grid=(1,),
        in_specs=[whole, whole, whole, vector, pl.BlockSpec((1, D, D), lambda i: (3, 0, 0))],
        out_specs=(whole, whole, whole, vector, vector),
        cost=cost(2 * total * D * D, 20 * total * D),
    )(inner, after, branch, gain, weights)


def mlp_kernel(
    block_rows,
    after,
    normed,
    cotangent,
    counts,
    read,
    up,
    up_bias,
    down,
    down_bias,
    layer_out,
    up_grad,
    down_grad,
    up_bias_grad,
    inner,
    branch,
    down_bias_grad,
    total_out,
    active,
    hidden_grad,
    live_col,
):
    step = pl.program_id(0)
    total = normed.shape[0]
    slots = cotangent.shape[0]

    @pl.when(step == 0)
    def _():
        index = lax.broadcasted_iota(jnp.int32, (total, 1), 0)
        live = jnp.where(live_of(index, counts, read, block_rows), 1.0, 0.0)
        live_col[...] = live
        upstream = cotangent[...].astype(F32) * live[:slots]
        upstream = jnp.concatenate([upstream, jnp.zeros((total - slots, D), F32)], axis=0)
        branch[...] = upstream.astype(BF16)
        down_bias_grad[...] = jnp.sum(upstream, axis=0, keepdims=True)
        inner[...] = jnp.zeros_like(inner)
        total_out[...] = after[...] + down_bias[...]

    bias_sum = jnp.zeros(up_bias.shape, F32)
    for start, size in chunks(total):
        rows = pl.ds(start, size)
        hidden = nn(normed[rows, :], up[0]) + up_bias[...]
        factor = (2.0 / jnp.pi) ** 0.5
        square = hidden * hidden
        bent = jnp.tanh(hidden * (factor + (factor * 0.044715) * square))
        half = 0.5 * (1.0 + bent)
        act = (hidden * half).astype(BF16)
        slope = half + (0.5 * hidden) * (1.0 - bent * bent) * (
            factor + (3.0 * factor * 0.044715) * square
        )
        back = (nt(branch[rows, :], down[...]) * slope).astype(BF16)
        bias_sum = bias_sum + jnp.sum(back.astype(F32), axis=0, keepdims=True)
        active[rows, :] = act
        hidden_grad[rows, :] = back
        total_out[rows, :] += nn(act, down[...])
        inner[rows, :] += nt(back, up[0])
    up_bias_grad[...] = bias_sum
    down_grad[...] = tn(active[...], branch[...]).astype(BF16)
    up_grad[0] = tn(normed[...], hidden_grad[...]).astype(BF16)

    @pl.when(step == pl.num_programs(0) - 1)
    def _():
        layer_out[...] = (total_out[...] * live_col[...])[:slots].astype(BF16)


def mlp(after, normed, cotangent, counts, read, up, up_bias, down, down_bias, block_rows):
    total = normed.shape[0]
    slots = cotangent.shape[0]
    hidden = up_bias.shape[1]
    per = D // FB
    whole = lambda rows: pl.BlockSpec((rows, D), lambda j: (0, 0))
    return call(
        functools.partial(mlp_kernel, block_rows),
        (
            struct((slots, D), BF16),
            struct((hidden // D, D, D), BF16),
            struct((hidden, D), BF16),
            struct((1, hidden), F32),
            struct((total, D), F32),
            struct((total, D), BF16),
            struct((1, D), F32),
        ),
        grid=(hidden // FB,),
        in_specs=[
            whole(total),
            whole(total),
            whole(slots),
            SMEM,
            SMEM,
            pl.BlockSpec((1, D, FB), lambda j: (j // per, 0, j % per)),
            pl.BlockSpec((1, FB), lambda j: (0, j)),
            pl.BlockSpec((FB, D), lambda j: (j, 0)),
            whole(1),
        ],
        out_specs=(
            whole(slots),
            pl.BlockSpec((1, D, FB), lambda j: (j // per, 0, j % per)),
            pl.BlockSpec((FB, D), lambda j: (j, 0)),
            pl.BlockSpec((1, FB), lambda j: (0, j)),
            whole(total),
            whole(total),
            whole(1),
        ),
        scratch_shapes=[
            pltpu.VMEM((total, D), F32),
            pltpu.VMEM((total, FB), BF16),
            pltpu.VMEM((total, FB), BF16),
            pltpu.VMEM((total, 1), F32),
        ],
        cost=cost(12 * total * D * hidden, 16 * D * hidden),
    )(after, normed, cotangent, counts, read, up, up_bias, down, down_bias)


def qkv_back_kernel(capacity, grads, weights, stream, gain, after_grad, embedded, readout, gains, biases):
    gain_sum = jnp.zeros((1, D), F32)
    bias_sum = jnp.zeros((1, D), F32)
    for start, size in chunks(stream.shape[0]):
        rows = pl.ds(start, size)
        upstream = (
            nt(grads[0, rows, :], weights[0])
            + nt(grads[1, rows, :], weights[1])
            + nt(grads[2, rows, :], weights[2])
        )
        xhat, rstd = normalise(stream[rows, :])
        gain_sum = gain_sum + jnp.sum(upstream * xhat, axis=0, keepdims=True)
        bias_sum = bias_sum + jnp.sum(upstream, axis=0, keepdims=True)
        total = after_grad[rows, :] + norm_input_grad(xhat, rstd, gain[...], upstream)
        inside = min(size, capacity - start)
        embedded[pl.ds(start, inside), :] = total[:inside].astype(BF16)
        if start + size > capacity:
            readout[...] = total[capacity - start : capacity - start + RD]
    gains[...] = gain_sum
    biases[...] = bias_sum


def qkv_back(grads, weights, stream, gain, after_grad):
    total = stream.shape[0]
    capacity = total - PAD
    whole = pl.BlockSpec((total, D), lambda i: (0, 0))
    vector = pl.BlockSpec((1, D), lambda i: (0, 0))
    return call(
        functools.partial(qkv_back_kernel, capacity),
        (
            struct((capacity, D), BF16),
            struct((RD, D), F32),
            struct((1, D), F32),
            struct((1, D), F32),
        ),
        grid=(1,),
        in_specs=[
            pl.BlockSpec((3, total, D), lambda i: (0, 0, 0)),
            pl.BlockSpec((3, D, D), lambda i: (0, 0, 0)),
            whole,
            vector,
            whole,
        ],
        out_specs=(
            pl.BlockSpec((capacity, D), lambda i: (0, 0)),
            pl.BlockSpec((RD, D), lambda i: (0, 0)),
            vector,
            vector,
        ),
        cost=cost(6 * total * D * D, 20 * total * D),
    )(grads, weights, stream, gain, after_grad)


def weight_kernel(normed, mixed, grads, attn_grad, out):
    step = pl.program_id(0)

    @pl.when(step < 3)
    def _():
        out[0] = tn(normed[...], grads[0]).astype(BF16)

    @pl.when(step == 3)
    def _():
        out[0] = tn(mixed[...], attn_grad[...]).astype(BF16)


def weight_grads(normed, mixed, grads, attn_grad):
    total = normed.shape[0]
    whole = pl.BlockSpec((total, D), lambda r: (0, 0))
    return call(
        weight_kernel,
        struct((4, D, D), BF16),
        grid=(4,),
        in_specs=[
            whole,
            whole,
            pl.BlockSpec((1, total, D), lambda r: (jnp.minimum(r, 2), 0, 0)),
            whole,
        ],
        out_specs=pl.BlockSpec((1, D, D), lambda r: (r, 0, 0)),
        cost=cost(8 * total * D * D, 8 * D * D + 12 * total * D),
    )(normed, mixed, grads, attn_grad)


def stem_back_kernel(cut, raw, embedded, out, patch_bias, lang_bias):
    out[0] = tn(raw[:cut, :], embedded[:cut, :]).astype(BF16)
    out[1] = tn(raw[cut:, :], embedded[cut:, :]).astype(BF16)
    patch_bias[...] = jnp.sum(embedded[:cut, :].astype(F32), axis=0, keepdims=True)
    lang_bias[...] = jnp.sum(embedded[cut:, :].astype(F32), axis=0, keepdims=True)


def stem_back(raw, embedded):
    capacity = raw.shape[0]
    return call(
        functools.partial(stem_back_kernel, 3 * capacity // 4),
        (struct((2, D, D), BF16), struct((1, D), F32), struct((1, D), F32)),
        in_specs=[VMEM, VMEM],
        out_specs=(VMEM, VMEM, VMEM),
        cost=cost(2 * capacity * D * D, 8 * capacity * D),
    )(raw, embedded)


def raw_kernel(image, grad, wp, wl, out):
    @pl.when(image[0] != 0)
    def _():
        out[...] = nt(grad[...], wp[...])

    @pl.when(image[0] == 0)
    def _():
        out[...] = nt(grad[...], wl[...])


def raw_back(image, grad, wp, wl):
    return call(
        raw_kernel,
        struct(grad.shape, F32),
        in_specs=[SMEM, VMEM, VMEM, VMEM],
        out_specs=VMEM,
        cost=cost(2 * grad.shape[0] * D * D, 6 * grad.shape[0] * D),
    )(image, grad, wp, wl)


class Grid:
    def __init__(self, mods, reps):
        self.mods, self.reps = mods, reps
        self.mod, self.rep = lax.axis_index("mod"), lax.axis_index("rep")

    def swap(self, value, mod=0, rep=0):
        pairs = [
            (m * self.reps + r, (m ^ mod) * self.reps + (r ^ rep))
            for m in range(self.mods)
            for r in range(self.reps)
        ]
        return lax.ppermute(value, AXES, pairs)

    def bit(self, mod=0, rep=0):
        return ((self.mod & mod) | (self.rep & rep)) != 0

    def joined(self, value, axis, **bit):
        other = self.swap(value, **bit)
        shape = [1] * (value.ndim + 1)
        shape[axis] = 2
        place = jnp.arange(2).reshape(shape) == self.bit(**bit)
        return jnp.where(place, jnp.expand_dims(value, axis), jnp.expand_dims(other, axis))

    def halved(self, value, axis, **bit):
        mine = self.bit(**bit).astype(jnp.int32)
        keep = lax.dynamic_index_in_dim(value, mine, axis, keepdims=False)
        give = lax.dynamic_index_in_dim(value, 1 - mine, axis, keepdims=False)
        return keep + self.swap(give, **bit)


def gather_piece(grid, piece, by_rank):
    rows = piece.shape[0]
    value = grid.joined(piece, 0, mod=2)
    value = grid.joined(value, 0, mod=4)
    value = grid.joined(value, 2, mod=1)
    axis = 0 if by_rank else 3
    value = grid.joined(value, axis, rep=2)
    value = grid.joined(value, axis + 1, rep=1)
    if by_rank:
        return value.reshape(4, grid.mods * rows, D)
    return value.reshape(grid.mods * 4 * rows, D)


def scatter_piece(grid, value, by_rank, y_first):
    if by_rank:
        value = value.reshape(2, 2, 2, 2, 2, -1, D)
        value = grid.halved(value, 1, rep=1)
        axis_x, axis_y = 0, 3
    else:
        value = value.reshape(2, 2, 2, 2, 2, -1, D)
        value = grid.halved(value, 4, rep=1)
        axis_x, axis_y = 3, 2
    if y_first:
        value = grid.halved(value, axis_y, mod=1)
        value = grid.halved(value, axis_x - (axis_x > axis_y), rep=2)
    else:
        value = grid.halved(value, axis_x, rep=2)
        value = grid.halved(value, axis_y - (axis_y > axis_x), mod=1)
    value = grid.halved(value, 0, mod=4)
    return grid.halved(value, 0, mod=2)


def share_ranks(grid, piece):
    value = grid.joined(piece, 0, rep=2)
    value = grid.joined(value, 1, rep=1)
    return value.reshape((4,) + piece.shape)


def sum_everywhere(grid, value):
    for bit in ({"rep": 1}, {"rep": 2}, {"mod": 1}, {"mod": 2}, {"mod": 4}):
        value = value + grid.swap(value, **bit)
    return value


def stem_sum(grid, value):
    shape = value.shape
    value = value.reshape(2, 2, 2, 2, 2, -1, D)
    order = ({"rep": 1}, {"rep": 2}, {"mod": 1}, {"mod": 4}, {"mod": 2})
    for bit in order:
        value = grid.halved(value, 0, **bit)
    for bit in reversed(order):
        value = grid.joined(value, 0, **bit)
    return value.reshape(shape)


def gathered_weights(grid, fast, qkv_weight, out_weight, up_weight, down_weight):
    if not fast:
        qkv = lax.all_gather(qkv_weight, "mod", axis=0, tiled=True)
        out = lax.all_gather(out_weight, "mod", axis=0, tiled=True)
        up = lax.all_gather(up_weight, "mod", axis=0, tiled=True)
        down = lax.all_gather(down_weight, "mod", axis=0, tiled=True)
        first = jnp.concatenate([qkv, out], axis=1)
        by_columns = lambda w: w.reshape(D, -1, D).transpose(1, 0, 2)
        return by_columns(first), by_columns(up), down
    rank = grid.rep
    pick = lambda w: lax.dynamic_slice_in_dim(w, rank * D, D, 1)
    first = gather_piece(grid, pick(jnp.concatenate([qkv_weight, out_weight], axis=1)), True)
    up = gather_piece(grid, pick(up_weight), True)
    quarter = down_weight.shape[0] // 4
    down = gather_piece(
        grid, lax.dynamic_slice_in_dim(down_weight, rank * quarter, quarter, 0), False
    )
    return first, up, down


def reduced_rows(value, fast):
    part = lax.psum_scatter(value, "mod", scatter_dimension=0, tiled=True)
    return lax.psum(part, "rep").astype(F32)


def per_device(
    raw_rows,
    recv_counts,
    slot_groups,
    read_counts,
    patch_convolution_weight,
    patch_stem_bias_vector,
    language_projection_weight,
    language_bias_vector,
    readout_table,
    attn_gain,
    attn_bias,
    qkv_weight,
    out_weight,
    mlp_gain,
    mlp_bias,
    up_weight,
    up_bias,
    down_weight,
    down_bias,
    out_cotangent,
):
    mods, reps = lax.axis_size("mod"), lax.axis_size("rep")
    fast = mods == 8 and reps == 4
    grid = Grid(mods, reps)
    block_rows = raw_rows.shape[1]
    capacity = mods * block_rows
    row = lambda v: v.reshape(1, -1)
    image = (grid.mod < 3 * mods // 4).astype(jnp.int32).reshape(1)
    group_row = slot_groups
    group_col = slot_groups.reshape(capacity, 1)

    received = lax.all_to_all(raw_rows, "mod", split_axis=0, concat_axis=0, tiled=True)
    first, up, down = gathered_weights(grid, fast, qkv_weight, out_weight, up_weight, down_weight)
    rows = received.reshape(capacity, D)
    stream, normed = stems(
        rows,
        patch_convolution_weight,
        row(patch_stem_bias_vector),
        language_projection_weight,
        row(language_bias_vector),
        readout_table,
        row(attn_gain),
        row(attn_bias),
    )
    qkv = project_qkv(normed, first)
    mixed, lse, lse_read = attend(qkv, recv_counts, read_counts, group_row, group_col, block_rows)
    after, normed2 = out_project(mixed, first, stream, row(mlp_gain), row(mlp_bias))
    layer_out, up_grad, down_grad, up_bias_grad, inner, branch, down_bias_grad = mlp(
        after,
        normed2,
        out_cotangent[0],
        recv_counts,
        read_counts,
        up,
        row(up_bias),
        down,
        row(down_bias),
        block_rows,
    )
    after_grad, attn_grad, mixed_grad, mlp_gain_grad, mlp_bias_grad = out_back(
        inner, after, branch, row(mlp_gain), first
    )
    grads = attend_back(
        qkv, mixed, mixed_grad, lse, lse_read, recv_counts, read_counts, group_row, group_col,
        block_rows,
    )
    embedded_grad, readout_grad, attn_gain_grad, attn_bias_grad = qkv_back(
        grads, first, stream, row(attn_gain), after_grad
    )
    first_grad = weight_grads(normed, mixed, grads, attn_grad)
    stem_grad, patch_bias_grad, lang_bias_grad = stem_back(rows, embedded_grad)
    returned = lax.all_to_all(
        embedded_grad.reshape(raw_rows.shape), "mod", split_axis=0, concat_axis=0, tiled=True
    )
    raw_grad = raw_back(
        image,
        returned.reshape(capacity, D),
        patch_convolution_weight,
        language_projection_weight,
    ).reshape(raw_rows.shape)

    small = jnp.concatenate(
        [
            patch_bias_grad,
            lang_bias_grad,
            attn_gain_grad,
            attn_bias_grad,
            mlp_gain_grad,
            mlp_bias_grad,
            down_bias_grad,
            up_bias_grad.reshape(-1, D),
            readout_grad,
        ],
        axis=0,
    )
    if fast:
        up_piece = share_ranks(grid, scatter_piece(grid, up_grad, True, True))
        down_piece = share_ranks(grid, scatter_piece(grid, down_grad, False, False))
        first_piece = share_ranks(grid, scatter_piece(grid, first_grad, True, False))
        flat = lambda p: p.transpose(1, 0, 2).reshape(p.shape[1], -1).astype(F32)
        qkv_sum = flat(first_piece[:3])
        out_sum = first_piece[3].astype(F32)
        up_sum = flat(up_piece)
        down_sum = down_piece.reshape(-1, D).astype(F32)
        small = sum_everywhere(grid, small)
        stem_grad = stem_sum(grid, stem_grad).astype(F32)
    else:
        flat = lambda p: p.transpose(1, 0, 2).reshape(D, -1)
        qkv_sum = reduced_rows(flat(first_grad[:3]), fast)
        out_sum = reduced_rows(first_grad[3], fast)
        up_sum = reduced_rows(flat(up_grad), fast)
        down_sum = reduced_rows(down_grad, fast)
        small = lax.psum(small, AXES)
        stem_grad = lax.psum(stem_grad.astype(F32), AXES)
    ups = up_bias.shape[0] // D
    return (
        layer_out[None],
        raw_grad,
        stem_grad[0],
        small[0],
        stem_grad[1],
        small[1],
        small[7 + ups : 7 + ups + RD],
        small[2],
        small[3],
        qkv_sum,
        out_sum,
        small[4],
        small[5],
        up_sum,
        small[7 : 7 + ups].reshape(-1),
        down_sum,
        small[6],
    )


def solution(mesh):
    both, rows, rep = P("mod", "rep", None), P("mod", None), P()
    pair = P("mod", "rep")
    return jax.shard_map(
        per_device,
        mesh=mesh,
        in_specs=(both, pair, pair, pair)
        + (rep,) * 7
        + (rows, rows, rep, rep, rows, rep, rows, rep, both),
        out_specs=(both, both)
        + (rep,) * 7
        + (rows, rows, rep, rep, rows, rep, rows, rep),
        check_vma=False,
    )
```

```python
import functools

import jax
import jax.numpy as jnp
from jax import lax
from jax.experimental import pallas as pl
from jax.experimental.pallas import tpu as pltpu
from jax.sharding import PartitionSpec as P

D = 768
HEADS = 12
HD = 64
RPS = 4
RD = 8
PAD = 16
PART = D // 2
LANES = 128
CHUNK = 256
FB = 256
EPS = 1e-6
NEG = -1e30
F32 = jnp.float32
BF16 = jnp.bfloat16
AXES = ("mod", "rep")
SCALE = HD ** (-0.5)
VMEM = pl.BlockSpec(memory_space=pltpu.VMEM)
SMEM = pl.BlockSpec(memory_space=pltpu.SMEM)
ANY = pl.BlockSpec(memory_space=pl.ANY)


def nn(left, right):
    return lax.dot_general(left, right, (((1,), (0,)), ((), ())), preferred_element_type=F32)


def nt(left, right):
    return lax.dot_general(left, right, (((1,), (1,)), ((), ())), preferred_element_type=F32)


def tn(left, right):
    return lax.dot_general(left, right, (((0,), (0,)), ((), ())), preferred_element_type=F32)


def line(vector):
    return vector[...].reshape(1, -1)


def chunks(rows):
    count = rows // CHUNK
    return [
        (i * CHUNK, (rows - i * CHUNK) if i == count - 1 else CHUNK) for i in range(count)
    ]


def normalise(rows):
    mean = jnp.mean(rows, axis=-1, keepdims=True)
    centred = rows - mean
    var = jnp.mean(centred * centred, axis=-1, keepdims=True)
    rstd = lax.rsqrt(var + EPS)
    return centred * rstd, rstd


def norm_input_grad(xhat, rstd, gain, upstream):
    scaled = upstream * gain
    first = jnp.mean(scaled, axis=-1, keepdims=True)
    second = jnp.mean(scaled * xhat, axis=-1, keepdims=True)
    return rstd * (scaled - first - xhat * second)


def call(kernel, out_shape, deps=(), **kw):
    limit = kw.pop("vmem", 56)
    estimate = kw.pop("cost", None)
    in_specs = kw.pop("in_specs")
    count, more = len(in_specs), len(deps)

    def body(*refs):
        kernel(*refs[:count], *refs[count + more :])

    built = pl.pallas_call(
        body,
        out_shape=out_shape,
        in_specs=list(in_specs) + [ANY] * more,
        cost_estimate=estimate,
        compiler_params=pltpu.CompilerParams(vmem_limit_bytes=limit * 1024 * 1024),
        **kw,
    )
    return lambda *args: built(*args, *deps)


def cost(us):
    return pl.CostEstimate(flops=int(us * 1.15e9), bytes_accessed=1 << 20, transcendentals=0)


def struct(shape, dtype):
    return jax.ShapeDtypeStruct(shape, dtype)


def live_of(index, counts, read, block_rows):
    groups_n = counts.shape[1]
    capacity = groups_n * block_rows
    live = index < 0
    for s in range(groups_n):
        live = live | ((index >= s * block_rows) & (index < s * block_rows + counts[0, s]))
    slot = index - capacity
    return live | ((slot >= 0) & (slot < RD) & (slot % RPS < read[0, 0]))


def place_bits(place, places):
    if places == 1:
        return 0
    return (place >> 2) + 2 * (place & 3)


def place_of(bits):
    return ((bits & 1) << 2) | (bits >> 1)


def fetch(ids, arrays, want, target, sem):
    places, rows = arrays[0].shape[0], arrays[0].shape[1]
    for k in range(4):

        @pl.when((ids[0] ^ k) == want)
        def _():
            fetch_array(ids, arrays[k], target, sem)


def fetch_array(ids, array, target, sem):
    places, rows = array.shape[0], array.shape[1]
    for place in range(places):
        shard = ids[1] ^ place_bits(place, places)
        start = pl.multiple_of(shard * rows, 16)
        pltpu.make_async_copy(array.at[place], target.at[pl.ds(start, rows), :], sem).start()


def fetched(target, sem):
    pltpu.make_async_copy(target, target, sem).wait()


def stem_kernel(cut, raw, wp, bp, wl, bl, table, gain, bias, stream, normed):
    capacity = raw.shape[0]
    step = capacity // 4
    for start in range(0, capacity, step):
        weight, shift = (wp, bp) if start < cut else (wl, bl)
        rows = pl.ds(start, step)
        embedded = (nn(raw[rows, :], weight[...]) + line(shift)).astype(BF16).astype(F32)
        stream[rows, :] = embedded
        xhat, _ = normalise(embedded)
        normed[rows, :] = (xhat * line(gain) + line(bias)).astype(BF16)
    tail = jnp.concatenate([table[...], jnp.zeros((PAD - RD, D), F32)], axis=0)
    stream[pl.ds(capacity, PAD), :] = tail
    xhat, _ = normalise(tail)
    normed[pl.ds(capacity, PAD), :] = (xhat * line(gain) + line(bias)).astype(BF16)


def stems(raw, wp, bp, wl, bl, table, gain, bias):
    capacity = raw.shape[0]
    total = capacity + PAD
    return call(
        functools.partial(stem_kernel, 3 * capacity // 4),
        (struct((total, D), F32), struct((total, D), BF16)),
        in_specs=[VMEM] * 8,
        out_specs=(VMEM, VMEM),
        cost=cost(5),
    )(raw, wp, bp, wl, bl, table, gain, bias)


def qkv_kernel(ids, rows, w0, w1, w2, w3, out, buffer, sem):
    for r in range(3):
        fetch(ids, (w0, w1, w2, w3), r, buffer.at[r], sem.at[r])
    for r in range(3):
        fetched(buffer.at[r], sem.at[r])
        for start, size in chunks(rows.shape[0]):
            out[r, pl.ds(start, size), :] = nn(rows[pl.ds(start, size), :], buffer[r]).astype(BF16)


def project_qkv(ids, normed, weights, deps=()):
    total = normed.shape[0]
    return call(
        qkv_kernel,
        struct((3, total, D), BF16),
        deps,
        in_specs=[SMEM, VMEM, ANY, ANY, ANY, ANY],
        out_specs=VMEM,
        scratch_shapes=[pltpu.VMEM((3, D, D), BF16), pltpu.SemaphoreType.DMA((3,))],
        cost=cost(7),
    )(ids, normed, *weights)


def visible_readout(group_row, live_row):
    capacity = group_row.shape[1]
    query = lax.broadcasted_iota(jnp.int32, (RD, capacity), 0)
    group = 2 * (query // RPS + 1) + 1
    keys = group_row[...]
    seen = live_row & (keys <= group) & ((keys % 2 == 0) | (keys == group))
    return jnp.where(seen, 0.0, NEG)


def visible_between(read):
    query = lax.broadcasted_iota(jnp.int32, (RD, PAD), 0)
    key = lax.broadcasted_iota(jnp.int32, (RD, PAD), 1)
    live = (key < RD) & (key % RPS < read[0, 0])
    seen = (query == key) | (live & (query // RPS == key // RPS))
    return jnp.where(seen, 0.0, NEG)


def tiled(rows, heads):
    return jnp.concatenate([rows] * heads, axis=0)


def own_head(heads):
    row = lax.broadcasted_iota(jnp.int32, (heads * RD, heads * HD), 0) // RD
    lane = lax.broadcasted_iota(jnp.int32, (heads * RD, heads * HD), 1) // HD
    return row == lane


def fold_heads(stack, mine):
    kept = jnp.where(mine, stack, 0.0)
    total = kept[:RD]
    for start in range(RD, stack.shape[0], RD):
        total = total + kept[start : start + RD]
    return jnp.concatenate([total, jnp.zeros((PAD - RD, stack.shape[1]), F32)], axis=0)


def attend_kernel(
    block_rows, qkv, counts, read, group_row, group_col, mixed, lse, lse_read, mask, lse_cols, tail
):
    step = pl.program_id(0)
    capacity = group_row.shape[1]

    @pl.when(step == 0)
    def _():
        slot_row = lax.broadcasted_iota(jnp.int32, (1, capacity), 1)
        live_row = live_of(slot_row, counts, read, block_rows)
        keys = group_row[...]
        for start in range(0, capacity, CHUNK):
            query = lax.broadcasted_iota(jnp.int32, (CHUNK, capacity), 0) + start
            group = group_col[pl.ds(start, CHUNK), :]
            seen = live_row & (keys <= group) & ((keys % 2 == 0) | (keys == group))
            seen = seen | (query == slot_row)
            mask[pl.ds(start, CHUNK), :] = jnp.where(seen, 0.0, NEG)
        lse_cols[...] = jnp.zeros_like(lse_cols)
        mine = own_head(HEADS)
        tail_rows = pl.ds(capacity, PAD)
        head_rows = pl.ds(0, capacity)
        query = qkv[0, tail_rows, :].astype(F32)[:RD] * SCALE
        query = jnp.where(mine, tiled(query, HEADS), 0.0).astype(BF16)
        far = nt(query, qkv[1, head_rows, :]) + tiled(visible_readout(group_row, live_row), HEADS)
        near = nt(query, qkv[1, tail_rows, :]) + tiled(visible_between(read), HEADS)
        peak = jnp.maximum(
            jnp.max(far, axis=1, keepdims=True), jnp.max(near, axis=1, keepdims=True)
        )
        far = jnp.exp(far - peak)
        near = jnp.exp(near - peak)
        total = jnp.sum(far, axis=1, keepdims=True) + jnp.sum(near, axis=1, keepdims=True)
        out = nn(far.astype(BF16), qkv[2, head_rows, :]) + nn(
            near.astype(BF16), qkv[2, tail_rows, :]
        )
        tail[...] = fold_heads(out / total, mine)
        lse_read[...] = jnp.broadcast_to(peak + jnp.log(total), lse_read.shape)

    lane = lax.broadcasted_iota(jnp.int32, (1, LANES), 1)
    columns = pl.ds(pl.multiple_of(step * LANES, LANES), LANES)
    keys = qkv[1, pl.ds(0, capacity), columns]
    values = qkv[2, pl.ds(0, capacity), columns]
    for start in range(0, capacity, CHUNK):
        rows = pl.ds(start, CHUNK)
        query = qkv[0, rows, columns] * SCALE
        outs = []
        logs = lse_cols[rows, :]
        for head in range(2):
            chosen = jnp.where(lane // HD == head, query, jnp.zeros_like(query))
            scores = nt(chosen.astype(BF16), keys) + mask[rows, :]
            peak = jnp.max(scores, axis=1, keepdims=True)
            weight = jnp.exp(scores - peak)
            total = jnp.sum(weight, axis=1, keepdims=True)
            outs.append(nn(weight.astype(BF16), values) / total)
            logs = jnp.where(lane == 2 * step + head, peak + jnp.log(total), logs)
        mixed[rows, :] = jnp.where(lane < HD, outs[0], outs[1]).astype(BF16)
        lse_cols[rows, :] = logs
    mixed[pl.ds(capacity, PAD), :] = tail[:, columns].astype(BF16)

    @pl.when(step == pl.num_programs(0) - 1)
    def _():
        lse[...] = lse_cols[...].T[: lse.shape[0], :]


def attend(qkv, counts, read, group_row, group_col, block_rows, deps=()):
    total = qkv.shape[1]
    capacity = total - PAD
    pairs = HEADS // 2
    return call(
        functools.partial(attend_kernel, block_rows),
        (
            struct((total, D), BF16),
            struct((16, capacity), F32),
            struct((HEADS * RD, LANES), F32),
        ),
        deps,
        grid=(pairs,),
        in_specs=[VMEM, SMEM, SMEM, VMEM, VMEM],
        out_specs=(pl.BlockSpec((total, LANES), lambda j: (0, j)), VMEM, VMEM),
        scratch_shapes=[
            pltpu.VMEM((capacity, capacity), F32),
            pltpu.VMEM((capacity, LANES), F32),
            pltpu.VMEM((PAD, D), F32),
        ],
        cost=cost(21),
    )(qkv, counts, read, group_row, group_col)


def attend_back_kernel(
    block_rows,
    part,
    qkv,
    mixed,
    grad,
    lse,
    lse_read,
    counts,
    read,
    group_row,
    group_col,
    out,
    mask,
    delta,
    key_more,
    value_more,
    tails,
):
    step = pl.program_id(0)
    capacity = group_row.shape[1]
    tail_rows = pl.ds(capacity, PAD)
    head_rows = pl.ds(0, capacity)
    heads = PART // HD
    mine_columns = pl.ds(part * PART, PART)

    @pl.when(step == 0)
    def _():
        slot_row = lax.broadcasted_iota(jnp.int32, (1, capacity), 1)
        group = group_row[...]
        for start in range(0, capacity, CHUNK):
            slot = lax.broadcasted_iota(jnp.int32, (CHUNK, 1), 0) + start
            live = live_of(slot, counts, read, block_rows)
            keys = group_col[pl.ds(start, CHUNK), :]
            seen = live & (keys <= group) & ((keys % 2 == 0) | (keys == group))
            seen = seen | (slot == slot_row)
            mask[pl.ds(start, CHUNK), :] = jnp.where(seen, 0.0, NEG)
        head = lax.broadcasted_iota(jnp.int32, (8, PART), 0)
        column = lax.broadcasted_iota(jnp.int32, (8, PART), 1)
        select = jnp.where(column // HD == head, 1.0, 0.0).astype(BF16)
        for start in range(0, capacity, CHUNK):
            rows = pl.ds(start, CHUNK)
            product = grad[rows, mine_columns].astype(F32) * mixed[rows, mine_columns].astype(F32)
            high = product.astype(BF16)
            low = (product - high.astype(F32)).astype(BF16)
            delta[:, rows] = nt(select, high) + nt(select, low)

        live_row = live_of(slot_row, counts, read, block_rows)
        mine = own_head(heads)
        query = qkv[0, tail_rows, mine_columns].astype(F32)[:RD] * SCALE
        query = jnp.where(mine, tiled(query, heads), 0.0).astype(BF16)
        upper = grad[tail_rows, mine_columns].astype(F32)[:RD]
        upper = jnp.where(mine, tiled(upper, heads), 0.0)
        result = tiled(mixed[tail_rows, mine_columns].astype(F32)[:RD], heads)
        row_delta = jnp.sum(upper * result, axis=1, keepdims=True)
        upper = upper.astype(BF16)
        logs = lse_read[pl.ds(part * heads * RD, heads * RD), 0:1]
        far = nt(query, qkv[1, head_rows, mine_columns]) + tiled(visible_readout(group_row, live_row), heads)
        near = nt(query, qkv[1, tail_rows, mine_columns]) + tiled(visible_between(read), heads)
        far = jnp.exp(far - logs)
        near = jnp.exp(near - logs)
        far_grad = (far * (nt(upper, qkv[2, head_rows, mine_columns]) - row_delta)).astype(BF16)
        near_grad = (near * (nt(upper, qkv[2, tail_rows, mine_columns]) - row_delta)).astype(BF16)
        query_grad = nn(far_grad, qkv[1, head_rows, mine_columns]) + nn(near_grad, qkv[1, tail_rows, mine_columns])
        tails[0] = fold_heads(query_grad, mine) * SCALE
        tails[1] = tn(near_grad, query)
        tails[2] = tn(near.astype(BF16), upper)
        key_more[...] = tn(far_grad, query)
        value_more[...] = tn(far.astype(BF16), upper)

    lane = lax.broadcasted_iota(jnp.int32, (1, LANES), 1)
    columns = pl.ds(pl.multiple_of(step * LANES, LANES), LANES)
    here = pl.ds(pl.multiple_of(part * PART + step * LANES, LANES), LANES)
    query = (qkv[0, head_rows, here] * SCALE).astype(BF16)
    upper = grad[head_rows, here]
    query_grad = jnp.zeros((capacity, LANES), F32)
    for start in range(0, capacity, CHUNK):
        rows = pl.ds(start, CHUNK)
        all_keys = qkv[1, rows, here]
        all_values = qkv[2, rows, here]
        key_parts = []
        value_parts = []
        for head in range(2):
            own = lane // HD == head
            keys = jnp.where(own, all_keys, jnp.zeros_like(all_keys))
            values = jnp.where(own, all_values, jnp.zeros_like(all_values))
            logs = lse[pl.ds(part * heads + 2 * step + head, 1), :]
            row_delta = delta[pl.ds(2 * step + head, 1), :]
            probs = jnp.exp(nt(keys, query) + mask[rows, :] - logs)
            score_grad = (probs * (nt(values, upper) - row_delta)).astype(BF16)
            value_parts.append(nn(probs.astype(BF16), upper))
            key_parts.append(nn(score_grad, query))
            query_grad = query_grad + tn(score_grad, keys)
        key_grad = jnp.where(lane < HD, key_parts[0], key_parts[1]) + key_more[rows, columns]
        value_grad = jnp.where(lane < HD, value_parts[0], value_parts[1]) + value_more[rows, columns]
        out[1, rows, :] = key_grad.astype(BF16)
        out[2, rows, :] = value_grad.astype(BF16)
    out[0, head_rows, :] = (query_grad * SCALE).astype(BF16)
    for part in range(3):
        out[part, tail_rows, :] = tails[part, :, columns].astype(BF16)


def attend_back(
    qkv, mixed, grad, lse, lse_read, counts, read, group_row, group_col, block_rows, part,
    deps=()
):
    total = qkv.shape[1]
    capacity = total - PAD
    pairs = PART // LANES
    return call(
        functools.partial(attend_back_kernel, block_rows, part),
        struct((3, total, PART), BF16),
        deps,
        grid=(pairs,),
        in_specs=[VMEM, VMEM, VMEM, VMEM, VMEM, SMEM, SMEM, VMEM, VMEM],
        out_specs=pl.BlockSpec((3, total, LANES), lambda j: (0, 0, j)),
        scratch_shapes=[
            pltpu.VMEM((capacity, capacity), F32),
            pltpu.VMEM((8, capacity), F32),
            pltpu.VMEM((capacity, PART), F32),
            pltpu.VMEM((capacity, PART), F32),
            pltpu.VMEM((3, PAD, PART), F32),
        ],
        cost=cost(15),
    )(qkv, mixed, grad, lse, lse_read, counts, read, group_row, group_col)


def out_kernel(ids, mixed, w0, w1, w2, w3, stream, gain, bias, after, normed, buffer, sem):
    fetch(ids, (w0, w1, w2, w3), 3, buffer, sem)
    fetched(buffer, sem)
    for start, size in chunks(mixed.shape[0]):
        rows = pl.ds(start, size)
        value = stream[rows, :] + nn(mixed[rows, :], buffer[...])
        after[rows, :] = value
        xhat, _ = normalise(value)
        normed[rows, :] = (xhat * line(gain) + line(bias)).astype(BF16)


def out_project(ids, mixed, weights, stream, gain, bias, deps=()):
    total = mixed.shape[0]
    return call(
        out_kernel,
        (struct((total, D), F32), struct((total, D), BF16)),
        deps,
        in_specs=[SMEM, VMEM, ANY, ANY, ANY, ANY, VMEM, VMEM, VMEM],
        out_specs=(VMEM, VMEM),
        scratch_shapes=[pltpu.VMEM((D, D), BF16), pltpu.SemaphoreType.DMA],
        cost=cost(6.4),
    )(ids, mixed, *weights, stream, gain, bias)


def out_back_kernel(
    ids, inner, after, branch, gain, w0, w1, w2, w3, grad, grad_low, mixed_grad, sums, buffer, sem
):
    fetch(ids, (w0, w1, w2, w3), 3, buffer, sem)
    fetched(buffer, sem)
    gain_sum = jnp.zeros((1, D), F32)
    bias_sum = jnp.zeros((1, D), F32)
    for start, size in chunks(inner.shape[0]):
        rows = pl.ds(start, size)
        upstream = inner[rows, :]
        xhat, rstd = normalise(after[rows, :])
        gain_sum = gain_sum + jnp.sum(upstream * xhat, axis=0, keepdims=True)
        bias_sum = bias_sum + jnp.sum(upstream, axis=0, keepdims=True)
        total = branch[rows, :].astype(F32) + norm_input_grad(xhat, rstd, line(gain), upstream)
        grad[rows, :] = total
        low = total.astype(BF16)
        grad_low[rows, :] = low
        mixed_grad[rows, :] = nt(low, buffer[...]).astype(BF16)
    sums[0:1, :] = gain_sum
    sums[1:2, :] = bias_sum


def out_back(ids, inner, after, branch, gain, weights, deps=()):
    total = inner.shape[0]
    return call(
        out_back_kernel,
        (
            struct((total, D), F32),
            struct((total, D), BF16),
            struct((total, D), BF16),
            struct((2, D), F32),
        ),
        deps,
        in_specs=[SMEM, VMEM, VMEM, VMEM, VMEM, ANY, ANY, ANY, ANY],
        out_specs=(VMEM, VMEM, VMEM, VMEM),
        scratch_shapes=[pltpu.VMEM((D, D), BF16), pltpu.SemaphoreType.DMA],
        cost=cost(8.5),
    )(ids, inner, after, branch, gain, *weights)


def prepare_kernel(block_rows, cotangent, counts, read, branch, bias_grad):
    total, slots = branch.shape[0], cotangent.shape[0]
    index = lax.broadcasted_iota(jnp.int32, (total, 1), 0)
    live = jnp.where(live_of(index, counts, read, block_rows), 1.0, 0.0)
    upstream = cotangent[...].astype(F32) * live[:slots]
    bias_grad[...] = jnp.sum(upstream, axis=0, keepdims=True)
    upstream = jnp.concatenate([upstream, jnp.zeros((total - slots, D), F32)], axis=0)
    branch[...] = upstream.astype(BF16)


def prepare(cotangent, counts, read, block_rows, total):
    return call(
        functools.partial(prepare_kernel, block_rows),
        (struct((total, D), BF16), struct((1, D), F32)),
        in_specs=[VMEM, SMEM, SMEM],
        out_specs=(VMEM, VMEM),
        cost=cost(3),
    )(cotangent, counts, read)


def mlp_kernel(
    block_rows,
    ks,
    first,
    last,
    slots,
    *refs,
):
    nk = len(ks)
    ids, counts, read, normed, branch, up_bias, down_bias, total_in, inner_in, sums_in = refs[:10]
    weights = refs[10 : 10 + 2 * nk]
    active, hidden_grad, total, inner, sums = refs[10 + 2 * nk : 15 + 2 * nk]
    up, down, sem = refs[-3:]
    step = pl.program_id(0)
    index = step // (D // FB)
    part = step % (D // FB)
    length = normed.shape[0]

    @pl.when(step == 0)
    def _():
        for i in range(nk):
            fetch_array(ids, weights[2 * i], up.at[i], sem.at[i, 0])
            fetch_array(ids, weights[2 * i + 1], down.at[i], sem.at[i, 1])
        sums[...] = sums_in[...]
        if first:
            total[...] = total_in[...] + line(down_bias)
            inner[...] = jnp.zeros_like(inner)
        else:
            total[...] = total_in[...]
            inner[...] = inner_in[...]

    @pl.when(part == 0)
    def _():
        fetched(up.at[index], sem.at[index, 0])
        fetched(down.at[index], sem.at[index, 1])

    columns = pl.ds(pl.multiple_of(part * FB, FB), FB)
    rank = ids[0] ^ ks[0]
    for i in range(1, nk):
        rank = jnp.where(index == i, ids[0] ^ ks[i], rank)
    up_part = up[index, :, columns]
    down_part = down[index, columns, :]
    shift = up_bias[pl.ds(rank, 1), columns]
    bias_sum = jnp.zeros((1, FB), F32)
    for start, size in chunks(length):
        rows = pl.ds(start, size)
        hidden = nn(normed[rows, :], up_part) + shift
        factor = (2.0 / jnp.pi) ** 0.5
        square = hidden * hidden
        bent = jnp.tanh(hidden * (factor + (factor * 0.044715) * square))
        half = 0.5 * (1.0 + bent)
        act = (hidden * half).astype(BF16)
        slope = half + (0.5 * hidden) * (1.0 - bent * bent) * (
            factor + (3.0 * factor * 0.044715) * square
        )
        back = (nt(branch[rows, :], down_part) * slope).astype(BF16)
        bias_sum = bias_sum + jnp.sum(back.astype(F32), axis=0, keepdims=True)
        active[0, rows, :] = act
        hidden_grad[0, rows, :] = back
        total[rows, :] += nn(act, down_part)
        inner[rows, :] += nt(back, up_part)
    sums[pl.ds(rank, 1), columns] = bias_sum

    if last:

        @pl.when(step == pl.num_programs(0) - 1)
        def _():
            at = lax.broadcasted_iota(jnp.int32, (length, 1), 0)
            live = jnp.where(live_of(at, counts, read, block_rows), 1.0, 0.0)
            total[...] = total[...] * live


def mlp(ids, ks, counts, read, normed, branch, up_bias, down_bias, state, weights, block_rows, slots, first, last, deps=()):
    total = normed.shape[0]
    nk = len(ks)
    per = D // FB
    whole = pl.BlockSpec((total, D), lambda j: (0, 0))
    vectors = pl.BlockSpec((4, D), lambda j: (0, 0))
    block = pl.BlockSpec((1, total, FB), lambda j: (j // per, 0, j % per))
    flat = [w for pair in weights for w in pair]
    return call(
        functools.partial(mlp_kernel, block_rows, ks, first, last, slots),
        (
            struct((nk, total, D), BF16),
            struct((nk, total, D), BF16),
            struct((total, D), F32),
            struct((total, D), F32),
            struct((4, D), F32),
        ),
        deps,
        grid=(nk * per,),
        in_specs=[SMEM, SMEM, SMEM, whole, whole, vectors, VMEM, whole, whole, vectors]
        + [ANY] * (2 * nk),
        out_specs=(block, block, whole, whole, vectors),
        scratch_shapes=[
            pltpu.VMEM((nk, D, D), BF16),
            pltpu.VMEM((nk, D, D), BF16),
            pltpu.SemaphoreType.DMA((nk, 2)),
        ],
        cost=cost(20),
    )(ids, counts, read, normed, branch, up_bias, down_bias, *state, *flat)


def put_rows(ids, value, first_row, places, store):
    rows = D // places
    for i in range(value.shape[0] // rows):
        bits = ids[1] ^ (first_row // rows + i)
        store(place_of(bits) if places > 1 else 0, value[i * rows : (i + 1) * rows])


def product_rows(ids, left, right, places, store):
    block = D // 2 if places > 1 else D
    for start in range(0, D, block):
        value = tn(left[:, start : start + block], right[...])
        put_rows(ids, value, start, places, store)


def to_give_kernel(places, count, ids, *refs):
    lefts, rights, out = refs[:count], refs[count : 2 * count], refs[2 * count]
    for i in range(count):

        def store(place, rows, i=i):
            out[i, pl.ds(place, 1)] = rows.astype(BF16)[None]

        product_rows(ids, lefts[i], rights[i], places, store)


def to_keep_kernel(places, y_first, ids, left0, right0, left2, right2, got0, got2, keep, give):
    half = max(places // 2, 1)
    for x, (left, right) in enumerate(((left0, right0), (left2, right2))):

        def store(place, rows, x=x):
            got = (got0, got2)[x]
            summed = (rows + got[pl.ds(place, 1)][0].astype(F32)).astype(BF16)[None]
            y, z = place // half, place % half
            if y_first:

                @pl.when(y == 0)
                def _():
                    keep[x, pl.ds(z, 1)] = summed

                @pl.when(y == 1)
                def _():
                    give[x, pl.ds(z, 1)] = summed
            else:
                (give if x else keep)[y, pl.ds(z, 1)] = summed

        product_rows(ids, left, right, places, store)


def column_spec(total):
    return pl.BlockSpec((total, D), lambda i: (0, 0))


def act_spec(total, index):
    return pl.BlockSpec((None, total, D), lambda i: (index, 0, 0))


def give_products(ids, pairs, specs, places, deps=()):
    count = len(pairs)
    total = pairs[0][0].shape[-2]
    rows = D // places
    return call(
        functools.partial(to_give_kernel, places, count),
        struct((count, places, rows, D), BF16),
        deps,
        grid=(1,),
        in_specs=[SMEM] + [s[0] for s in specs] + [s[1] for s in specs],
        out_specs=pl.BlockSpec((count, places, rows, D), lambda i: (0, 0, 0, 0)),
        cost=cost(6.5),
    )(ids, *[p[0] for p in pairs], *[p[1] for p in pairs])


def keep_products(ids, pairs, specs, got, index, places, y_first, deps=()):
    total = pairs[0][0].shape[-2]
    rows = D // places
    half = struct((2, max(places // 2, 1), rows, D), BF16)
    half_spec = pl.BlockSpec((2, max(places // 2, 1), rows, D), lambda i: (0, 0, 0, 0))
    return call(
        functools.partial(to_keep_kernel, places, y_first),
        (half, half),
        deps,
        grid=(1,),
        in_specs=[
            SMEM,
            specs[0][0],
            specs[0][1],
            specs[1][0],
            specs[1][1],
            pl.BlockSpec((None, places, rows, D), lambda i: (index, 0, 0, 0)),
            pl.BlockSpec((None, places, rows, D), lambda i: (index, 0, 0, 0)),
        ],
        out_specs=(half_spec, half_spec),
        cost=cost(8),
    )(ids, pairs[0][0], pairs[0][1], pairs[1][0], pairs[1][1], *got)


def first_fetch(ids, k, part, normed, mixed, grads, attn_grad, left, right, sem):
    rank = ids[0] ^ k

    @pl.when(rank < 3)
    def _():
        pltpu.make_async_copy(normed, left, sem.at[0]).start()
        pltpu.make_async_copy(grads.at[rank], right, sem.at[1]).start()

    @pl.when(rank == 3)
    def _():
        pltpu.make_async_copy(mixed, left, sem.at[0]).start()
        pltpu.make_async_copy(attn_grad.at[:, pl.ds(part * PART, PART)], right, sem.at[1]).start()


def first_give_kernel(places, part, ids, normed, mixed, grads, attn_grad, out, left, right, sem):
    ks = (1, 3)
    sources = (normed, mixed, grads, attn_grad)
    for i, k in enumerate(ks):
        first_fetch(ids, k, part, *sources, left.at[i], right.at[i], sem.at[i])
    for i, k in enumerate(ks):
        fetched(left.at[i], sem.at[i, 0])
        fetched(right.at[i], sem.at[i, 1])

        def store(place, rows, i=i):
            out[i, pl.ds(place, 1)] = rows.astype(BF16)[None]

        product_rows(ids, left.at[i], right.at[i], places, store)


def first_scratch(total):
    return [
        pltpu.VMEM((2, total, D), BF16),
        pltpu.VMEM((2, total, PART), BF16),
        pltpu.SemaphoreType.DMA((2, 2)),
    ]


def first_give(ids, part, normed, mixed, grads, attn_grad, places, deps=()):
    total = normed.shape[0]
    return call(
        functools.partial(first_give_kernel, places, part),
        struct((2, places, D // places, PART), BF16),
        deps,
        in_specs=[SMEM, ANY, ANY, ANY, ANY],
        out_specs=VMEM,
        scratch_shapes=first_scratch(total),
        cost=cost(5),
    )(ids, normed, mixed, grads, attn_grad)


def first_keep_kernel(
    places, part, y_first, ids, normed, mixed, grads, attn_grad, got, keep, give, left, right, sem
):
    sources = (normed, mixed, grads, attn_grad)
    for i, k in enumerate((0, 2)):
        first_fetch(ids, k, part, *sources, left.at[i], right.at[i], sem.at[i])
    for i in range(2):
        fetched(left.at[i], sem.at[i, 0])
        fetched(right.at[i], sem.at[i, 1])
    to_keep_kernel(
        places, y_first, ids, left.at[0], right.at[0], left.at[1], right.at[1], got.at[0], got.at[1],
        keep, give
    )


def first_keep(ids, part, normed, mixed, grads, attn_grad, got, places, y_first, deps=()):
    total = normed.shape[0]
    half = struct((2, max(places // 2, 1), D // places, PART), BF16)
    return call(
        functools.partial(first_keep_kernel, places, part, y_first),
        (half, half),
        deps,
        in_specs=[SMEM, ANY, ANY, ANY, ANY, VMEM],
        out_specs=(VMEM, VMEM),
        scratch_shapes=first_scratch(total),
        cost=cost(6),
    )(ids, normed, mixed, grads, attn_grad, got)


def qkv_back_kernel(capacity, ids, grads0, grads1, *refs):
    stream, gain, after_grad, embedded, readout, sums, buffer, sem = refs[4:]
    for r in range(3):
        fetch(ids, refs[:4], r, buffer.at[r], sem.at[r])
    for r in range(3):
        fetched(buffer.at[r], sem.at[r])
    gain_sum = jnp.zeros((1, D), F32)
    bias_sum = jnp.zeros((1, D), F32)
    for start, size in chunks(stream.shape[0]):
        rows = pl.ds(start, size)
        upstream = jnp.zeros((size, D), F32)
        for r in range(3):
            grad = jnp.concatenate([grads0[r, rows, :], grads1[r, rows, :]], axis=1)
            upstream = upstream + nt(grad, buffer[r])
        xhat, rstd = normalise(stream[rows, :])
        gain_sum = gain_sum + jnp.sum(upstream * xhat, axis=0, keepdims=True)
        bias_sum = bias_sum + jnp.sum(upstream, axis=0, keepdims=True)
        total = after_grad[rows, :] + norm_input_grad(xhat, rstd, line(gain), upstream)
        inside = min(size, capacity - start)
        embedded[pl.ds(start, inside), :] = total[:inside].astype(BF16)
        if start + size > capacity:
            readout[...] = total[capacity - start : capacity - start + RD]
    sums[0:1, :] = gain_sum
    sums[1:2, :] = bias_sum


def qkv_back(ids, grads, weights, stream, gain, after_grad, deps=()):
    total = stream.shape[0]
    capacity = total - PAD
    return call(
        functools.partial(qkv_back_kernel, capacity),
        (struct((capacity, D), BF16), struct((RD, D), F32), struct((2, D), F32)),
        deps,
        in_specs=[SMEM, VMEM, VMEM] + [ANY] * 4 + [VMEM, VMEM, VMEM],
        out_specs=(VMEM, VMEM, VMEM),
        scratch_shapes=[pltpu.VMEM((3, D, D), BF16), pltpu.SemaphoreType.DMA((3,))],
        cost=cost(10),
    )(ids, *grads, *weights, stream, gain, after_grad)


def stem_back_kernel(cut, places, ids, raw, embedded, keep, give, sums):
    for stem, part in enumerate((slice(0, cut), slice(cut, None))):
        sums[stem : stem + 1, :] = jnp.sum(embedded[part, :].astype(F32), axis=0, keepdims=True)
        value = tn(raw[part, :], embedded[part, :]).astype(BF16)
        if places == 1:
            (give if stem else keep)[...] = value.reshape(keep.shape)
            continue
        rows = D // places // 2
        mine = (ids[0] & 1) == stem
        for i in range(2 * places):
            place = place_of(ids[1] ^ (i // 2))
            x = (i % 2) ^ (ids[0] >> 1)
            at = (x * 2 + (place >> 2)) * 4 + (place & 3)
            piece = value[i * rows : (i + 1) * rows][None]

            @pl.when(mine)
            def _():
                keep[pl.ds(at, 1)] = piece

            @pl.when(jnp.logical_not(mine))
            def _():
                give[pl.ds(at, 1)] = piece


def stem_back(ids, raw, embedded, places, deps=()):
    capacity = raw.shape[0]
    shape = (2 * places, D // (2 * places), D) if places > 1 else (1, D, D)
    return call(
        functools.partial(stem_back_kernel, 3 * capacity // 4, places),
        (struct(shape, BF16), struct(shape, BF16), struct((2, D), F32)),
        deps,
        in_specs=[SMEM, VMEM, VMEM],
        out_specs=(VMEM, VMEM, VMEM),
        cost=cost(6),
    )(ids, raw, embedded)


def stem_out_kernel(ids, own, other, patch, lang):
    rows = own.shape[1]
    for i in range(own.shape[0]):
        shard = ids[1] ^ place_bits(((i >> 2) & 1) * 4 + (i & 3), 8)
        x = (i >> 3) ^ (ids[0] >> 1)
        at = pl.ds(pl.multiple_of((shard * 2 + x) * rows, 16), rows)
        mine, theirs = own[i].astype(F32), other[i].astype(F32)

        @pl.when((ids[0] & 1) == 0)
        def _():
            patch[at, :] = mine
            lang[at, :] = theirs

        @pl.when((ids[0] & 1) == 1)
        def _():
            patch[at, :] = theirs
            lang[at, :] = mine


def stem_out(ids, own, other):
    return call(
        stem_out_kernel,
        (struct((D, D), F32), struct((D, D), F32)),
        in_specs=[SMEM, VMEM, VMEM],
        out_specs=(VMEM, VMEM),
        cost=cost(4.4),
    )(ids, own, other)


def raw_kernel(image, grad, wp, wl, out):
    @pl.when(image[0] != 0)
    def _():
        out[...] = nt(grad[...], wp[...])

    @pl.when(image[0] == 0)
    def _():
        out[...] = nt(grad[...], wl[...])


def raw_back(image, grad, wp, wl, deps=()):
    return call(
        raw_kernel,
        struct(grad.shape, F32),
        deps,
        in_specs=[SMEM, VMEM, VMEM, VMEM],
        out_specs=VMEM,
        cost=cost(4.6),
    )(image, grad, wp, wl)


def first_out_kernel(ids, k0, k2, k13, qkv, out, ranks):
    ranks[0], ranks[2], ranks[1], ranks[3] = k0[...], k2[...], k13[0], k13[1]
    for r in range(3):
        qkv[:, r * D : (r + 1) * D] = ranks[pl.ds(ids[0] ^ r, 1)][0].astype(F32)
    out[...] = ranks[pl.ds(ids[0] ^ 3, 1)][0].astype(F32)


def first_out(ids, k0, k2, k13):
    rows = k0.shape[0]
    return call(
        first_out_kernel,
        (struct((rows, 3 * D), F32), struct((rows, D), F32)),
        in_specs=[SMEM, VMEM, VMEM, VMEM],
        out_specs=(VMEM, VMEM),
        scratch_shapes=[pltpu.VMEM((4, rows, D), BF16)],
        cost=cost(2.3),
    )(ids, k0, k2, k13)


def mlp_out_kernel(places, ids, k0, k2, k13, up, down, ranks):
    ranks[0], ranks[2], ranks[1], ranks[3] = k0[...], k2[...], k13[0], k13[1]
    rows, unit = k0.shape[1], D // places
    for r in range(4):
        both = ranks[pl.ds(ids[0] ^ r, 1)][0]
        value = both[0].astype(F32)
        for s in range(places):
            start = (4 * s + r) * unit
            up[:, start : start + unit] = value[:, s * unit : (s + 1) * unit]
        down[r * rows : (r + 1) * rows, :] = both[1].astype(F32)


def mlp_out(ids, k0, k2, k13, places):
    rows = k0.shape[1]
    return call(
        functools.partial(mlp_out_kernel, places),
        (struct((rows, 4 * D), F32), struct((4 * rows, D), F32)),
        in_specs=[SMEM, VMEM, VMEM, VMEM],
        out_specs=(VMEM, VMEM),
        scratch_shapes=[pltpu.VMEM((4, 2, rows, D), BF16)],
        cost=cost(3.1),
    )(ids, k0, k2, k13)


class Grid:
    def __init__(self, mods, reps):
        self.mods, self.reps = mods, reps
        self.mod, self.rep = lax.axis_index("mod"), lax.axis_index("rep")

    def swap(self, value, mod=0, rep=0):
        pairs = [
            (m * self.reps + r, (m ^ mod) * self.reps + (r ^ rep))
            for m in range(self.mods)
            for r in range(self.reps)
        ]
        return lax.ppermute(value, AXES, pairs)


CORE, X, Y, Z0, Z1 = {"rep": 1}, {"rep": 2}, {"mod": 1}, {"mod": 2}, {"mod": 4}
Z01, XY = {"mod": 6}, {"rep": 2, "mod": 1}


def tie(value, *deps):
    return lax.optimization_barrier((value,) + deps)[0]


def joined(*parts):
    return jnp.concatenate(parts, axis=0)


def gather_z(grid, piece):
    parts = [piece] + [grid.swap(piece, **bit) for bit in (Z0, Z1, Z01)]
    return jnp.stack(parts)


def reduce_z(grid, parts):
    total = parts[0]
    for part, bit in zip(parts[1:], (Z0, Z1, Z01)):
        total = total + grid.swap(part, **bit)
    return total


def per_device(
    raw_rows,
    recv_counts,
    slot_groups,
    read_counts,
    patch_convolution_weight,
    patch_stem_bias_vector,
    language_projection_weight,
    language_bias_vector,
    readout_table,
    attn_gain,
    attn_bias,
    qkv_weight,
    out_weight,
    mlp_gain,
    mlp_bias,
    up_weight,
    up_bias,
    down_weight,
    down_bias,
    out_cotangent,
):
    mods, reps = lax.axis_size("mod"), lax.axis_size("rep")
    fast = mods == 8 and reps == 4
    places = mods if fast else 1
    grid = Grid(mods, reps)
    block_rows = raw_rows.shape[1]
    capacity = mods * block_rows
    total = capacity + PAD
    slots = out_cotangent.shape[1]
    units = up_bias.shape[0] // (4 * mods)
    image = (grid.mod < 3 * mods // 4).astype(jnp.int32).reshape(1)
    rank = grid.rep if fast else jnp.zeros((), jnp.int32)
    ids = jnp.stack([rank, grid.mod if fast else jnp.zeros((), jnp.int32)]).astype(jnp.int32)
    group_row = slot_groups
    group_col = slot_groups.reshape(capacity, 1)
    marks = (recv_counts, read_counts, group_row, group_col)

    by_rank = lambda w: w.reshape(w.shape[0], -1, 4, units).transpose(2, 0, 1, 3).reshape(4, -1, D)
    up_bias_rows = up_bias.reshape(-1, 4, units).transpose(1, 0, 2).reshape(4, D)

    if fast:
        piece = lax.dynamic_slice_in_dim(
            jnp.concatenate([qkv_weight, out_weight], axis=1), rank * D, D, 1
        )
        quarter = down_weight.shape[0] // 4
        piece_up = lax.dynamic_index_in_dim(
            up_weight.reshape(-1, mods, 4, units), rank, 2, keepdims=False
        ).reshape(-1, D)
        piece_down = lax.dynamic_slice_in_dim(down_weight, rank * quarter, quarter, 0)
        first_z = gather_z(grid, piece)
        up_z = gather_z(grid, tie(piece_up, first_z))
        raw_rows = tie(raw_rows, first_z)
    received = lax.all_to_all(raw_rows, "mod", split_axis=0, concat_axis=0, tiled=True)
    rows = received.reshape(capacity, D)
    branch, down_bias_grad = prepare(out_cotangent[0], recv_counts, read_counts, block_rows, total)
    if fast:
        first0 = joined(first_z, grid.swap(first_z, **Y))
        first2 = grid.swap(first0, **X)
        first1 = grid.swap(first0, **CORE)
        first3 = grid.swap(first2, **CORE)
        first = (first0, first1, first2, first3)
        up0 = joined(up_z, grid.swap(tie(up_z, first0), **Y))
        rows, up0 = lax.optimization_barrier((rows, up0))
    else:
        whole = lambda w: lax.all_gather(w, "mod", axis=0, tiled=True)
        every = jnp.concatenate([whole(qkv_weight), whole(out_weight)], axis=1)
        first = tuple(every[None, :, r * D : (r + 1) * D] for r in range(4))
        every = by_rank(whole(up_weight))
        up0, up1, up2, up3 = (every[r : r + 1] for r in range(4))
        every = whole(down_weight).reshape(mods, 4, units, D).transpose(1, 0, 2, 3)
        every = every.reshape(4, D, D)
        down0, down1, down2, down3 = (every[r : r + 1] for r in range(4))

    stream, normed = stems(
        rows,
        patch_convolution_weight,
        patch_stem_bias_vector,
        language_projection_weight,
        language_bias_vector,
        readout_table,
        attn_gain,
        attn_bias,
    )
    deps = ()
    if fast:
        down_z = gather_z(grid, tie(piece_down, rows))
        up2 = grid.swap(tie(up0, first2, rows), **X)
        deps = (down_z,)
    qkv = project_qkv(ids, normed, first)
    mixed, lse, lse_read = attend(qkv, *marks, block_rows, deps)
    deps = ()
    if fast:
        down0 = joined(down_z, grid.swap(tie(down_z, qkv), **Y))
        up1 = grid.swap(tie(up0, qkv), **CORE)
        deps = (down0, up1, up2)
    after, normed2 = out_project(ids, mixed, first, stream, mlp_gain, mlp_bias, deps)
    if fast:
        down2 = grid.swap(tie(down0, up2), **X)
        down1 = grid.swap(down0, **CORE)
        up3 = grid.swap(tie(up2, mixed), **CORE)
        deps = (up3,)
    sums = jnp.zeros((4, D), F32)
    step = lambda ks, state, weights, first_call, last_call, deps: mlp(
        ids, ks, recv_counts, read_counts, normed2, branch, up_bias_rows, down_bias, state,
        weights, block_rows, slots, first_call, last_call, deps,
    )
    active01, hidden01, outer, inner, sums = step(
        (0, 1), (after, after, sums), ((up0, down0), (up1, down1)), True, False, deps
    )
    spec = column_spec(total)
    at = [act_spec(total, i) for i in range(2)]
    deps = ()
    if fast:
        down3 = grid.swap(tie(down2, inner), **CORE)
    give1 = give_products(
        ids, [(normed2, hidden01), (active01, branch)], [(spec, at[1]), (at[1], spec)], places
    )
    active23, hidden23, outer, inner, sums = step(
        (2, 3), (outer, inner, sums), ((up2, down2), (up3, down3)), False, True, (give1,)
    )
    layer_out = outer[:slots].astype(BF16)[None]
    give3 = give_products(
        ids, [(normed2, hidden23), (active23, branch)], [(spec, at[1]), (at[1], spec)], places
    )
    if fast:
        got1, got3 = grid.swap(give1, **CORE), grid.swap(give3, **CORE)
    else:
        got1, got3 = jnp.zeros_like(give1), jnp.zeros_like(give3)
    after_grad, attn_grad, mixed_grad, mlp_sums = out_back(
        ids, inner, after, branch, mlp_gain, first, (give3,)
    )
    keep_down, give_down = keep_products(
        ids, [(active01, branch), (active23, branch)], [(at[0], spec)] * 2, (got1, got3), 1,
        places, False, (attn_grad,)
    )
    keep_up, give_up = keep_products(
        ids, [(normed2, hidden01), (normed2, hidden23)], [(spec, at[0])] * 2, (got1, got3), 0,
        places, True, (keep_down,)
    )
    grads_a = attend_back(
        qkv, mixed, mixed_grad, lse, lse_read, *marks, block_rows, 0, (keep_up,)
    )
    first_a13 = first_give(ids, 0, normed, mixed, grads_a, attn_grad, places)
    deps = (first_a13,)
    if fast:
        got = grid.swap(give_down, **X)
        down_y = (keep_down[0] + got[0], keep_down[1] + got[1])
        got = grid.swap(give_up, **Y)
        up_x = (keep_up[0] + got[0], keep_up[1] + got[1])
        got_a = grid.swap(first_a13, **CORE)
        deps = deps + down_y + up_x
    else:
        got_a = jnp.zeros_like(first_a13)
    grads_b = attend_back(
        qkv, mixed, mixed_grad, lse, lse_read, *marks, block_rows, 1, deps
    )
    deps = (grads_b,)
    if fast:
        got_up = grid.swap(tie(up_x[1], grads_a), **X)
        got_down = grid.swap(tie(down_y[1], grads_a), **Y)
        up_w = [up_x[0][i] + got_up[i] for i in range(4)]
        down_w = [down_y[0][i] + got_down[i] for i in range(4)]
        deps = deps + (got_up, got_down)
    keep_a, give_a = first_keep(
        ids, 0, normed, mixed, grads_a, attn_grad, got_a, places, False, deps
    )
    first_b13 = first_give(ids, 1, normed, mixed, grads_b, attn_grad, places, (keep_a,))
    deps = (first_b13,)
    if fast:
        got_b = grid.swap(first_b13, **CORE)
        deps = deps + (got_b,)
    else:
        got_b = jnp.zeros_like(first_b13)
    embedded_grad, readout_grad, attn_sums = qkv_back(
        ids, (grads_a, grads_b), first, stream, attn_gain, after_grad, deps
    )
    returned = lax.all_to_all(
        embedded_grad.reshape(raw_rows.shape), "mod", split_axis=0, concat_axis=0, tiled=True
    )
    deps = ()
    if fast:
        got = grid.swap(tie(give_a, first_b13), **X)
        own_a, pass_a = keep_a[0] + got[0], keep_a[1] + got[1]
        both = jnp.stack([reduce_z(grid, up_w), reduce_z(grid, down_w)])
        deps = (own_a, pass_a, both)
    stem_keep, stem_give, stem_sums = stem_back(ids, rows, embedded_grad, places, deps)
    keep_b, give_b = first_keep(
        ids, 1, normed, mixed, grads_b, attn_grad, got_b, places, False, (stem_keep,)
    )
    raw_grad = raw_back(
        image,
        returned.reshape(capacity, D),
        patch_convolution_weight,
        language_projection_weight,
    ).reshape(raw_rows.shape)

    small = jnp.concatenate(
        [stem_sums, attn_sums, mlp_sums, down_bias_grad, sums, readout_grad], axis=0
    )
    if fast:
        together = lambda *values: lax.optimization_barrier(values)
        got_y = grid.swap(tie(pass_a, stem_keep), **Y)
        got = grid.swap(stem_give, **CORE)
        got_small = grid.swap(small, **CORE)
        parts = [stem_keep[4 * i : 4 * i + 4] + got[4 * i : 4 * i + 4] for i in range(4)]
        small = small + got_small
        *parts, small, give_b, both = together(*parts, small, give_b, both)
        got = [grid.swap(part, **bit) for part, bit in zip(parts[1:], (Y, X, XY))]
        got_small = grid.swap(small, **X)
        got_x = grid.swap(give_b, **X)
        from_x = grid.swap(both, **X)
        parts = [parts[0][i] + got[0][i] + got[1][i] + got[2][i] for i in range(4)]
        small = small + got_small
        own_b, pass_b = keep_b[0] + got_x[0], keep_b[1] + got_x[1]
        own_a = own_a + got_y
        *parts, small, pass_b, own_b, own_a, from_x, returned_ = together(
            *parts, small, pass_b, own_b, own_a, from_x, returned
        )
        got_y = grid.swap(pass_b, **Y)
        got_small = grid.swap(small, **Y)
        from_core = grid.swap(jnp.stack([both, from_x]), **CORE)
        piece = reduce_z(grid, parts)
        small = small + got_small
        own_b = own_b + got_y
        lasts = [jnp.concatenate([own_a[i], own_b[i]], axis=1) for i in range(4)]
        piece, small, from_core, *lasts = together(piece, small, from_core, *lasts)
        got_small = grid.swap(small, **Z0)
        piece = gather_z(grid, piece)
        small = small + got_small
        last = reduce_z(grid, lasts)
        piece, small, last = together(piece, small, last)
        got_small = grid.swap(small, **Z1)
        last_x = grid.swap(last, **X)
        piece = joined(piece, *[grid.swap(piece, **bit) for bit in (Y, X, XY)])
        small = small + got_small
        piece, last_x = together(piece, last_x)
        last_core = grid.swap(jnp.stack([last, last_x]), **CORE)
        patch_sum, lang_sum = stem_out(ids, piece, grid.swap(piece, **CORE))
        up_sum, down_sum = mlp_out(ids, both, from_x, from_core, places)
        qkv_sum, out_sum = first_out(ids, last, last_x, last_core)
    else:
        reduced = lambda v: lax.psum(
            lax.psum_scatter(v, "mod", scatter_dimension=0, tiled=True), "rep"
        ).astype(F32)
        every = []
        for keep, other, give in ((keep_a, first_a13, give_a), (keep_b, first_b13, give_b)):
            every.append(jnp.stack([keep[0, 0], other[0, 0], give[0, 0], other[1, 0]], axis=1))
        every = reduced(jnp.concatenate(every, axis=2).reshape(D, -1))
        qkv_sum, out_sum = every[:, : 3 * D], every[:, 3 * D :]
        every = jnp.stack([keep_up[0, 0], give1[0, 0], keep_up[1, 0], give3[0, 0]])
        every = every.reshape(4, D, mods, units).transpose(1, 2, 0, 3).reshape(D, -1)
        up_sum = reduced(every)
        every = jnp.stack([keep_down[0, 0], give1[1, 0], give_down[0, 0], give3[1, 0]])
        every = every.reshape(4, mods, units, D).transpose(1, 0, 2, 3).reshape(-1, D)
        down_sum = reduced(every)
        small = lax.psum(small, AXES)
        patch_sum = lax.psum(stem_keep[0].astype(F32), AXES)
        lang_sum = lax.psum(stem_give[0].astype(F32), AXES)
    up_bias_sum = small[7:11].reshape(4, -1, units).transpose(1, 0, 2).reshape(-1)
    return (
        layer_out,
        raw_grad,
        patch_sum,
        small[0],
        lang_sum,
        small[1],
        small[11 : 11 + RD],
        small[2],
        small[3],
        qkv_sum,
        out_sum,
        small[4],
        small[5],
        up_sum,
        up_bias_sum,
        down_sum,
        small[6],
    )


def solution(mesh):
    both, rows, rep = P("mod", "rep", None), P("mod", None), P()
    pair = P("mod", "rep")
    return jax.shard_map(
        per_device,
        mesh=mesh,
        in_specs=(both, pair, pair, pair)
        + (rep,) * 7
        + (rows, rows, rep, rep, rows, rep, rows, rep, both),
        out_specs=(both, both)
        + (rep,) * 7
        + (rows, rows, rep, rep, rows, rep, rows, rep),
        check_vma=False,
    )
```

```python
import functools

import jax
import jax.numpy as jnp
from jax import lax
from jax.experimental import pallas as pl
from jax.experimental.pallas import tpu as pltpu
from jax.sharding import PartitionSpec as P

D = 768
HEADS = 12
HD = 64
RPS = 4
RD = 8
PAD = 16
PART = D // 2
SMALL = 24
LANES = 128
CHUNK = 384
FB = 768
EPS = 1e-6
NEG = -1e30
F32 = jnp.float32
BF16 = jnp.bfloat16
AXES = ("mod", "rep")
SCALE = HD ** (-0.5)
VMEM = pl.BlockSpec(memory_space=pltpu.VMEM)
SMEM = pl.BlockSpec(memory_space=pltpu.SMEM)
ANY = pl.BlockSpec(memory_space=pl.ANY)


def nn(left, right):
    return lax.dot_general(left, right, (((1,), (0,)), ((), ())), preferred_element_type=F32)


def nt(left, right):
    return lax.dot_general(left, right, (((1,), (1,)), ((), ())), preferred_element_type=F32)


def tn(left, right):
    return lax.dot_general(left, right, (((0,), (0,)), ((), ())), preferred_element_type=F32)


def line(vector):
    return vector[...].reshape(1, -1)


def chunks(rows):
    count = rows // CHUNK
    return [
        (i * CHUNK, (rows - i * CHUNK) if i == count - 1 else CHUNK) for i in range(count)
    ]


def normalise(rows):
    mean = jnp.mean(rows, axis=-1, keepdims=True)
    centred = rows - mean
    var = jnp.mean(centred * centred, axis=-1, keepdims=True)
    rstd = lax.rsqrt(var + EPS)
    return centred * rstd, rstd


def norm_input_grad(xhat, rstd, gain, upstream):
    scaled = upstream * gain
    first = jnp.mean(scaled, axis=-1, keepdims=True)
    second = jnp.mean(scaled * xhat, axis=-1, keepdims=True)
    return rstd * (scaled - first - xhat * second)


def call(kernel, out_shape, deps=(), **kw):
    limit = kw.pop("vmem", 20)
    estimate = kw.pop("cost", None)
    in_specs = kw.pop("in_specs")
    count, more = len(in_specs), len(deps)

    def body(*refs):
        kernel(*refs[:count], *refs[count + more :])

    built = pl.pallas_call(
        body,
        out_shape=out_shape,
        in_specs=list(in_specs) + [ANY] * more,
        cost_estimate=estimate,
        compiler_params=pltpu.CompilerParams(vmem_limit_bytes=limit * 1024 * 1024),
        **kw,
    )
    return lambda *args: built(*args, *deps)


def cost(us):
    return pl.CostEstimate(flops=int(us * 1.15e9), bytes_accessed=1 << 20, transcendentals=0)


def struct(shape, dtype):
    return jax.ShapeDtypeStruct(shape, dtype)


def live_of(index, counts, read, block_rows):
    groups_n = counts.shape[1]
    capacity = groups_n * block_rows
    live = index < 0
    for s in range(groups_n):
        live = live | ((index >= s * block_rows) & (index < s * block_rows + counts[0, s]))
    slot = index - capacity
    return live | ((slot >= 0) & (slot < RD) & (slot % RPS < read[0, 0]))


def place_bits(place, places):
    if places == 1:
        return 0
    return (place >> 2) + 2 * (place & 3)


def place_of(bits):
    return ((bits & 1) << 2) | (bits >> 1)


def fetch(ids, arrays, want, target, sem):
    places, rows = arrays[0].shape[0], arrays[0].shape[1]
    for k in range(4):

        @pl.when((ids[0] ^ k) == want)
        def _():
            fetch_array(ids, arrays[k], target, sem)


def fetch_array(ids, array, target, sem, in_order=False):
    places, rows = array.shape[0], array.shape[1]
    for place in range(places):
        shard = place if in_order else ids[1] ^ place_bits(place, places)
        start = shard * rows if in_order else pl.multiple_of(shard * rows, 16)
        pltpu.make_async_copy(array.at[place], target.at[pl.ds(start, rows), :], sem).start()


def fetched(target, sem):
    pltpu.make_async_copy(target, target, sem).wait()


def stem_kernel(cut, raw, wp, bp, wl, bl, table, gain, bias, stream, normed):
    capacity = raw.shape[0]
    step = capacity // 4
    for start in range(0, capacity, step):
        weight, shift = (wp, bp) if start < cut else (wl, bl)
        rows = pl.ds(start, step)
        embedded = (nn(raw[rows, :], weight[...]) + line(shift)).astype(BF16).astype(F32)
        stream[rows, :] = embedded
        xhat, _ = normalise(embedded)
        normed[rows, :] = (xhat * line(gain) + line(bias)).astype(BF16)
    tail = jnp.concatenate([table[...], jnp.zeros((PAD - RD, D), F32)], axis=0)
    stream[pl.ds(capacity, PAD), :] = tail
    xhat, _ = normalise(tail)
    normed[pl.ds(capacity, PAD), :] = (xhat * line(gain) + line(bias)).astype(BF16)


def stems(raw, wp, bp, wl, bl, table, gain, bias):
    capacity = raw.shape[0]
    total = capacity + PAD
    return call(
        functools.partial(stem_kernel, 3 * capacity // 4),
        (struct((total, D), F32), struct((total, D), BF16)),
        in_specs=[VMEM] * 8,
        out_specs=(VMEM, VMEM),
        cost=cost(5),
    )(raw, wp, bp, wl, bl, table, gain, bias)


def qkv_kernel(ids, rows, w0, w1, w2, w3, out, buffer, sem):
    for r in range(3):
        fetch(ids, (w0, w1, w2, w3), r, buffer.at[r], sem.at[r])
    for r in range(3):
        fetched(buffer.at[r], sem.at[r])
        for start, size in chunks(rows.shape[0]):
            out[r, pl.ds(start, size), :] = nn(rows[pl.ds(start, size), :], buffer[r]).astype(BF16)


def project_qkv(ids, normed, weights, deps=()):
    total = normed.shape[0]
    return call(
        qkv_kernel,
        struct((3, total, D), BF16),
        deps,
        in_specs=[SMEM, VMEM, ANY, ANY, ANY, ANY],
        out_specs=VMEM,
        scratch_shapes=[pltpu.VMEM((3, D, D), BF16), pltpu.SemaphoreType.DMA((3,))],
        cost=cost(7),
    )(ids, normed, *weights)


def visible_readout(group_row, live_row):
    capacity = group_row.shape[1]
    query = lax.broadcasted_iota(jnp.int32, (RD, capacity), 0)
    group = 2 * (query // RPS + 1) + 1
    keys = group_row[...]
    seen = live_row & (keys <= group) & ((keys % 2 == 0) | (keys == group))
    return jnp.where(seen, 0.0, NEG)


def visible_between(read):
    query = lax.broadcasted_iota(jnp.int32, (RD, PAD), 0)
    key = lax.broadcasted_iota(jnp.int32, (RD, PAD), 1)
    live = (key < RD) & (key % RPS < read[0, 0])
    seen = (query == key) | (live & (query // RPS == key // RPS))
    return jnp.where(seen, 0.0, NEG)


def tiled(rows, heads):
    return jnp.concatenate([rows] * heads, axis=0)


def own_head(heads):
    row = lax.broadcasted_iota(jnp.int32, (heads * RD, heads * HD), 0) // RD
    lane = lax.broadcasted_iota(jnp.int32, (heads * RD, heads * HD), 1) // HD
    return row == lane


def fold_heads(stack, mine):
    kept = jnp.where(mine, stack, 0.0)
    total = kept[:RD]
    for start in range(RD, stack.shape[0], RD):
        total = total + kept[start : start + RD]
    return jnp.concatenate([total, jnp.zeros((PAD - RD, stack.shape[1]), F32)], axis=0)


def attend_kernel(
    block_rows, qkv, counts, read, group_row, group_col, mixed, lse, lse_read, mask, lse_cols, tail
):
    step = pl.program_id(0)
    capacity = group_row.shape[1]

    @pl.when(step == 0)
    def _():
        slot_row = lax.broadcasted_iota(jnp.int32, (1, capacity), 1)
        live_row = live_of(slot_row, counts, read, block_rows)
        keys = group_row[...]
        for start in range(0, capacity, CHUNK):
            query = lax.broadcasted_iota(jnp.int32, (CHUNK, capacity), 0) + start
            group = group_col[pl.ds(start, CHUNK), :]
            seen = live_row & (keys <= group) & ((keys % 2 == 0) | (keys == group))
            seen = seen | (query == slot_row)
            mask[pl.ds(start, CHUNK), :] = jnp.where(seen, 0.0, NEG)
        lse_cols[...] = jnp.zeros_like(lse_cols)
        mine = own_head(HEADS)
        tail_rows = pl.ds(capacity, PAD)
        head_rows = pl.ds(0, capacity)
        query = qkv[0, tail_rows, :].astype(F32)[:RD] * SCALE
        query = jnp.where(mine, tiled(query, HEADS), 0.0).astype(BF16)
        far = nt(query, qkv[1, head_rows, :]) + tiled(visible_readout(group_row, live_row), HEADS)
        near = nt(query, qkv[1, tail_rows, :]) + tiled(visible_between(read), HEADS)
        peak = jnp.maximum(
            jnp.max(far, axis=1, keepdims=True), jnp.max(near, axis=1, keepdims=True)
        )
        far = jnp.exp(far - peak)
        near = jnp.exp(near - peak)
        total = jnp.sum(far, axis=1, keepdims=True) + jnp.sum(near, axis=1, keepdims=True)
        out = nn(far.astype(BF16), qkv[2, head_rows, :]) + nn(
            near.astype(BF16), qkv[2, tail_rows, :]
        )
        tail[...] = fold_heads(out / total, mine)
        lse_read[...] = jnp.broadcast_to(peak + jnp.log(total), lse_read.shape)

    lane = lax.broadcasted_iota(jnp.int32, (1, LANES), 1)
    columns = pl.ds(pl.multiple_of(step * LANES, LANES), LANES)
    keys = qkv[1, pl.ds(0, capacity), columns]
    values = qkv[2, pl.ds(0, capacity), columns]
    for start in range(0, capacity, CHUNK):
        rows = pl.ds(start, CHUNK)
        query = qkv[0, rows, columns] * SCALE
        outs = []
        logs = lse_cols[rows, :]
        for head in range(2):
            chosen = jnp.where(lane // HD == head, query, jnp.zeros_like(query))
            scores = nt(chosen.astype(BF16), keys) + mask[rows, :]
            peak = jnp.max(scores, axis=1, keepdims=True)
            weight = jnp.exp(scores - peak)
            total = jnp.sum(weight, axis=1, keepdims=True)
            outs.append(nn(weight.astype(BF16), values) / total)
            logs = jnp.where(lane == 2 * step + head, peak + jnp.log(total), logs)
        mixed[rows, :] = jnp.where(lane < HD, outs[0], outs[1]).astype(BF16)
        lse_cols[rows, :] = logs
    mixed[pl.ds(capacity, PAD), :] = tail[:, columns].astype(BF16)

    @pl.when(step == pl.num_programs(0) - 1)
    def _():
        lse[...] = lse_cols[...].T[: lse.shape[0], :]


def attend(qkv, counts, read, group_row, group_col, block_rows, deps=()):
    total = qkv.shape[1]
    capacity = total - PAD
    pairs = HEADS // 2
    return call(
        functools.partial(attend_kernel, block_rows),
        (
            struct((total, D), BF16),
            struct((16, capacity), F32),
            struct((HEADS * RD, LANES), F32),
        ),
        deps,
        grid=(pairs,),
        in_specs=[VMEM, SMEM, SMEM, VMEM, VMEM],
        out_specs=(pl.BlockSpec((total, LANES), lambda j: (0, j)), VMEM, VMEM),
        scratch_shapes=[
            pltpu.VMEM((capacity, capacity), F32),
            pltpu.VMEM((capacity, LANES), F32),
            pltpu.VMEM((PAD, D), F32),
        ],
        cost=cost(21),
    )(qkv, counts, read, group_row, group_col)


def attend_back_kernel(
    block_rows,
    part,
    qkv,
    mixed,
    grad,
    lse,
    lse_read,
    counts,
    read,
    group_row,
    group_col,
    out,
    mask,
    delta,
    key_more,
    value_more,
    tails,
):
    step = pl.program_id(0)
    capacity = group_row.shape[1]
    tail_rows = pl.ds(capacity, PAD)
    head_rows = pl.ds(0, capacity)
    heads = PART // HD
    mine_columns = pl.ds(part * PART, PART)

    @pl.when(step == 0)
    def _():
        slot_row = lax.broadcasted_iota(jnp.int32, (1, capacity), 1)
        group = group_row[...]
        for start in range(0, capacity, CHUNK):
            slot = lax.broadcasted_iota(jnp.int32, (CHUNK, 1), 0) + start
            live = live_of(slot, counts, read, block_rows)
            keys = group_col[pl.ds(start, CHUNK), :]
            seen = live & (keys <= group) & ((keys % 2 == 0) | (keys == group))
            seen = seen | (slot == slot_row)
            mask[pl.ds(start, CHUNK), :] = jnp.where(seen, 0.0, NEG)
        head = lax.broadcasted_iota(jnp.int32, (8, PART), 0)
        column = lax.broadcasted_iota(jnp.int32, (8, PART), 1)
        select = jnp.where(column // HD == head, 1.0, 0.0).astype(BF16)
        for start in range(0, capacity, CHUNK):
            rows = pl.ds(start, CHUNK)
            product = grad[rows, mine_columns].astype(F32) * mixed[rows, mine_columns].astype(F32)
            high = product.astype(BF16)
            low = (product - high.astype(F32)).astype(BF16)
            delta[:, rows] = nt(select, high) + nt(select, low)

        live_row = live_of(slot_row, counts, read, block_rows)
        mine = own_head(heads)
        query = qkv[0, tail_rows, mine_columns].astype(F32)[:RD] * SCALE
        query = jnp.where(mine, tiled(query, heads), 0.0).astype(BF16)
        upper = grad[tail_rows, mine_columns].astype(F32)[:RD]
        upper = jnp.where(mine, tiled(upper, heads), 0.0)
        result = tiled(mixed[tail_rows, mine_columns].astype(F32)[:RD], heads)
        row_delta = jnp.sum(upper * result, axis=1, keepdims=True)
        upper = upper.astype(BF16)
        logs = lse_read[pl.ds(part * heads * RD, heads * RD), 0:1]
        far = nt(query, qkv[1, head_rows, mine_columns]) + tiled(visible_readout(group_row, live_row), heads)
        near = nt(query, qkv[1, tail_rows, mine_columns]) + tiled(visible_between(read), heads)
        far = jnp.exp(far - logs)
        near = jnp.exp(near - logs)
        far_grad = (far * (nt(upper, qkv[2, head_rows, mine_columns]) - row_delta)).astype(BF16)
        near_grad = (near * (nt(upper, qkv[2, tail_rows, mine_columns]) - row_delta)).astype(BF16)
        query_grad = nn(far_grad, qkv[1, head_rows, mine_columns]) + nn(near_grad, qkv[1, tail_rows, mine_columns])
        tails[0] = fold_heads(query_grad, mine) * SCALE
        tails[1] = tn(near_grad, query)
        tails[2] = tn(near.astype(BF16), upper)
        key_more[...] = tn(far_grad, query)
        value_more[...] = tn(far.astype(BF16), upper)

    lane = lax.broadcasted_iota(jnp.int32, (1, LANES), 1)
    columns = pl.ds(pl.multiple_of(step * LANES, LANES), LANES)
    here = pl.ds(pl.multiple_of(part * PART + step * LANES, LANES), LANES)
    query = (qkv[0, head_rows, here] * SCALE).astype(BF16)
    upper = grad[head_rows, here]
    query_grad = jnp.zeros((capacity, LANES), F32)
    for start in range(0, capacity, CHUNK):
        rows = pl.ds(start, CHUNK)
        all_keys = qkv[1, rows, here]
        all_values = qkv[2, rows, here]
        key_parts = []
        value_parts = []
        for head in range(2):
            own = lane // HD == head
            keys = jnp.where(own, all_keys, jnp.zeros_like(all_keys))
            values = jnp.where(own, all_values, jnp.zeros_like(all_values))
            logs = lse[pl.ds(part * heads + 2 * step + head, 1), :]
            row_delta = delta[pl.ds(2 * step + head, 1), :]
            probs = jnp.exp(nt(keys, query) + mask[rows, :] - logs)
            score_grad = (probs * (nt(values, upper) - row_delta)).astype(BF16)
            value_parts.append(nn(probs.astype(BF16), upper))
            key_parts.append(nn(score_grad, query))
            query_grad = query_grad + tn(score_grad, keys)
        key_grad = jnp.where(lane < HD, key_parts[0], key_parts[1]) + key_more[rows, columns]
        value_grad = jnp.where(lane < HD, value_parts[0], value_parts[1]) + value_more[rows, columns]
        out[1, rows, :] = key_grad.astype(BF16)
        out[2, rows, :] = value_grad.astype(BF16)
    out[0, head_rows, :] = (query_grad * SCALE).astype(BF16)
    for part in range(3):
        out[part, tail_rows, :] = tails[part, :, columns].astype(BF16)


def attend_back(
    qkv, mixed, grad, lse, lse_read, counts, read, group_row, group_col, block_rows, part,
    deps=()
):
    total = qkv.shape[1]
    capacity = total - PAD
    pairs = PART // LANES
    return call(
        functools.partial(attend_back_kernel, block_rows, part),
        struct((3, total, PART), BF16),
        deps,
        grid=(pairs,),
        in_specs=[VMEM, VMEM, VMEM, VMEM, VMEM, SMEM, SMEM, VMEM, VMEM],
        out_specs=pl.BlockSpec((3, total, LANES), lambda j: (0, 0, j)),
        scratch_shapes=[
            pltpu.VMEM((capacity, capacity), F32),
            pltpu.VMEM((8, capacity), F32),
            pltpu.VMEM((capacity, PART), F32),
            pltpu.VMEM((capacity, PART), F32),
            pltpu.VMEM((3, PAD, PART), F32),
        ],
        cost=cost(15),
    )(qkv, mixed, grad, lse, lse_read, counts, read, group_row, group_col)


def out_kernel(ids, mixed, w0, w1, w2, w3, stream, gain, bias, after, normed, buffer, sem):
    fetch(ids, (w0, w1, w2, w3), 3, buffer, sem)
    fetched(buffer, sem)
    for start, size in chunks(mixed.shape[0]):
        rows = pl.ds(start, size)
        value = stream[rows, :] + nn(mixed[rows, :], buffer[...])
        after[rows, :] = value
        xhat, _ = normalise(value)
        normed[rows, :] = (xhat * line(gain) + line(bias)).astype(BF16)


def out_project(ids, mixed, weights, stream, gain, bias, deps=()):
    total = mixed.shape[0]
    return call(
        out_kernel,
        (struct((total, D), F32), struct((total, D), BF16)),
        deps,
        in_specs=[SMEM, VMEM, ANY, ANY, ANY, ANY, VMEM, VMEM, VMEM],
        out_specs=(VMEM, VMEM),
        scratch_shapes=[pltpu.VMEM((D, D), BF16), pltpu.SemaphoreType.DMA],
        cost=cost(6.4),
    )(ids, mixed, *weights, stream, gain, bias)


def out_back_kernel(
    ids, inner, after, branch, gain, w0, w1, w2, w3, grad, grad_low, mixed_grad, sums, buffer, sem
):
    fetch(ids, (w0, w1, w2, w3), 3, buffer, sem)
    fetched(buffer, sem)
    gain_sum = jnp.zeros((1, D), F32)
    bias_sum = jnp.zeros((1, D), F32)
    for start, size in chunks(inner.shape[0]):
        rows = pl.ds(start, size)
        upstream = inner[rows, :]
        xhat, rstd = normalise(after[rows, :])
        gain_sum = gain_sum + jnp.sum(upstream * xhat, axis=0, keepdims=True)
        bias_sum = bias_sum + jnp.sum(upstream, axis=0, keepdims=True)
        total = branch[rows, :].astype(F32) + norm_input_grad(xhat, rstd, line(gain), upstream)
        grad[rows, :] = total
        low = total.astype(BF16)
        grad_low[rows, :] = low
        mixed_grad[rows, :] = nt(low, buffer[...]).astype(BF16)
    sums[0:1, :] = gain_sum
    sums[1:2, :] = bias_sum


def out_back(ids, inner, after, branch, gain, weights, deps=()):
    total = inner.shape[0]
    return call(
        out_back_kernel,
        (
            struct((total, D), F32),
            struct((total, D), BF16),
            struct((total, D), BF16),
            struct((2, D), F32),
        ),
        deps,
        in_specs=[SMEM, VMEM, VMEM, VMEM, VMEM, ANY, ANY, ANY, ANY],
        out_specs=(VMEM, VMEM, VMEM, VMEM),
        scratch_shapes=[pltpu.VMEM((D, D), BF16), pltpu.SemaphoreType.DMA],
        cost=cost(8.5),
    )(ids, inner, after, branch, gain, *weights)


def prepare_kernel(block_rows, cotangent, counts, read, branch, bias_grad):
    total, slots = branch.shape[0], cotangent.shape[0]
    index = lax.broadcasted_iota(jnp.int32, (total, 1), 0)
    live = jnp.where(live_of(index, counts, read, block_rows), 1.0, 0.0)
    upstream = cotangent[...].astype(F32) * live[:slots]
    bias_grad[...] = jnp.sum(upstream, axis=0, keepdims=True)
    upstream = jnp.concatenate([upstream, jnp.zeros((total - slots, D), F32)], axis=0)
    branch[...] = upstream.astype(BF16)


def prepare(cotangent, counts, read, block_rows, total):
    return call(
        functools.partial(prepare_kernel, block_rows),
        (struct((total, D), BF16), struct((1, D), F32)),
        in_specs=[VMEM, SMEM, SMEM],
        out_specs=(VMEM, VMEM),
        cost=cost(3),
    )(cotangent, counts, read)


def mlp_kernel(
    block_rows,
    ks,
    first,
    last,
    slots,
    *refs,
):
    nk = len(ks)
    ids, counts, read, normed, branch, up_bias, down_bias, total_in, inner_in, sums_in = refs[:10]
    weights = refs[10 : 10 + 2 * nk]
    active, hidden_grad, total, inner, sums = refs[10 + 2 * nk : 15 + 2 * nk]
    up, down, sem = refs[-3:]
    step = pl.program_id(0)
    index = step // (D // FB)
    part = step % (D // FB)
    length = normed.shape[0]

    @pl.when(step == 0)
    def _():
        for i in range(nk):
            fetch_array(ids, weights[2 * i], up.at[i], sem.at[i, 0])
            fetch_array(ids, weights[2 * i + 1], down.at[i], sem.at[i, 1], True)
        sums[...] = sums_in[...]
        if first:
            total[...] = total_in[...] + line(down_bias)
            inner[...] = jnp.zeros_like(inner)
        else:
            total[...] = total_in[...]
            inner[...] = inner_in[...]

    @pl.when(part == 0)
    def _():
        fetched(up.at[index], sem.at[index, 0])
        fetched(down.at[index], sem.at[index, 1])

    columns = pl.ds(pl.multiple_of(part * FB, FB), FB)
    rank = ids[0] ^ ks[0]
    for i in range(1, nk):
        rank = jnp.where(index == i, ids[0] ^ ks[i], rank)
    up_part = up[index, :, columns]
    down_part = down[index, columns, :]
    shift = up_bias[pl.ds(rank, 1), columns]
    bias_sum = jnp.zeros((1, FB), F32)
    for start, size in chunks(length):
        rows = pl.ds(start, size)
        hidden = nn(normed[rows, :], up_part) + shift
        factor = (2.0 / jnp.pi) ** 0.5
        square = hidden * hidden
        bent = jnp.tanh(hidden * (factor + (factor * 0.044715) * square))
        half = 0.5 * (1.0 + bent)
        act = (hidden * half).astype(BF16)
        slope = half + (0.5 * hidden) * (1.0 - bent * bent) * (
            factor + (3.0 * factor * 0.044715) * square
        )
        back = (nt(branch[rows, :], down_part) * slope).astype(BF16)
        bias_sum = bias_sum + jnp.sum(back.astype(F32), axis=0, keepdims=True)
        active[0, rows, :] = act
        hidden_grad[0, rows, :] = back
        total[rows, :] += nn(act, down_part)
        inner[rows, :] += nt(back, up_part)
    sums[pl.ds(rank, 1), columns] = bias_sum

    if last:

        @pl.when(step == pl.num_programs(0) - 1)
        def _():
            at = lax.broadcasted_iota(jnp.int32, (length, 1), 0)
            live = jnp.where(live_of(at, counts, read, block_rows), 1.0, 0.0)
            total[...] = total[...] * live


def mlp(ids, ks, counts, read, normed, branch, up_bias, down_bias, state, weights, block_rows, slots, first, last, deps=()):
    total = normed.shape[0]
    nk = len(ks)
    per = D // FB
    whole = pl.BlockSpec((total, D), lambda j: (0, 0))
    vectors = pl.BlockSpec((4, D), lambda j: (0, 0))
    block = pl.BlockSpec((1, total, FB), lambda j: (j // per, 0, j % per))
    flat = [w for pair in weights for w in pair]
    return call(
        functools.partial(mlp_kernel, block_rows, ks, first, last, slots),
        (
            struct((nk, total, D), BF16),
            struct((nk, total, D), BF16),
            struct((total, D), F32),
            struct((total, D), F32),
            struct((4, D), F32),
        ),
        deps,
        grid=(nk * per,),
        in_specs=[SMEM, SMEM, SMEM, whole, whole, vectors, VMEM, whole, whole, vectors]
        + [ANY] * (2 * nk),
        out_specs=(block, block, whole, whole, vectors),
        scratch_shapes=[
            pltpu.VMEM((nk, D, D), BF16),
            pltpu.VMEM((nk, D, D), BF16),
            pltpu.SemaphoreType.DMA((nk, 2)),
        ],
        cost=cost(20),
    )(ids, counts, read, normed, branch, up_bias, down_bias, *state, *flat)


def put_rows(ids, value, first_row, places, store):
    rows = D // places
    for i in range(value.shape[0] // rows):
        bits = ids[1] ^ (first_row // rows + i)
        store(place_of(bits) if places > 1 else 0, value[i * rows : (i + 1) * rows])


def product_rows(ids, left, right, places, store):
    block = D // 2 if places > 1 else D
    for start in range(0, D, block):
        value = tn(left[:, start : start + block], right[...])
        put_rows(ids, value, start, places, store)


def to_give_kernel(places, count, ids, *refs):
    lefts, rights, out = refs[:count], refs[count : 2 * count], refs[2 * count]
    for i in range(count):

        def store(place, rows, i=i):
            out[i, pl.ds(place, 1)] = rows.astype(BF16)[None]

        product_rows(ids, lefts[i], rights[i], places, store)


def to_keep_kernel(places, y_first, ids, left0, right0, left2, right2, got0, got2, keep, give):
    half = max(places // 2, 1)
    for x, (left, right) in enumerate(((left0, right0), (left2, right2))):

        def store(place, rows, x=x):
            got = (got0, got2)[x]
            summed = (rows + got[pl.ds(place, 1)][0].astype(F32)).astype(BF16)[None]
            y, z = place // half, place % half
            if y_first:

                @pl.when(y == 0)
                def _():
                    keep[x, pl.ds(z, 1)] = summed

                @pl.when(y == 1)
                def _():
                    give[x, pl.ds(z, 1)] = summed
            else:
                (give if x else keep)[y, pl.ds(z, 1)] = summed

        product_rows(ids, left, right, places, store)


def column_spec(total):
    return pl.BlockSpec((total, D), lambda i: (0, 0))


def act_spec(total, index):
    return pl.BlockSpec((None, total, D), lambda i: (index, 0, 0))


def give_products(ids, pairs, specs, places, deps=()):
    count = len(pairs)
    total = pairs[0][0].shape[-2]
    rows = D // places
    return call(
        functools.partial(to_give_kernel, places, count),
        struct((count, places, rows, D), BF16),
        deps,
        grid=(1,),
        in_specs=[SMEM] + [s[0] for s in specs] + [s[1] for s in specs],
        out_specs=pl.BlockSpec((count, places, rows, D), lambda i: (0, 0, 0, 0)),
        cost=cost(6.5),
    )(ids, *[p[0] for p in pairs], *[p[1] for p in pairs])


def keep_products(ids, pairs, specs, got, index, places, y_first, deps=()):
    total = pairs[0][0].shape[-2]
    rows = D // places
    half = struct((2, max(places // 2, 1), rows, D), BF16)
    half_spec = pl.BlockSpec((2, max(places // 2, 1), rows, D), lambda i: (0, 0, 0, 0))
    return call(
        functools.partial(to_keep_kernel, places, y_first),
        (half, half),
        deps,
        grid=(1,),
        in_specs=[
            SMEM,
            specs[0][0],
            specs[0][1],
            specs[1][0],
            specs[1][1],
            pl.BlockSpec((None, places, rows, D), lambda i: (index, 0, 0, 0)),
            pl.BlockSpec((None, places, rows, D), lambda i: (index, 0, 0, 0)),
        ],
        out_specs=(half_spec, half_spec),
        cost=cost(8),
    )(ids, pairs[0][0], pairs[0][1], pairs[1][0], pairs[1][1], *got)


def first_fetch(ids, k, part, normed, mixed, grads, attn_grad, left, right, sem):
    rank = ids[0] ^ k

    @pl.when(rank < 3)
    def _():
        pltpu.make_async_copy(normed, left, sem.at[0]).start()
        pltpu.make_async_copy(grads.at[rank], right, sem.at[1]).start()

    @pl.when(rank == 3)
    def _():
        pltpu.make_async_copy(mixed, left, sem.at[0]).start()
        pltpu.make_async_copy(attn_grad.at[:, pl.ds(part * PART, PART)], right, sem.at[1]).start()


def first_give_kernel(places, part, ids, normed, mixed, grads, attn_grad, out, left, right, sem):
    ks = (1, 3)
    sources = (normed, mixed, grads, attn_grad)
    for i, k in enumerate(ks):
        first_fetch(ids, k, part, *sources, left.at[i], right.at[i], sem.at[i])
    for i, k in enumerate(ks):
        fetched(left.at[i], sem.at[i, 0])
        fetched(right.at[i], sem.at[i, 1])

        def store(place, rows, i=i):
            out[i, pl.ds(place, 1)] = rows.astype(BF16)[None]

        product_rows(ids, left.at[i], right.at[i], places, store)


def first_scratch(total):
    return [
        pltpu.VMEM((2, total, D), BF16),
        pltpu.VMEM((2, total, PART), BF16),
        pltpu.SemaphoreType.DMA((2, 2)),
    ]


def first_give(ids, part, normed, mixed, grads, attn_grad, places, deps=()):
    total = normed.shape[0]
    return call(
        functools.partial(first_give_kernel, places, part),
        struct((2, places, D // places, PART), BF16),
        deps,
        in_specs=[SMEM, ANY, ANY, ANY, ANY],
        out_specs=VMEM,
        scratch_shapes=first_scratch(total),
        cost=cost(5),
    )(ids, normed, mixed, grads, attn_grad)


def first_keep_kernel(places, part, y_first, ids, normed, mixed, grads, attn_grad, got, *refs):
    keep, give, left, right, sem = refs[-5:]
    sources = (normed, mixed, grads, attn_grad)
    for i, k in enumerate((0, 2)):
        first_fetch(ids, k, part, *sources, left.at[i], right.at[i], sem.at[i])
    for i in range(2):
        fetched(left.at[i], sem.at[i, 0])
        fetched(right.at[i], sem.at[i, 1])
    if len(refs) > 5:
        before = refs[0]
        give[:, :, :, :PART] = before[...]
        give = give.at[:, :, :, pl.ds(PART, PART)]
    to_keep_kernel(
        places, y_first, ids, left.at[0], right.at[0], left.at[1], right.at[1], got.at[0], got.at[1],
        keep, give
    )


def first_keep(
    ids, part, normed, mixed, grads, attn_grad, got, places, y_first, deps=(), before=None
):
    total = normed.shape[0]
    half = struct((2, max(places // 2, 1), D // places, PART), BF16)
    return call(
        functools.partial(first_keep_kernel, places, part, y_first),
        (half, half if before is None else struct(half.shape[:3] + (D,), BF16)),
        deps,
        in_specs=[SMEM, ANY, ANY, ANY, ANY, VMEM] + [VMEM] * (before is not None),
        out_specs=(VMEM, VMEM),
        scratch_shapes=first_scratch(total),
        cost=cost(6),
    )(ids, normed, mixed, grads, attn_grad, got, *([] if before is None else [before]))


def qkv_back_kernel(capacity, ids, grads0, grads1, *refs):
    stream, gain, after_grad, embedded, readout, sums, buffer, sem = refs[4:]
    for r in range(3):
        fetch(ids, refs[:4], r, buffer.at[r], sem.at[r])
    for r in range(3):
        fetched(buffer.at[r], sem.at[r])
    gain_sum = jnp.zeros((1, D), F32)
    bias_sum = jnp.zeros((1, D), F32)
    for start, size in chunks(stream.shape[0]):
        rows = pl.ds(start, size)
        upstream = jnp.zeros((size, D), F32)
        for r in range(3):
            grad = jnp.concatenate([grads0[r, rows, :], grads1[r, rows, :]], axis=1)
            upstream = upstream + nt(grad, buffer[r])
        xhat, rstd = normalise(stream[rows, :])
        gain_sum = gain_sum + jnp.sum(upstream * xhat, axis=0, keepdims=True)
        bias_sum = bias_sum + jnp.sum(upstream, axis=0, keepdims=True)
        total = after_grad[rows, :] + norm_input_grad(xhat, rstd, line(gain), upstream)
        inside = min(size, capacity - start)
        embedded[pl.ds(start, inside), :] = total[:inside].astype(BF16)
        if start + size > capacity:
            readout[...] = total[capacity - start : capacity - start + RD]
    sums[0:1, :] = gain_sum
    sums[1:2, :] = bias_sum


def qkv_back(ids, grads, weights, stream, gain, after_grad, deps=()):
    total = stream.shape[0]
    capacity = total - PAD
    return call(
        functools.partial(qkv_back_kernel, capacity),
        (struct((capacity, D), BF16), struct((RD, D), F32), struct((2, D), F32)),
        deps,
        in_specs=[SMEM, VMEM, VMEM] + [ANY] * 4 + [VMEM, VMEM, VMEM],
        out_specs=(VMEM, VMEM, VMEM),
        scratch_shapes=[pltpu.VMEM((3, D, D), BF16), pltpu.SemaphoreType.DMA((3,))],
        cost=cost(10),
    )(ids, *grads, *weights, stream, gain, after_grad)


def stem_back_kernel(cut, places, ids, raw, embedded, *refs):
    keep, give = refs[-4:-2], refs[-2:]
    rows = D // places // 2
    small = [part[...] for part in refs[:-4]]
    sums = [
        jnp.sum(embedded[part, :].astype(F32), axis=0, keepdims=True)
        for part in (slice(0, cut), slice(cut, None))
    ]
    small = jnp.concatenate(sums + small, axis=0)
    small = jnp.concatenate([small, jnp.zeros((SMALL - small.shape[0], D), F32)], axis=0)
    for stem, part in enumerate((slice(0, cut), slice(cut, None))):
        value = tn(raw[part, :], embedded[part, :])
        mine = (ids[0] & 1) == stem
        for i in range(2 * places):
            place = place_of(ids[1] ^ (i // 2))
            x = (i % 2) ^ (ids[0] >> 1)
            more = jnp.zeros((8, D), F32)
            if stem == 0 and 8 * i < SMALL:
                more = small[8 * i : 8 * i + 8]
            piece = jnp.concatenate([value[i * rows : (i + 1) * rows], more], axis=0)
            piece = piece.astype(BF16)[None]

            for side in range(2):

                @pl.when(mine & (x == side))
                def _():
                    keep[side][pl.ds(place, 1)] = piece

                @pl.when(jnp.logical_not(mine) & (x == side))
                def _():
                    give[side][pl.ds(place, 1)] = piece


def stem_back_plain_kernel(cut, raw, embedded, *refs):
    keep, give, out = refs[-3:]
    sums = [
        jnp.sum(embedded[part, :].astype(F32), axis=0, keepdims=True)
        for part in (slice(0, cut), slice(cut, None))
    ]
    small = jnp.concatenate(sums + [part[...] for part in refs[:-3]], axis=0)
    out[...] = jnp.concatenate([small, jnp.zeros((SMALL - small.shape[0], D), F32)], axis=0)
    keep[0] = tn(raw[:cut, :], embedded[:cut, :]).astype(BF16)
    give[0] = tn(raw[cut:, :], embedded[cut:, :]).astype(BF16)


def stem_back(ids, raw, embedded, small, places, deps=()):
    capacity = raw.shape[0]
    cut = 3 * capacity // 4
    if places == 1:
        return call(
            functools.partial(stem_back_plain_kernel, cut),
            (struct((1, D, D), BF16), struct((1, D, D), BF16), struct((SMALL, D), F32)),
            deps,
            in_specs=[VMEM, VMEM] + [VMEM] * len(small),
            out_specs=(VMEM, VMEM, VMEM),
            cost=cost(6),
        )(raw, embedded, *small)
    shape = (places, D // (2 * places) + 8, D)
    return call(
        functools.partial(stem_back_kernel, cut, places),
        (struct(shape, BF16),) * 4,
        deps,
        in_specs=[SMEM, VMEM, VMEM] + [VMEM] * len(small),
        out_specs=(VMEM,) * 4,
        cost=cost(6),
    )(ids, raw, embedded, *small)


def stem_out_kernel(ids, own, other, patch, lang, small):
    rows = own.shape[1] - 8
    for i in range(own.shape[0]):
        shard = ids[1] ^ place_bits(((i >> 2) & 1) * 4 + (i & 3), 8)
        x = (i >> 3) ^ (ids[0] >> 1)
        slot = shard * 2 + x
        at = pl.ds(pl.multiple_of(slot * rows, 16), rows)
        mine, theirs = own[i].astype(F32), other[i].astype(F32)
        first = (ids[0] & 1) == 0
        pieces = jnp.where(first, mine, theirs), jnp.where(first, theirs, mine)
        patch[at, :] = pieces[0][:rows]
        lang[at, :] = pieces[1][:rows]

        @pl.when(slot * 8 < SMALL)
        def _():
            small[pl.ds(pl.multiple_of(slot * 8, 8), 8), :] = pieces[0][rows:]


def stem_out(ids, own, other):
    return call(
        stem_out_kernel,
        (struct((D, D), F32), struct((D, D), F32), struct((SMALL, D), F32)),
        in_specs=[SMEM, VMEM, VMEM],
        out_specs=(VMEM, VMEM, VMEM),
        cost=cost(4.4),
    )(ids, own, other)


def raw_kernel(image, grad, wp, wl, out):
    @pl.when(image[0] != 0)
    def _():
        out[...] = nt(grad[...], wp[...])

    @pl.when(image[0] == 0)
    def _():
        out[...] = nt(grad[...], wl[...])


def raw_back(image, grad, wp, wl, deps=()):
    return call(
        raw_kernel,
        struct(grad.shape, F32),
        deps,
        in_specs=[SMEM, VMEM, VMEM, VMEM],
        out_specs=VMEM,
        cost=cost(4.6),
    )(image, grad, wp, wl)


def first_out_kernel(ids, k0, k2, k13, qkv, out, ranks):
    ranks[0], ranks[2], ranks[1], ranks[3] = k0[...], k2[...], k13[0], k13[1]
    for r in range(3):
        qkv[:, r * D : (r + 1) * D] = ranks[pl.ds(ids[0] ^ r, 1)][0].astype(F32)
    out[...] = ranks[pl.ds(ids[0] ^ 3, 1)][0].astype(F32)


def first_out(ids, k0, k2, k13):
    rows = k0.shape[0]
    return call(
        first_out_kernel,
        (struct((rows, 3 * D), F32), struct((rows, D), F32)),
        in_specs=[SMEM, VMEM, VMEM, VMEM],
        out_specs=(VMEM, VMEM),
        scratch_shapes=[pltpu.VMEM((4, rows, D), BF16)],
        cost=cost(2.3),
    )(ids, k0, k2, k13)


def mlp_out_kernel(places, ids, k0, k2, k13, up, down, ranks):
    ranks[0], ranks[2], ranks[1], ranks[3] = k0[...], k2[...], k13[0], k13[1]
    rows, unit = k0.shape[1], D // places
    for r in range(4):
        both = ranks[pl.ds(ids[0] ^ r, 1)][0]
        value = both[0].astype(F32)
        for s in range(places):
            start = (4 * s + r) * unit
            up[:, start : start + unit] = value[:, s * unit : (s + 1) * unit]
        down[r * rows : (r + 1) * rows, :] = both[1].astype(F32)


def mlp_out(ids, k0, k2, k13, places):
    rows = k0.shape[1]
    return call(
        functools.partial(mlp_out_kernel, places),
        (struct((rows, 4 * D), F32), struct((4 * rows, D), F32)),
        in_specs=[SMEM, VMEM, VMEM, VMEM],
        out_specs=(VMEM, VMEM),
        scratch_shapes=[pltpu.VMEM((4, 2, rows, D), BF16)],
        cost=cost(3.1),
    )(ids, k0, k2, k13)


class Grid:
    def __init__(self, mods, reps):
        self.mods, self.reps = mods, reps
        self.mod, self.rep = lax.axis_index("mod"), lax.axis_index("rep")

    def swap(self, value, mod=0, rep=0):
        pairs = [
            (m * self.reps + r, (m ^ mod) * self.reps + (r ^ rep))
            for m in range(self.mods)
            for r in range(self.reps)
        ]
        return lax.ppermute(value, AXES, pairs)


CORE, X, Y, Z0, Z1 = {"rep": 1}, {"rep": 2}, {"mod": 1}, {"mod": 2}, {"mod": 4}
Z01, XY = {"mod": 6}, {"rep": 2, "mod": 1}


def tie(value, *deps):
    return lax.optimization_barrier((value,) + deps)[0]


def joined(*parts):
    return jnp.concatenate(parts, axis=0)


def gather_z(grid, piece):
    parts = [piece] + [grid.swap(piece, **bit) for bit in (Z0, Z1, Z01)]
    return jnp.stack(parts)


def double_z(grid, piece):
    value = jnp.stack([piece, grid.swap(piece, **Z0)])
    return joined(value, grid.swap(value, **Z1))


def halve_z(grid, value):
    value = value[:2] + grid.swap(value[2:], **Z1)
    return value[0] + grid.swap(value[1], **Z0)


def reduce_z(grid, parts):
    total = parts[0]
    for part, bit in zip(parts[1:], (Z0, Z1, Z01)):
        total = total + grid.swap(part, **bit)
    return total


def per_device(
    raw_rows,
    recv_counts,
    slot_groups,
    read_counts,
    patch_convolution_weight,
    patch_stem_bias_vector,
    language_projection_weight,
    language_bias_vector,
    readout_table,
    attn_gain,
    attn_bias,
    qkv_weight,
    out_weight,
    mlp_gain,
    mlp_bias,
    up_weight,
    up_bias,
    down_weight,
    down_bias,
    out_cotangent,
):
    mods, reps = lax.axis_size("mod"), lax.axis_size("rep")
    fast = mods == 8 and reps == 4
    places = mods if fast else 1
    grid = Grid(mods, reps)
    block_rows = raw_rows.shape[1]
    capacity = mods * block_rows
    total = capacity + PAD
    slots = out_cotangent.shape[1]
    units = up_bias.shape[0] // (4 * mods)
    image = (grid.mod < 3 * mods // 4).astype(jnp.int32).reshape(1)
    rank = grid.rep if fast else jnp.zeros((), jnp.int32)
    ids = jnp.stack([rank, grid.mod if fast else jnp.zeros((), jnp.int32)]).astype(jnp.int32)
    group_row = slot_groups
    group_col = slot_groups.reshape(capacity, 1)
    marks = (recv_counts, read_counts, group_row, group_col)

    by_rank = lambda w: w.reshape(w.shape[0], -1, 4, units).transpose(2, 0, 1, 3).reshape(4, -1, D)
    up_bias_rows = up_bias.reshape(-1, 4, units).transpose(1, 0, 2).reshape(4, D)

    if fast:
        piece = lax.dynamic_slice_in_dim(
            jnp.concatenate([qkv_weight, out_weight], axis=1), rank * D, D, 1
        )
        quarter = down_weight.shape[0] // 4
        piece_up = lax.dynamic_index_in_dim(
            up_weight.reshape(-1, mods, 4, units), rank, 2, keepdims=False
        ).reshape(-1, D)
        piece_down = lax.dynamic_slice_in_dim(down_weight, rank * quarter, quarter, 0)
        first_z = gather_z(grid, piece)
        first_y = grid.swap(first_z, **Y)
        first_x = grid.swap(first_z, **X)
        up_z = gather_z(grid, tie(piece_up, first_z))
        raw_rows = tie(raw_rows, first_y, up_z)
    received = lax.all_to_all(raw_rows, "mod", split_axis=0, concat_axis=0, tiled=True)
    rows = received.reshape(capacity, D)
    branch, down_bias_grad = prepare(out_cotangent[0], recv_counts, read_counts, block_rows, total)
    if fast:
        first0 = joined(first_z, first_y)
        first2 = joined(first_x, grid.swap(first_y, **X))
        first1 = grid.swap(first0, **CORE)
        first3 = grid.swap(first2, **CORE)
        first = (first0, first1, first2, first3)
        down0 = lax.all_gather(piece_down, "mod", axis=0)
    else:
        whole = lambda w: lax.all_gather(w, "mod", axis=0, tiled=True)
        every = jnp.concatenate([whole(qkv_weight), whole(out_weight)], axis=1)
        first = tuple(every[None, :, r * D : (r + 1) * D] for r in range(4))
        every = by_rank(whole(up_weight))
        up0, up1, up2, up3 = (every[r : r + 1] for r in range(4))
        every = whole(down_weight).reshape(mods, 4, units, D).transpose(1, 0, 2, 3)
        every = every.reshape(4, D, D)
        down0, down1, down2, down3 = (every[r : r + 1] for r in range(4))

    stream, normed = stems(
        rows,
        patch_convolution_weight,
        patch_stem_bias_vector,
        language_projection_weight,
        language_bias_vector,
        readout_table,
        attn_gain,
        attn_bias,
    )
    if fast:
        down2 = grid.swap(tie(down0, first1, first3), **X)
    qkv = project_qkv(ids, normed, first)
    deps = ()
    mixed, lse, lse_read = attend(qkv, *marks, block_rows, deps)
    deps = ()
    if fast:
        down1 = grid.swap(tie(down0, up_z), **CORE)
        up0 = joined(up_z, grid.swap(tie(up_z, first_y), **Y))
        deps = (up0, down1, down2)
    after, normed2 = out_project(ids, mixed, first, stream, mlp_gain, mlp_bias, deps)
    deps = ()
    if fast:
        up1 = grid.swap(up0, **CORE)
        up2 = grid.swap(tie(up0, down2, down1), **X)
        down3 = grid.swap(tie(down2, mixed), **CORE)
    sums = jnp.zeros((4, D), F32)
    step = lambda ks, state, weights, first_call, last_call, deps: mlp(
        ids, ks, recv_counts, read_counts, normed2, branch, up_bias_rows, down_bias, state,
        weights, block_rows, slots, first_call, last_call, deps,
    )
    active01, hidden01, outer, inner, sums = step(
        (0, 1), (after, after, sums), ((up0, down0), (up1, down1)), True, False, deps
    )
    spec = column_spec(total)
    at = [act_spec(total, i) for i in range(2)]
    deps = ()
    if fast:
        up3 = grid.swap(tie(up2, inner), **CORE)
    give1 = give_products(
        ids, [(normed2, hidden01), (active01, branch)], [(spec, at[1]), (at[1], spec)], places
    )
    active23, hidden23, outer, inner, sums = step(
        (2, 3), (outer, inner, sums), ((up2, down2), (up3, down3)), False, True, (give1,)
    )
    layer_out = outer[:slots].astype(BF16)[None]
    give3 = give_products(
        ids, [(normed2, hidden23), (active23, branch)], [(spec, at[1]), (at[1], spec)], places
    )
    if fast:
        got1, got3 = grid.swap(give1, **CORE), grid.swap(give3, **CORE)
    else:
        got1, got3 = jnp.zeros_like(give1), jnp.zeros_like(give3)
    after_grad, attn_grad, mixed_grad, mlp_sums = out_back(
        ids, inner, after, branch, mlp_gain, first, (give3,)
    )
    keep_down, give_down = keep_products(
        ids, [(active01, branch), (active23, branch)], [(at[0], spec)] * 2, (got1, got3), 1,
        places, False, (attn_grad,)
    )
    keep_up, give_up = keep_products(
        ids, [(normed2, hidden01), (normed2, hidden23)], [(spec, at[0])] * 2, (got1, got3), 0,
        places, True, (keep_down,)
    )
    grads_a = attend_back(
        qkv, mixed, mixed_grad, lse, lse_read, *marks, block_rows, 0, (keep_up,)
    )
    first_a13 = first_give(ids, 0, normed, mixed, grads_a, attn_grad, places)
    deps = (first_a13,)
    if fast:
        got = grid.swap(give_down, **X)
        down_y = (keep_down[0] + got[0], keep_down[1] + got[1])
        got = grid.swap(give_up, **Y)
        up_x = (keep_up[0] + got[0], keep_up[1] + got[1])
        got_a = grid.swap(first_a13, **CORE)
        deps = deps + down_y + up_x
    else:
        got_a = jnp.zeros_like(first_a13)
    grads_b = attend_back(
        qkv, mixed, mixed_grad, lse, lse_read, *marks, block_rows, 1, deps
    )
    first_b13 = first_give(ids, 1, normed, mixed, grads_b, attn_grad, places)
    keep_a, give_a = first_keep(
        ids, 0, normed, mixed, grads_a, attn_grad, got_a, places, False, (first_b13,)
    )
    got_b = grid.swap(first_b13, **CORE) if fast else jnp.zeros_like(first_b13)
    deps = (keep_a,)
    if fast:
        got_up = grid.swap(tie(up_x[1], grads_a), **X)
        got_down = grid.swap(tie(down_y[1], grads_a), **Y)
        both = jnp.stack([up_x[0] + got_up, down_y[0] + got_down], axis=1)
        deps = deps + (both,)
    keep_b, give_b = first_keep(
        ids, 1, normed, mixed, grads_b, attn_grad, got_b, places, False, deps, give_a
    )
    embedded_grad, readout_grad, attn_sums = qkv_back(
        ids, (grads_a, grads_b), first, stream, attn_gain, after_grad, (keep_b,)
    )
    returned = lax.all_to_all(
        embedded_grad.reshape(raw_rows.shape), "mod", split_axis=0, concat_axis=0, tiled=True
    )
    small = (attn_sums, mlp_sums, down_bias_grad, sums, readout_grad)
    stem_parts = stem_back(ids, rows, embedded_grad, small, places)

    if fast:
        together = lambda *values: lax.optimization_barrier(values)
        got_z = grid.swap(both[2:], **Z1)
        got_x = grid.swap(give_b, **X)
        got = [grid.swap(give, **CORE) for give in stem_parts[2:]]
        parts = [
            stem_parts[x][4 * y : 4 * y + 4] + got[x][4 * y : 4 * y + 4]
            for x in range(2)
            for y in range(2)
        ]
        own = jnp.concatenate([keep_a[0], keep_b[0]], axis=2) + got_x[0]
        away = jnp.concatenate([keep_a[1], keep_b[1]], axis=2) + got_x[1]
        both = both[:2] + got_z
        *parts, own, away, both = together(*parts, own, away, both)
        got = [grid.swap(part, **bit) for part, bit in zip(parts[1:], (Y, X, XY))]
        parts = [parts[0][i] + got[0][i] + got[1][i] + got[2][i] for i in range(4)]
        *parts, away, own, returned, both = together(*parts, away, own, returned, both)
        got_both = grid.swap(both[1], **Z0)
        got_y = grid.swap(away, **Y)
        piece = reduce_z(grid, parts)
        last = own + got_y
        both = both[0] + got_both
        piece, last, both = together(piece, last, both)
        both_x = grid.swap(both, **X)
        got_z = grid.swap(last[2:], **Z1)
        piece = gather_z(grid, piece)
        last = last[:2] + got_z
        raw_grad = raw_back(
            image,
            returned.reshape(capacity, D),
            patch_convolution_weight,
            language_projection_weight,
        )
        piece, last, raw_grad, layer_out, both_x = together(
            piece, last, raw_grad, layer_out, both_x
        )
        both_core = grid.swap(jnp.stack([both, both_x]), **CORE)
        got_z = grid.swap(last[1], **Z0)
        piece = joined(piece, *[grid.swap(piece, **bit) for bit in (Y, X, XY)])
        last = last[0] + got_z
        piece, last, both_core = together(piece, last, both_core)
        up_sum, down_sum = mlp_out(ids, both, both_x, both_core, places)
        last_x = grid.swap(last, **X)
        theirs = grid.swap(piece, **CORE)
        theirs, last_x, up_sum = together(theirs, last_x, up_sum)
        last_core = grid.swap(jnp.stack([last, last_x]), **CORE)
        patch_sum, lang_sum, small = stem_out(ids, piece, theirs)
        qkv_sum, out_sum = first_out(ids, last, last_x, last_core)
    else:
        reduced = lambda v: lax.psum(
            lax.psum_scatter(v, "mod", scatter_dimension=0, tiled=True), "rep"
        ).astype(F32)
        every = []
        for keep, other, give in ((keep_a, first_a13, give_a), (keep_b, first_b13, give_b[..., PART:])):
            every.append(jnp.stack([keep[0, 0], other[0, 0], give[0, 0], other[1, 0]], axis=1))
        every = reduced(jnp.concatenate(every, axis=2).reshape(D, -1))
        qkv_sum, out_sum = every[:, : 3 * D], every[:, 3 * D :]
        every = jnp.stack([keep_up[0, 0], give1[0, 0], keep_up[1, 0], give3[0, 0]])
        every = every.reshape(4, D, mods, units).transpose(1, 2, 0, 3).reshape(D, -1)
        up_sum = reduced(every)
        every = jnp.stack([keep_down[0, 0], give1[1, 0], give_down[0, 0], give3[1, 0]])
        every = every.reshape(4, mods, units, D).transpose(1, 0, 2, 3).reshape(-1, D)
        down_sum = reduced(every)
        stem_keep, stem_give, small = stem_parts
        small = lax.psum(small, AXES)
        patch_sum = lax.psum(stem_keep[0].astype(F32), AXES)
        lang_sum = lax.psum(stem_give[0].astype(F32), AXES)
        raw_grad = raw_back(
            image,
            returned.reshape(capacity, D),
            patch_convolution_weight,
            language_projection_weight,
        )
    raw_grad = raw_grad.reshape(raw_rows.shape)
    up_bias_sum = small[7:11].reshape(4, -1, units).transpose(1, 0, 2).reshape(-1)
    return (
        layer_out,
        raw_grad,
        patch_sum,
        small[0],
        lang_sum,
        small[1],
        small[11 : 11 + RD],
        small[2],
        small[3],
        qkv_sum,
        out_sum,
        small[4],
        small[5],
        up_sum,
        up_bias_sum,
        down_sum,
        small[6],
    )


def solution(mesh):
    both, rows, rep = P("mod", "rep", None), P("mod", None), P()
    pair = P("mod", "rep")
    return jax.shard_map(
        per_device,
        mesh=mesh,
        in_specs=(both, pair, pair, pair)
        + (rep,) * 7
        + (rows, rows, rep, rep, rows, rep, rows, rep, both),
        out_specs=(both, both)
        + (rep,) * 7
        + (rows, rows, rep, rep, rows, rep, rows, rep),
        check_vma=False,
    )
```

```python
import functools

import jax
import jax.numpy as jnp
from jax import lax
from jax.experimental import pallas as pl
from jax.experimental.pallas import tpu as pltpu
from jax.sharding import PartitionSpec as P

D = 768
HEADS = 12
HD = 64
RPS = 4
RD = 8
PAD = 16
PART = D // 2
SMALL = 24
LANES = 128
CHUNK = 384
FB = 768
EPS = 1e-6
NEG = -1e30
F32 = jnp.float32
BF16 = jnp.bfloat16
AXES = ("mod", "rep")
SCALE = HD ** (-0.5)
VMEM = pl.BlockSpec(memory_space=pltpu.VMEM)
SMEM = pl.BlockSpec(memory_space=pltpu.SMEM)
ANY = pl.BlockSpec(memory_space=pl.ANY)


def nn(left, right):
    return lax.dot_general(left, right, (((1,), (0,)), ((), ())), preferred_element_type=F32)


def nt(left, right):
    return lax.dot_general(left, right, (((1,), (1,)), ((), ())), preferred_element_type=F32)


def tn(left, right):
    return lax.dot_general(left, right, (((0,), (0,)), ((), ())), preferred_element_type=F32)


def line(vector):
    return vector[...].reshape(1, -1)


def chunks(rows):
    count = rows // CHUNK
    return [
        (i * CHUNK, (rows - i * CHUNK) if i == count - 1 else CHUNK) for i in range(count)
    ]


def normalise(rows):
    mean = jnp.mean(rows, axis=-1, keepdims=True)
    centred = rows - mean
    var = jnp.mean(centred * centred, axis=-1, keepdims=True)
    rstd = lax.rsqrt(var + EPS)
    return centred * rstd, rstd


def norm_input_grad(xhat, rstd, gain, upstream):
    scaled = upstream * gain
    first = jnp.mean(scaled, axis=-1, keepdims=True)
    second = jnp.mean(scaled * xhat, axis=-1, keepdims=True)
    return rstd * (scaled - first - xhat * second)


def call(kernel, out_shape, deps=(), **kw):
    limit = kw.pop("vmem", 20)
    estimate = kw.pop("cost", None)
    in_specs = kw.pop("in_specs")
    count, more = len(in_specs), len(deps)

    def body(*refs):
        kernel(*refs[:count], *refs[count + more :])

    built = pl.pallas_call(
        body,
        out_shape=out_shape,
        in_specs=list(in_specs) + [ANY] * more,
        cost_estimate=estimate,
        compiler_params=pltpu.CompilerParams(vmem_limit_bytes=limit * 1024 * 1024),
        **kw,
    )
    return lambda *args: built(*args, *deps)


def cost(us):
    return pl.CostEstimate(flops=int(us * 1.15e9), bytes_accessed=1 << 20, transcendentals=0)


def struct(shape, dtype):
    return jax.ShapeDtypeStruct(shape, dtype)


def live_of(index, counts, read, block_rows):
    groups_n = counts.shape[1]
    capacity = groups_n * block_rows
    live = index < 0
    for s in range(groups_n):
        live = live | ((index >= s * block_rows) & (index < s * block_rows + counts[0, s]))
    slot = index - capacity
    return live | ((slot >= 0) & (slot < RD) & (slot % RPS < read[0, 0]))


def place_bits(place, places):
    if places == 1:
        return 0
    return (place >> 2) + 2 * (place & 3)


def place_of(bits):
    return ((bits & 1) << 2) | (bits >> 1)


def fetch(ids, arrays, want, target, sem):
    places, rows = arrays[0].shape[0], arrays[0].shape[1]
    for k in range(4):

        @pl.when((ids[0] ^ k) == want)
        def _():
            fetch_array(ids, arrays[k], target, sem)


def fetch_array(ids, array, target, sem, in_order=False):
    places, rows = array.shape[0], array.shape[1]
    for place in range(places):
        shard = place if in_order else ids[1] ^ place_bits(place, places)
        start = shard * rows if in_order else pl.multiple_of(shard * rows, 16)
        pltpu.make_async_copy(array.at[place], target.at[pl.ds(start, rows), :], sem).start()


def fetched(target, sem):
    pltpu.make_async_copy(target, target, sem).wait()


def stem_kernel(cut, raw, wp, bp, wl, bl, table, gain, bias, stream, normed):
    capacity = raw.shape[0]
    step = capacity // 4
    for start in range(0, capacity, step):
        weight, shift = (wp, bp) if start < cut else (wl, bl)
        rows = pl.ds(start, step)
        embedded = (nn(raw[rows, :], weight[...]) + line(shift)).astype(BF16).astype(F32)
        stream[rows, :] = embedded
        xhat, _ = normalise(embedded)
        normed[rows, :] = (xhat * line(gain) + line(bias)).astype(BF16)
    tail = jnp.concatenate([table[...], jnp.zeros((PAD - RD, D), F32)], axis=0)
    stream[pl.ds(capacity, PAD), :] = tail
    xhat, _ = normalise(tail)
    normed[pl.ds(capacity, PAD), :] = (xhat * line(gain) + line(bias)).astype(BF16)


def stems(raw, wp, bp, wl, bl, table, gain, bias):
    capacity = raw.shape[0]
    total = capacity + PAD
    return call(
        functools.partial(stem_kernel, 3 * capacity // 4),
        (struct((total, D), F32), struct((total, D), BF16)),
        in_specs=[VMEM] * 8,
        out_specs=(VMEM, VMEM),
        cost=cost(5),
    )(raw, wp, bp, wl, bl, table, gain, bias)


def qkv_kernel(ids, rows, w0, w1, w2, w3, out, buffer, sem):
    for r in range(3):
        fetch(ids, (w0, w1, w2, w3), r, buffer.at[r], sem.at[r])
    for r in range(3):
        fetched(buffer.at[r], sem.at[r])
        for start, size in chunks(rows.shape[0]):
            out[r, pl.ds(start, size), :] = nn(rows[pl.ds(start, size), :], buffer[r]).astype(BF16)


def project_qkv(ids, normed, weights, deps=()):
    total = normed.shape[0]
    return call(
        qkv_kernel,
        struct((3, total, D), BF16),
        deps,
        in_specs=[SMEM, VMEM, ANY, ANY, ANY, ANY],
        out_specs=VMEM,
        scratch_shapes=[pltpu.VMEM((3, D, D), BF16), pltpu.SemaphoreType.DMA((3,))],
        cost=cost(7),
    )(ids, normed, *weights)


def visible_readout(group_row, live_row):
    capacity = group_row.shape[1]
    query = lax.broadcasted_iota(jnp.int32, (RD, capacity), 0)
    group = 2 * (query // RPS + 1) + 1
    keys = group_row[...]
    seen = live_row & (keys <= group) & ((keys % 2 == 0) | (keys == group))
    return jnp.where(seen, 0.0, NEG)


def visible_between(read):
    query = lax.broadcasted_iota(jnp.int32, (RD, PAD), 0)
    key = lax.broadcasted_iota(jnp.int32, (RD, PAD), 1)
    live = (key < RD) & (key % RPS < read[0, 0])
    seen = (query == key) | (live & (query // RPS == key // RPS))
    return jnp.where(seen, 0.0, NEG)


def tiled(rows, heads):
    return jnp.concatenate([rows] * heads, axis=0)


def own_head(heads):
    row = lax.broadcasted_iota(jnp.int32, (heads * RD, heads * HD), 0) // RD
    lane = lax.broadcasted_iota(jnp.int32, (heads * RD, heads * HD), 1) // HD
    return row == lane


def fold_heads(stack, mine):
    kept = jnp.where(mine, stack, 0.0)
    total = kept[:RD]
    for start in range(RD, stack.shape[0], RD):
        total = total + kept[start : start + RD]
    return jnp.concatenate([total, jnp.zeros((PAD - RD, stack.shape[1]), F32)], axis=0)


def attend_kernel(
    block_rows, qkv, counts, read, group_row, group_col, mixed, lse, lse_read, mask, lse_cols, tail
):
    step = pl.program_id(0)
    capacity = group_row.shape[1]

    @pl.when(step == 0)
    def _():
        slot_row = lax.broadcasted_iota(jnp.int32, (1, capacity), 1)
        live_row = live_of(slot_row, counts, read, block_rows)
        keys = group_row[...]
        for start in range(0, capacity, CHUNK):
            query = lax.broadcasted_iota(jnp.int32, (CHUNK, capacity), 0) + start
            group = group_col[pl.ds(start, CHUNK), :]
            seen = live_row & (keys <= group) & ((keys % 2 == 0) | (keys == group))
            seen = seen | (query == slot_row)
            mask[pl.ds(start, CHUNK), :] = jnp.where(seen, 0.0, NEG)
        lse_cols[...] = jnp.zeros_like(lse_cols)
        mine = own_head(HEADS)
        tail_rows = pl.ds(capacity, PAD)
        head_rows = pl.ds(0, capacity)
        query = qkv[0, tail_rows, :].astype(F32)[:RD] * SCALE
        query = jnp.where(mine, tiled(query, HEADS), 0.0).astype(BF16)
        far = nt(query, qkv[1, head_rows, :]) + tiled(visible_readout(group_row, live_row), HEADS)
        near = nt(query, qkv[1, tail_rows, :]) + tiled(visible_between(read), HEADS)
        peak = jnp.maximum(
            jnp.max(far, axis=1, keepdims=True), jnp.max(near, axis=1, keepdims=True)
        )
        far = jnp.exp(far - peak)
        near = jnp.exp(near - peak)
        total = jnp.sum(far, axis=1, keepdims=True) + jnp.sum(near, axis=1, keepdims=True)
        out = nn(far.astype(BF16), qkv[2, head_rows, :]) + nn(
            near.astype(BF16), qkv[2, tail_rows, :]
        )
        tail[...] = fold_heads(out / total, mine)
        lse_read[...] = jnp.broadcast_to(peak + jnp.log(total), lse_read.shape)

    lane = lax.broadcasted_iota(jnp.int32, (1, LANES), 1)
    columns = pl.ds(pl.multiple_of(step * LANES, LANES), LANES)
    keys = qkv[1, pl.ds(0, capacity), columns]
    values = qkv[2, pl.ds(0, capacity), columns]
    for start in range(0, capacity, CHUNK):
        rows = pl.ds(start, CHUNK)
        query = qkv[0, rows, columns] * SCALE
        outs = []
        logs = lse_cols[rows, :]
        for head in range(2):
            chosen = jnp.where(lane // HD == head, query, jnp.zeros_like(query))
            scores = nt(chosen.astype(BF16), keys) + mask[rows, :]
            peak = jnp.max(scores, axis=1, keepdims=True)
            weight = jnp.exp(scores - peak)
            total = jnp.sum(weight, axis=1, keepdims=True)
            outs.append(nn(weight.astype(BF16), values) / total)
            logs = jnp.where(lane == 2 * step + head, peak + jnp.log(total), logs)
        mixed[rows, :] = jnp.where(lane < HD, outs[0], outs[1]).astype(BF16)
        lse_cols[rows, :] = logs
    mixed[pl.ds(capacity, PAD), :] = tail[:, columns].astype(BF16)

    @pl.when(step == pl.num_programs(0) - 1)
    def _():
        lse[...] = lse_cols[...].T[: lse.shape[0], :]


def attend(qkv, counts, read, group_row, group_col, block_rows, deps=()):
    total = qkv.shape[1]
    capacity = total - PAD
    pairs = HEADS // 2
    return call(
        functools.partial(attend_kernel, block_rows),
        (
            struct((total, D), BF16),
            struct((16, capacity), F32),
            struct((HEADS * RD, LANES), F32),
        ),
        deps,
        grid=(pairs,),
        in_specs=[VMEM, SMEM, SMEM, VMEM, VMEM],
        out_specs=(pl.BlockSpec((total, LANES), lambda j: (0, j)), VMEM, VMEM),
        scratch_shapes=[
            pltpu.VMEM((capacity, capacity), F32),
            pltpu.VMEM((capacity, LANES), F32),
            pltpu.VMEM((PAD, D), F32),
        ],
        cost=cost(21),
    )(qkv, counts, read, group_row, group_col)


def attend_back_kernel(
    block_rows,
    part,
    qkv,
    mixed,
    grad,
    lse,
    lse_read,
    counts,
    read,
    group_row,
    group_col,
    out,
    mask,
    delta,
    key_more,
    value_more,
    tails,
):
    step = pl.program_id(0)
    capacity = group_row.shape[1]
    tail_rows = pl.ds(capacity, PAD)
    head_rows = pl.ds(0, capacity)
    heads = PART // HD
    mine_columns = pl.ds(part * PART, PART)

    @pl.when(step == 0)
    def _():
        slot_row = lax.broadcasted_iota(jnp.int32, (1, capacity), 1)
        group = group_row[...]
        for start in range(0, capacity, CHUNK):
            slot = lax.broadcasted_iota(jnp.int32, (CHUNK, 1), 0) + start
            live = live_of(slot, counts, read, block_rows)
            keys = group_col[pl.ds(start, CHUNK), :]
            seen = live & (keys <= group) & ((keys % 2 == 0) | (keys == group))
            seen = seen | (slot == slot_row)
            mask[pl.ds(start, CHUNK), :] = jnp.where(seen, 0.0, NEG)
        head = lax.broadcasted_iota(jnp.int32, (8, PART), 0)
        column = lax.broadcasted_iota(jnp.int32, (8, PART), 1)
        select = jnp.where(column // HD == head, 1.0, 0.0).astype(BF16)
        for start in range(0, capacity, CHUNK):
            rows = pl.ds(start, CHUNK)
            product = grad[rows, mine_columns].astype(F32) * mixed[rows, mine_columns].astype(F32)
            high = product.astype(BF16)
            low = (product - high.astype(F32)).astype(BF16)
            delta[:, rows] = nt(select, high) + nt(select, low)

        live_row = live_of(slot_row, counts, read, block_rows)
        mine = own_head(heads)
        query = qkv[0, tail_rows, mine_columns].astype(F32)[:RD] * SCALE
        query = jnp.where(mine, tiled(query, heads), 0.0).astype(BF16)
        upper = grad[tail_rows, mine_columns].astype(F32)[:RD]
        upper = jnp.where(mine, tiled(upper, heads), 0.0)
        result = tiled(mixed[tail_rows, mine_columns].astype(F32)[:RD], heads)
        row_delta = jnp.sum(upper * result, axis=1, keepdims=True)
        upper = upper.astype(BF16)
        logs = lse_read[pl.ds(part * heads * RD, heads * RD), 0:1]
        far = nt(query, qkv[1, head_rows, mine_columns]) + tiled(visible_readout(group_row, live_row), heads)
        near = nt(query, qkv[1, tail_rows, mine_columns]) + tiled(visible_between(read), heads)
        far = jnp.exp(far - logs)
        near = jnp.exp(near - logs)
        far_grad = (far * (nt(upper, qkv[2, head_rows, mine_columns]) - row_delta)).astype(BF16)
        near_grad = (near * (nt(upper, qkv[2, tail_rows, mine_columns]) - row_delta)).astype(BF16)
        query_grad = nn(far_grad, qkv[1, head_rows, mine_columns]) + nn(near_grad, qkv[1, tail_rows, mine_columns])
        tails[0] = fold_heads(query_grad, mine) * SCALE
        tails[1] = tn(near_grad, query)
        tails[2] = tn(near.astype(BF16), upper)
        key_more[...] = tn(far_grad, query)
        value_more[...] = tn(far.astype(BF16), upper)

    lane = lax.broadcasted_iota(jnp.int32, (1, LANES), 1)
    columns = pl.ds(pl.multiple_of(step * LANES, LANES), LANES)
    here = pl.ds(pl.multiple_of(part * PART + step * LANES, LANES), LANES)
    query = (qkv[0, head_rows, here] * SCALE).astype(BF16)
    upper = grad[head_rows, here]
    query_grad = jnp.zeros((capacity, LANES), F32)
    for start in range(0, capacity, CHUNK):
        rows = pl.ds(start, CHUNK)
        all_keys = qkv[1, rows, here]
        all_values = qkv[2, rows, here]
        key_parts = []
        value_parts = []
        for head in range(2):
            own = lane // HD == head
            keys = jnp.where(own, all_keys, jnp.zeros_like(all_keys))
            values = jnp.where(own, all_values, jnp.zeros_like(all_values))
            logs = lse[pl.ds(part * heads + 2 * step + head, 1), :]
            row_delta = delta[pl.ds(2 * step + head, 1), :]
            probs = jnp.exp(nt(keys, query) + mask[rows, :] - logs)
            score_grad = (probs * (nt(values, upper) - row_delta)).astype(BF16)
            value_parts.append(nn(probs.astype(BF16), upper))
            key_parts.append(nn(score_grad, query))
            query_grad = query_grad + tn(score_grad, keys)
        key_grad = jnp.where(lane < HD, key_parts[0], key_parts[1]) + key_more[rows, columns]
        value_grad = jnp.where(lane < HD, value_parts[0], value_parts[1]) + value_more[rows, columns]
        out[1, rows, :] = key_grad.astype(BF16)
        out[2, rows, :] = value_grad.astype(BF16)
    out[0, head_rows, :] = (query_grad * SCALE).astype(BF16)
    for part in range(3):
        out[part, tail_rows, :] = tails[part, :, columns].astype(BF16)


def attend_back(
    qkv, mixed, grad, lse, lse_read, counts, read, group_row, group_col, block_rows, part,
    deps=()
):
    total = qkv.shape[1]
    capacity = total - PAD
    pairs = PART // LANES
    return call(
        functools.partial(attend_back_kernel, block_rows, part),
        struct((3, total, PART), BF16),
        deps,
        grid=(pairs,),
        in_specs=[VMEM, VMEM, VMEM, VMEM, VMEM, SMEM, SMEM, VMEM, VMEM],
        out_specs=pl.BlockSpec((3, total, LANES), lambda j: (0, 0, j)),
        scratch_shapes=[
            pltpu.VMEM((capacity, capacity), F32),
            pltpu.VMEM((8, capacity), F32),
            pltpu.VMEM((capacity, PART), F32),
            pltpu.VMEM((capacity, PART), F32),
            pltpu.VMEM((3, PAD, PART), F32),
        ],
        cost=cost(15),
    )(qkv, mixed, grad, lse, lse_read, counts, read, group_row, group_col)


def out_kernel(ids, mixed, w0, w1, w2, w3, stream, gain, bias, after, normed, buffer, sem):
    fetch(ids, (w0, w1, w2, w3), 3, buffer, sem)
    fetched(buffer, sem)
    for start, size in chunks(mixed.shape[0]):
        rows = pl.ds(start, size)
        value = stream[rows, :] + nn(mixed[rows, :], buffer[...])
        after[rows, :] = value
        xhat, _ = normalise(value)
        normed[rows, :] = (xhat * line(gain) + line(bias)).astype(BF16)


def out_project(ids, mixed, weights, stream, gain, bias, deps=()):
    total = mixed.shape[0]
    return call(
        out_kernel,
        (struct((total, D), F32), struct((total, D), BF16)),
        deps,
        in_specs=[SMEM, VMEM, ANY, ANY, ANY, ANY, VMEM, VMEM, VMEM],
        out_specs=(VMEM, VMEM),
        scratch_shapes=[pltpu.VMEM((D, D), BF16), pltpu.SemaphoreType.DMA],
        cost=cost(6.4),
    )(ids, mixed, *weights, stream, gain, bias)


def out_back_kernel(
    ids, inner, after, branch, gain, w0, w1, w2, w3, grad, grad_low, mixed_grad, sums, buffer, sem
):
    fetch(ids, (w0, w1, w2, w3), 3, buffer, sem)
    fetched(buffer, sem)
    gain_sum = jnp.zeros((1, D), F32)
    bias_sum = jnp.zeros((1, D), F32)
    for start, size in chunks(inner.shape[0]):
        rows = pl.ds(start, size)
        upstream = inner[rows, :]
        xhat, rstd = normalise(after[rows, :])
        gain_sum = gain_sum + jnp.sum(upstream * xhat, axis=0, keepdims=True)
        bias_sum = bias_sum + jnp.sum(upstream, axis=0, keepdims=True)
        total = branch[rows, :].astype(F32) + norm_input_grad(xhat, rstd, line(gain), upstream)
        grad[rows, :] = total
        low = total.astype(BF16)
        grad_low[rows, :] = low
        mixed_grad[rows, :] = nt(low, buffer[...]).astype(BF16)
    sums[0:1, :] = gain_sum
    sums[1:2, :] = bias_sum


def out_back(ids, inner, after, branch, gain, weights, deps=()):
    total = inner.shape[0]
    return call(
        out_back_kernel,
        (
            struct((total, D), F32),
            struct((total, D), BF16),
            struct((total, D), BF16),
            struct((2, D), F32),
        ),
        deps,
        in_specs=[SMEM, VMEM, VMEM, VMEM, VMEM, ANY, ANY, ANY, ANY],
        out_specs=(VMEM, VMEM, VMEM, VMEM),
        scratch_shapes=[pltpu.VMEM((D, D), BF16), pltpu.SemaphoreType.DMA],
        cost=cost(8.5),
    )(ids, inner, after, branch, gain, *weights)


def prepare_kernel(block_rows, cotangent, counts, read, branch, bias_grad):
    total, slots = branch.shape[0], cotangent.shape[0]
    index = lax.broadcasted_iota(jnp.int32, (total, 1), 0)
    live = jnp.where(live_of(index, counts, read, block_rows), 1.0, 0.0)
    upstream = cotangent[...].astype(F32) * live[:slots]
    bias_grad[...] = jnp.sum(upstream, axis=0, keepdims=True)
    upstream = jnp.concatenate([upstream, jnp.zeros((total - slots, D), F32)], axis=0)
    branch[...] = upstream.astype(BF16)


def prepare(cotangent, counts, read, block_rows, total):
    return call(
        functools.partial(prepare_kernel, block_rows),
        (struct((total, D), BF16), struct((1, D), F32)),
        in_specs=[VMEM, SMEM, SMEM],
        out_specs=(VMEM, VMEM),
        cost=cost(3),
    )(cotangent, counts, read)


def mlp_kernel(
    block_rows,
    ks,
    first,
    last,
    slots,
    *refs,
):
    nk = len(ks)
    ids, counts, read, normed, branch, up_bias, down_bias, total_in, inner_in, sums_in = refs[:10]
    weights = refs[10 : 10 + 2 * nk]
    active, hidden_grad, total, inner, sums = refs[10 + 2 * nk : 15 + 2 * nk]
    up, down, sem = refs[-3:]
    step = pl.program_id(0)
    index = step // (D // FB)
    part = step % (D // FB)
    length = normed.shape[0]

    @pl.when(step == 0)
    def _():
        for i in range(nk):
            fetch_array(ids, weights[2 * i], up.at[i], sem.at[i, 0])
            fetch_array(ids, weights[2 * i + 1], down.at[i], sem.at[i, 1], True)
        sums[...] = sums_in[...]
        if first:
            total[...] = total_in[...] + line(down_bias)
            inner[...] = jnp.zeros_like(inner)
        else:
            total[...] = total_in[...]
            inner[...] = inner_in[...]

    @pl.when(part == 0)
    def _():
        fetched(up.at[index], sem.at[index, 0])
        fetched(down.at[index], sem.at[index, 1])

    columns = pl.ds(pl.multiple_of(part * FB, FB), FB)
    rank = ids[0] ^ ks[0]
    for i in range(1, nk):
        rank = jnp.where(index == i, ids[0] ^ ks[i], rank)
    up_part = up[index, :, columns]
    down_part = down[index, columns, :]
    shift = up_bias[pl.ds(rank, 1), columns]
    bias_sum = jnp.zeros((1, FB), F32)
    for start, size in chunks(length):
        rows = pl.ds(start, size)
        hidden = nn(normed[rows, :], up_part) + shift
        factor = (2.0 / jnp.pi) ** 0.5
        square = hidden * hidden
        bent = jnp.tanh(hidden * (factor + (factor * 0.044715) * square))
        half = 0.5 * (1.0 + bent)
        act = (hidden * half).astype(BF16)
        slope = half + (0.5 * hidden) * (1.0 - bent * bent) * (
            factor + (3.0 * factor * 0.044715) * square
        )
        back = (nt(branch[rows, :], down_part) * slope).astype(BF16)
        bias_sum = bias_sum + jnp.sum(back.astype(F32), axis=0, keepdims=True)
        active[0, rows, :] = act
        hidden_grad[0, rows, :] = back
        total[rows, :] += nn(act, down_part)
        inner[rows, :] += nt(back, up_part)
    sums[pl.ds(rank, 1), columns] = bias_sum

    if last:

        @pl.when(step == pl.num_programs(0) - 1)
        def _():
            at = lax.broadcasted_iota(jnp.int32, (length, 1), 0)
            live = jnp.where(live_of(at, counts, read, block_rows), 1.0, 0.0)
            total[...] = total[...] * live


def mlp(ids, ks, counts, read, normed, branch, up_bias, down_bias, state, weights, block_rows, slots, first, last, deps=()):
    total = normed.shape[0]
    nk = len(ks)
    per = D // FB
    whole = pl.BlockSpec((total, D), lambda j: (0, 0))
    vectors = pl.BlockSpec((4, D), lambda j: (0, 0))
    block = pl.BlockSpec((1, total, FB), lambda j: (j // per, 0, j % per))
    flat = [w for pair in weights for w in pair]
    return call(
        functools.partial(mlp_kernel, block_rows, ks, first, last, slots),
        (
            struct((nk, total, D), BF16),
            struct((nk, total, D), BF16),
            struct((total, D), F32),
            struct((total, D), F32),
            struct((4, D), F32),
        ),
        deps,
        grid=(nk * per,),
        in_specs=[SMEM, SMEM, SMEM, whole, whole, vectors, VMEM, whole, whole, vectors]
        + [ANY] * (2 * nk),
        out_specs=(block, block, whole, whole, vectors),
        scratch_shapes=[
            pltpu.VMEM((nk, D, D), BF16),
            pltpu.VMEM((nk, D, D), BF16),
            pltpu.SemaphoreType.DMA((nk, 2)),
        ],
        cost=cost(20),
    )(ids, counts, read, normed, branch, up_bias, down_bias, *state, *flat)


def put_rows(ids, value, first_row, places, store):
    rows = D // places
    for i in range(value.shape[0] // rows):
        bits = ids[1] ^ (first_row // rows + i)
        store(place_of(bits) if places > 1 else 0, value[i * rows : (i + 1) * rows])


def product_rows(ids, left, right, places, store):
    block = D // 2 if places > 1 else D
    for start in range(0, D, block):
        value = tn(left[:, start : start + block], right[...])
        put_rows(ids, value, start, places, store)


def to_give_kernel(places, count, ids, *refs):
    lefts, rights, out = refs[:count], refs[count : 2 * count], refs[2 * count]
    for i in range(count):

        def store(place, rows, i=i):
            out[i, pl.ds(place, 1)] = rows.astype(BF16)[None]

        product_rows(ids, lefts[i], rights[i], places, store)


def to_keep_kernel(places, y_first, ids, left0, right0, left2, right2, got0, got2, keep, give):
    half = max(places // 2, 1)
    for x, (left, right) in enumerate(((left0, right0), (left2, right2))):

        def store(place, rows, x=x):
            got = (got0, got2)[x]
            summed = (rows + got[pl.ds(place, 1)][0].astype(F32)).astype(BF16)[None]
            y, z = place // half, place % half
            if y_first:

                @pl.when(y == 0)
                def _():
                    keep[x, pl.ds(z, 1)] = summed

                @pl.when(y == 1)
                def _():
                    give[x, pl.ds(z, 1)] = summed
            else:
                (give if x else keep)[y, pl.ds(z, 1)] = summed

        product_rows(ids, left, right, places, store)


def column_spec(total):
    return pl.BlockSpec((total, D), lambda i: (0, 0))


def act_spec(total, index):
    return pl.BlockSpec((None, total, D), lambda i: (index, 0, 0))


def give_products(ids, pairs, specs, places, deps=()):
    count = len(pairs)
    total = pairs[0][0].shape[-2]
    rows = D // places
    return call(
        functools.partial(to_give_kernel, places, count),
        struct((count, places, rows, D), BF16),
        deps,
        grid=(1,),
        in_specs=[SMEM] + [s[0] for s in specs] + [s[1] for s in specs],
        out_specs=pl.BlockSpec((count, places, rows, D), lambda i: (0, 0, 0, 0)),
        cost=cost(6.5),
    )(ids, *[p[0] for p in pairs], *[p[1] for p in pairs])


def keep_products(ids, pairs, specs, got, index, places, y_first, deps=()):
    total = pairs[0][0].shape[-2]
    rows = D // places
    half = struct((2, max(places // 2, 1), rows, D), BF16)
    half_spec = pl.BlockSpec((2, max(places // 2, 1), rows, D), lambda i: (0, 0, 0, 0))
    return call(
        functools.partial(to_keep_kernel, places, y_first),
        (half, half),
        deps,
        grid=(1,),
        in_specs=[
            SMEM,
            specs[0][0],
            specs[0][1],
            specs[1][0],
            specs[1][1],
            pl.BlockSpec((None, places, rows, D), lambda i: (index, 0, 0, 0)),
            pl.BlockSpec((None, places, rows, D), lambda i: (index, 0, 0, 0)),
        ],
        out_specs=(half_spec, half_spec),
        cost=cost(8),
    )(ids, pairs[0][0], pairs[0][1], pairs[1][0], pairs[1][1], *got)


def first_fetch(ids, k, part, normed, mixed, grads, attn_grad, left, right, sem):
    rank = ids[0] ^ k

    @pl.when(rank < 3)
    def _():
        pltpu.make_async_copy(normed, left, sem.at[0]).start()
        pltpu.make_async_copy(grads.at[rank], right, sem.at[1]).start()

    @pl.when(rank == 3)
    def _():
        pltpu.make_async_copy(mixed, left, sem.at[0]).start()
        pltpu.make_async_copy(attn_grad.at[:, pl.ds(part * PART, PART)], right, sem.at[1]).start()


def first_give_kernel(places, part, ids, normed, mixed, grads, attn_grad, out, left, right, sem):
    ks = (1, 3)
    sources = (normed, mixed, grads, attn_grad)
    for i, k in enumerate(ks):
        first_fetch(ids, k, part, *sources, left.at[i], right.at[i], sem.at[i])
    for i, k in enumerate(ks):
        fetched(left.at[i], sem.at[i, 0])
        fetched(right.at[i], sem.at[i, 1])

        def store(place, rows, i=i):
            out[i, pl.ds(place, 1)] = rows.astype(BF16)[None]

        product_rows(ids, left.at[i], right.at[i], places, store)


def first_scratch(total):
    return [
        pltpu.VMEM((2, total, D), BF16),
        pltpu.VMEM((2, total, PART), BF16),
        pltpu.SemaphoreType.DMA((2, 2)),
    ]


def first_give(ids, part, normed, mixed, grads, attn_grad, places, deps=()):
    total = normed.shape[0]
    return call(
        functools.partial(first_give_kernel, places, part),
        struct((2, places, D // places, PART), BF16),
        deps,
        in_specs=[SMEM, ANY, ANY, ANY, ANY],
        out_specs=VMEM,
        scratch_shapes=first_scratch(total),
        cost=cost(5),
    )(ids, normed, mixed, grads, attn_grad)


def first_keep_kernel(places, part, y_first, ids, normed, mixed, grads, attn_grad, got, *refs):
    keep, give, left, right, sem = refs[-5:]
    sources = (normed, mixed, grads, attn_grad)
    for i, k in enumerate((0, 2)):
        first_fetch(ids, k, part, *sources, left.at[i], right.at[i], sem.at[i])
    for i in range(2):
        fetched(left.at[i], sem.at[i, 0])
        fetched(right.at[i], sem.at[i, 1])
    if len(refs) > 5:
        before = refs[0]
        give[:, :, :, :PART] = before[...]
        give = give.at[:, :, :, pl.ds(PART, PART)]
    to_keep_kernel(
        places, y_first, ids, left.at[0], right.at[0], left.at[1], right.at[1], got.at[0], got.at[1],
        keep, give
    )


def first_keep(
    ids, part, normed, mixed, grads, attn_grad, got, places, y_first, deps=(), before=None
):
    total = normed.shape[0]
    half = struct((2, max(places // 2, 1), D // places, PART), BF16)
    return call(
        functools.partial(first_keep_kernel, places, part, y_first),
        (half, half if before is None else struct(half.shape[:3] + (D,), BF16)),
        deps,
        in_specs=[SMEM, ANY, ANY, ANY, ANY, VMEM] + [VMEM] * (before is not None),
        out_specs=(VMEM, VMEM),
        scratch_shapes=first_scratch(total),
        cost=cost(6),
    )(ids, normed, mixed, grads, attn_grad, got, *([] if before is None else [before]))


def qkv_back_kernel(capacity, ids, grads0, grads1, *refs):
    stream, gain, after_grad, embedded, readout, sums, buffer, sem = refs[4:]
    for r in range(3):
        fetch(ids, refs[:4], r, buffer.at[r], sem.at[r])
    for r in range(3):
        fetched(buffer.at[r], sem.at[r])
    gain_sum = jnp.zeros((1, D), F32)
    bias_sum = jnp.zeros((1, D), F32)
    for start, size in chunks(stream.shape[0]):
        rows = pl.ds(start, size)
        upstream = jnp.zeros((size, D), F32)
        for r in range(3):
            grad = jnp.concatenate([grads0[r, rows, :], grads1[r, rows, :]], axis=1)
            upstream = upstream + nt(grad, buffer[r])
        xhat, rstd = normalise(stream[rows, :])
        gain_sum = gain_sum + jnp.sum(upstream * xhat, axis=0, keepdims=True)
        bias_sum = bias_sum + jnp.sum(upstream, axis=0, keepdims=True)
        total = after_grad[rows, :] + norm_input_grad(xhat, rstd, line(gain), upstream)
        inside = min(size, capacity - start)
        embedded[pl.ds(start, inside), :] = total[:inside].astype(BF16)
        if start + size > capacity:
            readout[...] = total[capacity - start : capacity - start + RD]
    sums[0:1, :] = gain_sum
    sums[1:2, :] = bias_sum


def qkv_back(ids, grads, weights, stream, gain, after_grad, deps=()):
    total = stream.shape[0]
    capacity = total - PAD
    return call(
        functools.partial(qkv_back_kernel, capacity),
        (struct((capacity, D), BF16), struct((RD, D), F32), struct((2, D), F32)),
        deps,
        in_specs=[SMEM, VMEM, VMEM] + [ANY] * 4 + [VMEM, VMEM, VMEM],
        out_specs=(VMEM, VMEM, VMEM),
        scratch_shapes=[pltpu.VMEM((3, D, D), BF16), pltpu.SemaphoreType.DMA((3,))],
        cost=cost(10),
    )(ids, *grads, *weights, stream, gain, after_grad)


def stem_back_kernel(cut, places, ids, raw, embedded, *refs):
    keep, give = refs[-4:-2], refs[-2:]
    rows = D // places // 2
    small = [part[...] for part in refs[:-4]]
    sums = [
        jnp.sum(embedded[part, :].astype(F32), axis=0, keepdims=True)
        for part in (slice(0, cut), slice(cut, None))
    ]
    small = jnp.concatenate(sums + small, axis=0)
    small = jnp.concatenate([small, jnp.zeros((SMALL - small.shape[0], D), F32)], axis=0)
    for stem, part in enumerate((slice(0, cut), slice(cut, None))):
        value = tn(raw[part, :], embedded[part, :])
        mine = (ids[0] & 1) == stem
        for i in range(2 * places):
            place = place_of(ids[1] ^ (i // 2))
            x = (i % 2) ^ (ids[0] >> 1)
            more = jnp.zeros((8, D), F32)
            if stem == 0 and 8 * i < SMALL:
                more = small[8 * i : 8 * i + 8]
            piece = jnp.concatenate([value[i * rows : (i + 1) * rows], more], axis=0)
            piece = piece.astype(BF16)[None]

            for side in range(2):

                @pl.when(mine & (x == side))
                def _():
                    keep[side][pl.ds(place, 1)] = piece

                @pl.when(jnp.logical_not(mine) & (x == side))
                def _():
                    give[side][pl.ds(place, 1)] = piece


def stem_back_plain_kernel(cut, raw, embedded, *refs):
    keep, give, out = refs[-3:]
    sums = [
        jnp.sum(embedded[part, :].astype(F32), axis=0, keepdims=True)
        for part in (slice(0, cut), slice(cut, None))
    ]
    small = jnp.concatenate(sums + [part[...] for part in refs[:-3]], axis=0)
    out[...] = jnp.concatenate([small, jnp.zeros((SMALL - small.shape[0], D), F32)], axis=0)
    keep[0] = tn(raw[:cut, :], embedded[:cut, :]).astype(BF16)
    give[0] = tn(raw[cut:, :], embedded[cut:, :]).astype(BF16)


def stem_back(ids, raw, embedded, small, places, deps=()):
    capacity = raw.shape[0]
    cut = 3 * capacity // 4
    if places == 1:
        return call(
            functools.partial(stem_back_plain_kernel, cut),
            (struct((1, D, D), BF16), struct((1, D, D), BF16), struct((SMALL, D), F32)),
            deps,
            in_specs=[VMEM, VMEM] + [VMEM] * len(small),
            out_specs=(VMEM, VMEM, VMEM),
            cost=cost(6),
        )(raw, embedded, *small)
    shape = (places, D // (2 * places) + 8, D)
    return call(
        functools.partial(stem_back_kernel, cut, places),
        (struct(shape, BF16),) * 4,
        deps,
        in_specs=[SMEM, VMEM, VMEM] + [VMEM] * len(small),
        out_specs=(VMEM,) * 4,
        cost=cost(6),
    )(ids, raw, embedded, *small)


def stem_out_kernel(ids, own, other, patch, lang, small):
    rows = own.shape[1] - 8
    for i in range(own.shape[0]):
        shard = ids[1] ^ place_bits(((i >> 2) & 1) * 4 + (i & 3), 8)
        x = (i >> 3) ^ (ids[0] >> 1)
        slot = shard * 2 + x
        at = pl.ds(pl.multiple_of(slot * rows, 16), rows)
        mine, theirs = own[i].astype(F32), other[i].astype(F32)
        first = (ids[0] & 1) == 0
        pieces = jnp.where(first, mine, theirs), jnp.where(first, theirs, mine)
        patch[at, :] = pieces[0][:rows]
        lang[at, :] = pieces[1][:rows]

        @pl.when(slot * 8 < SMALL)
        def _():
            small[pl.ds(pl.multiple_of(slot * 8, 8), 8), :] = pieces[0][rows:]


def stem_out(ids, own, other):
    return call(
        stem_out_kernel,
        (struct((D, D), F32), struct((D, D), F32), struct((SMALL, D), F32)),
        in_specs=[SMEM, VMEM, VMEM],
        out_specs=(VMEM, VMEM, VMEM),
        cost=cost(4.4),
    )(ids, own, other)


def raw_kernel(image, grad, wp, wl, out):
    @pl.when(image[0] != 0)
    def _():
        out[...] = nt(grad[...], wp[...])

    @pl.when(image[0] == 0)
    def _():
        out[...] = nt(grad[...], wl[...])


def raw_back(image, grad, wp, wl, deps=()):
    return call(
        raw_kernel,
        struct(grad.shape, F32),
        deps,
        in_specs=[SMEM, VMEM, VMEM, VMEM],
        out_specs=VMEM,
        cost=cost(4.6),
    )(image, grad, wp, wl)


def first_out_kernel(ids, k0, k2, k13, qkv, out, ranks):
    ranks[0], ranks[2], ranks[1], ranks[3] = k0[...], k2[...], k13[0], k13[1]
    for r in range(3):
        qkv[:, r * D : (r + 1) * D] = ranks[pl.ds(ids[0] ^ r, 1)][0].astype(F32)
    out[...] = ranks[pl.ds(ids[0] ^ 3, 1)][0].astype(F32)


def first_out(ids, k0, k2, k13):
    rows = k0.shape[0]
    return call(
        first_out_kernel,
        (struct((rows, 3 * D), F32), struct((rows, D), F32)),
        in_specs=[SMEM, VMEM, VMEM, VMEM],
        out_specs=(VMEM, VMEM),
        scratch_shapes=[pltpu.VMEM((4, rows, D), BF16)],
        cost=cost(2.3),
    )(ids, k0, k2, k13)


def mlp_out_kernel(places, ids, k0, k2, k13, up, down, ranks):
    ranks[0], ranks[2], ranks[1], ranks[3] = k0[...], k2[...], k13[0], k13[1]
    rows, unit = k0.shape[1], D // places
    for r in range(4):
        both = ranks[pl.ds(ids[0] ^ r, 1)][0]
        value = both[0].astype(F32)
        for s in range(places):
            start = (4 * s + r) * unit
            up[:, start : start + unit] = value[:, s * unit : (s + 1) * unit]
        down[r * rows : (r + 1) * rows, :] = both[1].astype(F32)


def mlp_out(ids, k0, k2, k13, places):
    rows = k0.shape[1]
    return call(
        functools.partial(mlp_out_kernel, places),
        (struct((rows, 4 * D), F32), struct((4 * rows, D), F32)),
        in_specs=[SMEM, VMEM, VMEM, VMEM],
        out_specs=(VMEM, VMEM),
        scratch_shapes=[pltpu.VMEM((4, 2, rows, D), BF16)],
        cost=cost(3.1),
    )(ids, k0, k2, k13)


class Grid:
    def __init__(self, mods, reps):
        self.mods, self.reps = mods, reps
        self.mod, self.rep = lax.axis_index("mod"), lax.axis_index("rep")

    def swap(self, value, mod=0, rep=0):
        pairs = [
            (m * self.reps + r, (m ^ mod) * self.reps + (r ^ rep))
            for m in range(self.mods)
            for r in range(self.reps)
        ]
        return lax.ppermute(value, AXES, pairs)


CORE, X, Y, Z0, Z1 = {"rep": 1}, {"rep": 2}, {"mod": 1}, {"mod": 2}, {"mod": 4}
Z01, XY = {"mod": 6}, {"rep": 2, "mod": 1}


def tie(value, *deps):
    return lax.optimization_barrier((value,) + deps)[0]


def joined(*parts):
    return jnp.concatenate(parts, axis=0)


def gather_z(grid, piece):
    parts = [piece] + [grid.swap(piece, **bit) for bit in (Z0, Z1, Z01)]
    return jnp.stack(parts)


def double_z(grid, piece):
    value = jnp.stack([piece, grid.swap(piece, **Z0)])
    return joined(value, grid.swap(value, **Z1))


def halve_z(grid, value):
    value = value[:2] + grid.swap(value[2:], **Z1)
    return value[0] + grid.swap(value[1], **Z0)


def reduce_z(grid, parts):
    total = parts[0]
    for part, bit in zip(parts[1:], (Z0, Z1, Z01)):
        total = total + grid.swap(part, **bit)
    return total


def per_device(
    raw_rows,
    recv_counts,
    slot_groups,
    read_counts,
    patch_convolution_weight,
    patch_stem_bias_vector,
    language_projection_weight,
    language_bias_vector,
    readout_table,
    attn_gain,
    attn_bias,
    qkv_weight,
    out_weight,
    mlp_gain,
    mlp_bias,
    up_weight,
    up_bias,
    down_weight,
    down_bias,
    out_cotangent,
):
    mods, reps = lax.axis_size("mod"), lax.axis_size("rep")
    fast = mods == 8 and reps == 4
    places = mods if fast else 1
    grid = Grid(mods, reps)
    block_rows = raw_rows.shape[1]
    capacity = mods * block_rows
    total = capacity + PAD
    slots = out_cotangent.shape[1]
    units = up_bias.shape[0] // (4 * mods)
    image = (grid.mod < 3 * mods // 4).astype(jnp.int32).reshape(1)
    rank = grid.rep if fast else jnp.zeros((), jnp.int32)
    ids = jnp.stack([rank, grid.mod if fast else jnp.zeros((), jnp.int32)]).astype(jnp.int32)
    group_row = slot_groups
    group_col = slot_groups.reshape(capacity, 1)
    marks = (recv_counts, read_counts, group_row, group_col)

    by_rank = lambda w: w.reshape(w.shape[0], -1, 4, units).transpose(2, 0, 1, 3).reshape(4, -1, D)
    up_bias_rows = up_bias.reshape(-1, 4, units).transpose(1, 0, 2).reshape(4, D)

    if fast:
        piece = lax.dynamic_slice_in_dim(
            jnp.concatenate([qkv_weight, out_weight], axis=1), rank * D, D, 1
        )
        quarter = down_weight.shape[0] // 4
        piece_up = lax.dynamic_index_in_dim(
            up_weight.reshape(-1, mods, 4, units), rank, 2, keepdims=False
        ).reshape(-1, D)
        piece_down = lax.dynamic_slice_in_dim(down_weight, rank * quarter, quarter, 0)
        first_z = gather_z(grid, piece)
        first_y = grid.swap(first_z, **Y)
        first_x = grid.swap(first_z, **X)
        up_z = gather_z(grid, tie(piece_up, first_z))
        raw_rows = tie(raw_rows, first_y, up_z)
    received = lax.all_to_all(raw_rows, "mod", split_axis=0, concat_axis=0, tiled=True)
    rows = received.reshape(capacity, D)
    branch, down_bias_grad = prepare(out_cotangent[0], recv_counts, read_counts, block_rows, total)
    if fast:
        first0 = joined(first_z, first_y)
        first2 = joined(first_x, grid.swap(first_y, **X))
        first1 = grid.swap(first0, **CORE)
        first3 = grid.swap(first2, **CORE)
        first = (first0, first1, first2, first3)
        down0 = lax.all_gather(piece_down, "mod", axis=0)
        piece_down = lax.dynamic_slice_in_dim(down_weight, (rank ^ 2) * quarter, quarter, 0)
        down2 = lax.all_gather(piece_down, "mod", axis=0)
    else:
        whole = lambda w: lax.all_gather(w, "mod", axis=0, tiled=True)
        every = jnp.concatenate([whole(qkv_weight), whole(out_weight)], axis=1)
        first = tuple(every[None, :, r * D : (r + 1) * D] for r in range(4))
        every = by_rank(whole(up_weight))
        up0, up1, up2, up3 = (every[r : r + 1] for r in range(4))
        every = whole(down_weight).reshape(mods, 4, units, D).transpose(1, 0, 2, 3)
        every = every.reshape(4, D, D)
        down0, down1, down2, down3 = (every[r : r + 1] for r in range(4))

    stream, normed = stems(
        rows,
        patch_convolution_weight,
        patch_stem_bias_vector,
        language_projection_weight,
        language_bias_vector,
        readout_table,
        attn_gain,
        attn_bias,
    )
    if fast:
        up0 = joined(up_z, grid.swap(tie(up_z, first_y), **Y))
    qkv = project_qkv(ids, normed, first)
    deps = ()
    mixed, lse, lse_read = attend(qkv, *marks, block_rows, deps)
    deps = ()
    if fast:
        down1 = grid.swap(tie(down0, up_z), **CORE)
        up2 = grid.swap(tie(up0, first1, first3), **X)
        deps = (up0, down1)
    after, normed2 = out_project(ids, mixed, first, stream, mlp_gain, mlp_bias, deps)
    deps = ()
    if fast:
        up1 = grid.swap(up0, **CORE)
        down3 = grid.swap(tie(down2, mixed), **CORE)
    sums = jnp.zeros((4, D), F32)
    step = lambda ks, state, weights, first_call, last_call, deps: mlp(
        ids, ks, recv_counts, read_counts, normed2, branch, up_bias_rows, down_bias, state,
        weights, block_rows, slots, first_call, last_call, deps,
    )
    active01, hidden01, outer, inner, sums = step(
        (0, 1), (after, after, sums), ((up0, down0), (up1, down1)), True, False, deps
    )
    spec = column_spec(total)
    at = [act_spec(total, i) for i in range(2)]
    deps = ()
    if fast:
        up3 = grid.swap(tie(up2, inner), **CORE)
    give1 = give_products(
        ids, [(normed2, hidden01), (active01, branch)], [(spec, at[1]), (at[1], spec)], places
    )
    active23, hidden23, outer, inner, sums = step(
        (2, 3), (outer, inner, sums), ((up2, down2), (up3, down3)), False, True, (give1,)
    )
    layer_out = outer[:slots].astype(BF16)[None]
    give3 = give_products(
        ids, [(normed2, hidden23), (active23, branch)], [(spec, at[1]), (at[1], spec)], places
    )
    if fast:
        got1, got3 = grid.swap(give1, **CORE), grid.swap(give3, **CORE)
    else:
        got1, got3 = jnp.zeros_like(give1), jnp.zeros_like(give3)
    after_grad, attn_grad, mixed_grad, mlp_sums = out_back(
        ids, inner, after, branch, mlp_gain, first, (give3,)
    )
    keep_down, give_down = keep_products(
        ids, [(active01, branch), (active23, branch)], [(at[0], spec)] * 2, (got1, got3), 1,
        places, False, (attn_grad,)
    )
    keep_up, give_up = keep_products(
        ids, [(normed2, hidden01), (normed2, hidden23)], [(spec, at[0])] * 2, (got1, got3), 0,
        places, True, (keep_down,)
    )
    grads_a = attend_back(
        qkv, mixed, mixed_grad, lse, lse_read, *marks, block_rows, 0, (keep_up,)
    )
    first_a13 = first_give(ids, 0, normed, mixed, grads_a, attn_grad, places)
    deps = (first_a13,)
    if fast:
        got = grid.swap(give_down, **X)
        down_y = (keep_down[0] + got[0], keep_down[1] + got[1])
        got = grid.swap(give_up, **Y)
        up_x = (keep_up[0] + got[0], keep_up[1] + got[1])
        got_a = grid.swap(first_a13, **CORE)
    else:
        got_a = jnp.zeros_like(first_a13)
    grads_b = attend_back(
        qkv, mixed, mixed_grad, lse, lse_read, *marks, block_rows, 1, deps
    )
    first_b13 = first_give(ids, 1, normed, mixed, grads_b, attn_grad, places)
    keep_a, give_a = first_keep(
        ids, 0, normed, mixed, grads_a, attn_grad, got_a, places, False, (first_b13,)
    )
    got_b = grid.swap(first_b13, **CORE) if fast else jnp.zeros_like(first_b13)
    deps = (keep_a,)
    if fast:
        got_up = grid.swap(tie(up_x[1], grads_a), **X)
        got_down = grid.swap(tie(down_y[1], grads_a), **Y)
        both = jnp.stack([up_x[0] + got_up, down_y[0] + got_down], axis=1)
        deps = deps + (both,)
    keep_b, give_b = first_keep(
        ids, 1, normed, mixed, grads_b, attn_grad, got_b, places, False, deps, give_a
    )
    embedded_grad, readout_grad, attn_sums = qkv_back(
        ids, (grads_a, grads_b), first, stream, attn_gain, after_grad, (keep_b,)
    )
    returned = lax.all_to_all(
        embedded_grad.reshape(raw_rows.shape), "mod", split_axis=0, concat_axis=0, tiled=True
    )
    small = (attn_sums, mlp_sums, down_bias_grad, sums, readout_grad)
    stem_parts = stem_back(ids, rows, embedded_grad, small, places)

    if fast:
        together = lambda *values: lax.optimization_barrier(values)
        got_z = grid.swap(both[2:], **Z1)
        got_x = grid.swap(give_b, **X)
        got = [grid.swap(give, **CORE) for give in stem_parts[2:]]
        parts = [
            stem_parts[x][4 * y : 4 * y + 4] + got[x][4 * y : 4 * y + 4]
            for x in range(2)
            for y in range(2)
        ]
        own = jnp.concatenate([keep_a[0], keep_b[0]], axis=2) + got_x[0]
        away = jnp.concatenate([keep_a[1], keep_b[1]], axis=2) + got_x[1]
        both = both[:2] + got_z
        *parts, own, away, both = together(*parts, own, away, both)
        got = [grid.swap(part, **bit) for part, bit in zip(parts[1:], (Y, X, XY))]
        parts = [parts[0][i] + got[0][i] + got[1][i] + got[2][i] for i in range(4)]
        *parts, away, own, both = together(*parts, away, own, both)
        got_both = grid.swap(both[1], **Z0)
        got_y = grid.swap(away, **Y)
        piece = reduce_z(grid, parts)
        last = own + got_y
        both = both[0] + got_both
        piece, last, both = together(piece, last, both)
        both_x = grid.swap(both, **X)
        got_z = grid.swap(last[2:], **Z1)
        piece = gather_z(grid, piece)
        last = last[:2] + got_z
        raw_grad = raw_back(
            image,
            returned.reshape(capacity, D),
            patch_convolution_weight,
            language_projection_weight,
        )
        piece, last, layer_out, both_x = together(piece, last, layer_out, both_x)
        both_core = grid.swap(jnp.stack([both, both_x]), **CORE)
        got_z = grid.swap(last[1], **Z0)
        piece = joined(piece, *[grid.swap(piece, **bit) for bit in (Y, X, XY)])
        last = last[0] + got_z
        piece, last, both_core, raw_grad = together(piece, last, both_core, raw_grad)
        up_sum, down_sum = mlp_out(ids, both, both_x, both_core, places)
        last_x = grid.swap(last, **X)
        theirs = grid.swap(piece, **CORE)
        theirs, last_x, up_sum = together(theirs, last_x, up_sum)
        last_core = grid.swap(jnp.stack([last, last_x]), **CORE)
        patch_sum, lang_sum, small = stem_out(ids, piece, theirs)
        qkv_sum, out_sum = first_out(ids, last, last_x, last_core)
    else:
        reduced = lambda v: lax.psum(
            lax.psum_scatter(v, "mod", scatter_dimension=0, tiled=True), "rep"
        ).astype(F32)
        every = []
        for keep, other, give in ((keep_a, first_a13, give_a), (keep_b, first_b13, give_b[..., PART:])):
            every.append(jnp.stack([keep[0, 0], other[0, 0], give[0, 0], other[1, 0]], axis=1))
        every = reduced(jnp.concatenate(every, axis=2).reshape(D, -1))
        qkv_sum, out_sum = every[:, : 3 * D], every[:, 3 * D :]
        every = jnp.stack([keep_up[0, 0], give1[0, 0], keep_up[1, 0], give3[0, 0]])
        every = every.reshape(4, D, mods, units).transpose(1, 2, 0, 3).reshape(D, -1)
        up_sum = reduced(every)
        every = jnp.stack([keep_down[0, 0], give1[1, 0], give_down[0, 0], give3[1, 0]])
        every = every.reshape(4, mods, units, D).transpose(1, 0, 2, 3).reshape(-1, D)
        down_sum = reduced(every)
        stem_keep, stem_give, small = stem_parts
        small = lax.psum(small, AXES)
        patch_sum = lax.psum(stem_keep[0].astype(F32), AXES)
        lang_sum = lax.psum(stem_give[0].astype(F32), AXES)
        raw_grad = raw_back(
            image,
            returned.reshape(capacity, D),
            patch_convolution_weight,
            language_projection_weight,
        )
    raw_grad = raw_grad.reshape(raw_rows.shape)
    up_bias_sum = small[7:11].reshape(4, -1, units).transpose(1, 0, 2).reshape(-1)
    return (
        layer_out,
        raw_grad,
        patch_sum,
        small[0],
        lang_sum,
        small[1],
        small[11 : 11 + RD],
        small[2],
        small[3],
        qkv_sum,
        out_sum,
        small[4],
        small[5],
        up_sum,
        up_bias_sum,
        down_sum,
        small[6],
    )


def solution(mesh):
    both, rows, rep = P("mod", "rep", None), P("mod", None), P()
    pair = P("mod", "rep")
    return jax.shard_map(
        per_device,
        mesh=mesh,
        in_specs=(both, pair, pair, pair)
        + (rep,) * 7
        + (rows, rows, rep, rep, rows, rep, rows, rep, both),
        out_specs=(both, both)
        + (rep,) * 7
        + (rows, rows, rep, rep, rows, rep, rows, rep),
        check_vma=False,
    )
```

```python
import functools

import jax
import jax.numpy as jnp
from jax import lax
from jax.experimental import pallas as pl
from jax.experimental.pallas import tpu as pltpu
from jax.sharding import PartitionSpec as P

D = 768
HEADS = 12
HD = 64
RPS = 4
RD = 8
PAD = 16
PART = D // 2
SMALL = 24
LANES = 128
CHUNK = 384
FB = 768
EPS = 1e-6
NEG = -1e30
F32 = jnp.float32
BF16 = jnp.bfloat16
AXES = ("mod", "rep")
SCALE = HD ** (-0.5)
VMEM = pl.BlockSpec(memory_space=pltpu.VMEM)
SMEM = pl.BlockSpec(memory_space=pltpu.SMEM)
ANY = pl.BlockSpec(memory_space=pl.ANY)


def nn(left, right):
    return lax.dot_general(left, right, (((1,), (0,)), ((), ())), preferred_element_type=F32)


def nt(left, right):
    return lax.dot_general(left, right, (((1,), (1,)), ((), ())), preferred_element_type=F32)


def tn(left, right):
    return lax.dot_general(left, right, (((0,), (0,)), ((), ())), preferred_element_type=F32)


def line(vector):
    return vector[...].reshape(1, -1)


def chunks(rows):
    count = rows // CHUNK
    return [
        (i * CHUNK, (rows - i * CHUNK) if i == count - 1 else CHUNK) for i in range(count)
    ]


def normalise(rows):
    mean = jnp.mean(rows, axis=-1, keepdims=True)
    centred = rows - mean
    var = jnp.mean(centred * centred, axis=-1, keepdims=True)
    rstd = lax.rsqrt(var + EPS)
    return centred * rstd, rstd


def norm_input_grad(xhat, rstd, gain, upstream):
    scaled = upstream * gain
    first = jnp.mean(scaled, axis=-1, keepdims=True)
    second = jnp.mean(scaled * xhat, axis=-1, keepdims=True)
    return rstd * (scaled - first - xhat * second)


def call(kernel, out_shape, deps=(), **kw):
    limit = kw.pop("vmem", 16)
    estimate = kw.pop("cost", None)
    in_specs = kw.pop("in_specs")
    count, more = len(in_specs), len(deps)

    def body(*refs):
        kernel(*refs[:count], *refs[count + more :])

    built = pl.pallas_call(
        body,
        out_shape=out_shape,
        in_specs=list(in_specs) + [ANY] * more,
        cost_estimate=estimate,
        compiler_params=pltpu.CompilerParams(vmem_limit_bytes=limit * 1024 * 1024),
        **kw,
    )
    return lambda *args: built(*args, *deps)


def cost(us):
    return pl.CostEstimate(flops=int(us * 1.15e9), bytes_accessed=1 << 20, transcendentals=0)


def struct(shape, dtype):
    return jax.ShapeDtypeStruct(shape, dtype)


def live_of(index, counts, read, block_rows):
    groups_n = counts.shape[1]
    capacity = groups_n * block_rows
    live = index < 0
    for s in range(groups_n):
        live = live | ((index >= s * block_rows) & (index < s * block_rows + counts[0, s]))
    slot = index - capacity
    return live | ((slot >= 0) & (slot < RD) & (slot % RPS < read[0, 0]))


def place_bits(place, places):
    if places == 1:
        return 0
    return (place >> 2) + 2 * (place & 3)


def place_of(bits):
    return ((bits & 1) << 2) | (bits >> 1)


def fetch(ids, arrays, want, target, sem):
    places, rows = arrays[0].shape[0], arrays[0].shape[1]
    for k in range(4):

        @pl.when((ids[0] ^ k) == want)
        def _():
            fetch_array(ids, arrays[k], target, sem)


def fetch_array(ids, array, target, sem, in_order=False):
    places, rows = array.shape[0], array.shape[1]
    for place in range(places):
        shard = place if in_order else ids[1] ^ place_bits(place, places)
        start = shard * rows if in_order else pl.multiple_of(shard * rows, 16)
        pltpu.make_async_copy(array.at[place], target.at[pl.ds(start, rows), :], sem).start()


def fetched(target, sem):
    pltpu.make_async_copy(target, target, sem).wait()


def stem_kernel(cut, raw, wp, bp, wl, bl, table, gain, bias, stream, normed):
    capacity = raw.shape[0]
    step = capacity // 4
    for start in range(0, capacity, step):
        weight, shift = (wp, bp) if start < cut else (wl, bl)
        rows = pl.ds(start, step)
        embedded = (nn(raw[rows, :], weight[...]) + line(shift)).astype(BF16).astype(F32)
        stream[rows, :] = embedded
        xhat, _ = normalise(embedded)
        normed[rows, :] = (xhat * line(gain) + line(bias)).astype(BF16)
    tail = jnp.concatenate([table[...], jnp.zeros((PAD - RD, D), F32)], axis=0)
    stream[pl.ds(capacity, PAD), :] = tail
    xhat, _ = normalise(tail)
    normed[pl.ds(capacity, PAD), :] = (xhat * line(gain) + line(bias)).astype(BF16)


def stems(raw, wp, bp, wl, bl, table, gain, bias):
    capacity = raw.shape[0]
    total = capacity + PAD
    return call(
        functools.partial(stem_kernel, 3 * capacity // 4),
        (struct((total, D), F32), struct((total, D), BF16)),
        in_specs=[VMEM] * 8,
        out_specs=(VMEM, VMEM),
        cost=cost(5),
    )(raw, wp, bp, wl, bl, table, gain, bias)


def qkv_kernel(ids, rows, w0, w1, w2, w3, out, buffer, sem):
    for r in range(3):
        fetch(ids, (w0, w1, w2, w3), r, buffer.at[r], sem.at[r])
    for r in range(3):
        fetched(buffer.at[r], sem.at[r])
        for start, size in chunks(rows.shape[0]):
            out[r, pl.ds(start, size), :] = nn(rows[pl.ds(start, size), :], buffer[r]).astype(BF16)


def project_qkv(ids, normed, weights, deps=()):
    total = normed.shape[0]
    return call(
        qkv_kernel,
        struct((3, total, D), BF16),
        deps,
        in_specs=[SMEM, VMEM, ANY, ANY, ANY, ANY],
        out_specs=VMEM,
        scratch_shapes=[pltpu.VMEM((3, D, D), BF16), pltpu.SemaphoreType.DMA((3,))],
        cost=cost(7),
    )(ids, normed, *weights)


def visible_readout(group_row, live_row):
    capacity = group_row.shape[1]
    query = lax.broadcasted_iota(jnp.int32, (RD, capacity), 0)
    group = 2 * (query // RPS + 1) + 1
    keys = group_row[...]
    seen = live_row & (keys <= group) & ((keys % 2 == 0) | (keys == group))
    return jnp.where(seen, 0.0, NEG)


def visible_between(read):
    query = lax.broadcasted_iota(jnp.int32, (RD, PAD), 0)
    key = lax.broadcasted_iota(jnp.int32, (RD, PAD), 1)
    live = (key < RD) & (key % RPS < read[0, 0])
    seen = (query == key) | (live & (query // RPS == key // RPS))
    return jnp.where(seen, 0.0, NEG)


def tiled(rows, heads):
    return jnp.concatenate([rows] * heads, axis=0)


def own_head(heads):
    row = lax.broadcasted_iota(jnp.int32, (heads * RD, heads * HD), 0) // RD
    lane = lax.broadcasted_iota(jnp.int32, (heads * RD, heads * HD), 1) // HD
    return row == lane


def fold_heads(stack, mine):
    kept = jnp.where(mine, stack, 0.0)
    total = kept[:RD]
    for start in range(RD, stack.shape[0], RD):
        total = total + kept[start : start + RD]
    return jnp.concatenate([total, jnp.zeros((PAD - RD, stack.shape[1]), F32)], axis=0)


def attend_kernel(
    block_rows, qkv, counts, read, group_row, group_col, mixed, lse, lse_read, mask, lse_cols, tail
):
    step = pl.program_id(0)
    capacity = group_row.shape[1]

    @pl.when(step == 0)
    def _():
        slot_row = lax.broadcasted_iota(jnp.int32, (1, capacity), 1)
        live_row = live_of(slot_row, counts, read, block_rows)
        keys = group_row[...]
        for start in range(0, capacity, CHUNK):
            query = lax.broadcasted_iota(jnp.int32, (CHUNK, capacity), 0) + start
            group = group_col[pl.ds(start, CHUNK), :]
            seen = live_row & (keys <= group) & ((keys % 2 == 0) | (keys == group))
            seen = seen | (query == slot_row)
            mask[pl.ds(start, CHUNK), :] = jnp.where(seen, 0.0, NEG)
        lse_cols[...] = jnp.zeros_like(lse_cols)
        mine = own_head(HEADS)
        tail_rows = pl.ds(capacity, PAD)
        head_rows = pl.ds(0, capacity)
        query = qkv[0, tail_rows, :].astype(F32)[:RD] * SCALE
        query = jnp.where(mine, tiled(query, HEADS), 0.0).astype(BF16)
        far = nt(query, qkv[1, head_rows, :]) + tiled(visible_readout(group_row, live_row), HEADS)
        near = nt(query, qkv[1, tail_rows, :]) + tiled(visible_between(read), HEADS)
        peak = jnp.maximum(
            jnp.max(far, axis=1, keepdims=True), jnp.max(near, axis=1, keepdims=True)
        )
        far = jnp.exp(far - peak)
        near = jnp.exp(near - peak)
        total = jnp.sum(far, axis=1, keepdims=True) + jnp.sum(near, axis=1, keepdims=True)
        out = nn(far.astype(BF16), qkv[2, head_rows, :]) + nn(
            near.astype(BF16), qkv[2, tail_rows, :]
        )
        tail[...] = fold_heads(out / total, mine)
        lse_read[...] = jnp.broadcast_to(peak + jnp.log(total), lse_read.shape)

    lane = lax.broadcasted_iota(jnp.int32, (1, LANES), 1)
    columns = pl.ds(pl.multiple_of(step * LANES, LANES), LANES)
    keys = qkv[1, pl.ds(0, capacity), columns]
    values = qkv[2, pl.ds(0, capacity), columns]
    for start in range(0, capacity, CHUNK):
        rows = pl.ds(start, CHUNK)
        query = qkv[0, rows, columns] * SCALE
        outs = []
        logs = lse_cols[rows, :]
        for head in range(2):
            chosen = jnp.where(lane // HD == head, query, jnp.zeros_like(query))
            scores = nt(chosen.astype(BF16), keys) + mask[rows, :]
            peak = jnp.max(scores, axis=1, keepdims=True)
            weight = jnp.exp(scores - peak)
            total = jnp.sum(weight, axis=1, keepdims=True)
            outs.append(nn(weight.astype(BF16), values) / total)
            logs = jnp.where(lane == 2 * step + head, peak + jnp.log(total), logs)
        mixed[rows, :] = jnp.where(lane < HD, outs[0], outs[1]).astype(BF16)
        lse_cols[rows, :] = logs
    mixed[pl.ds(capacity, PAD), :] = tail[:, columns].astype(BF16)

    @pl.when(step == pl.num_programs(0) - 1)
    def _():
        lse[...] = lse_cols[...].T[: lse.shape[0], :]


def attend(qkv, counts, read, group_row, group_col, block_rows, deps=()):
    total = qkv.shape[1]
    capacity = total - PAD
    pairs = HEADS // 2
    return call(
        functools.partial(attend_kernel, block_rows),
        (
            struct((total, D), BF16),
            struct((16, capacity), F32),
            struct((HEADS * RD, LANES), F32),
        ),
        deps,
        grid=(pairs,),
        in_specs=[VMEM, SMEM, SMEM, VMEM, VMEM],
        out_specs=(pl.BlockSpec((total, LANES), lambda j: (0, j)), VMEM, VMEM),
        scratch_shapes=[
            pltpu.VMEM((capacity, capacity), F32),
            pltpu.VMEM((capacity, LANES), F32),
            pltpu.VMEM((PAD, D), F32),
        ],
        cost=cost(21),
    )(qkv, counts, read, group_row, group_col)


def attend_back_kernel(
    block_rows,
    part,
    qkv,
    mixed,
    grad,
    lse,
    lse_read,
    counts,
    read,
    group_row,
    group_col,
    out,
    mask,
    delta,
    key_more,
    value_more,
    tails,
):
    step = pl.program_id(0)
    capacity = group_row.shape[1]
    tail_rows = pl.ds(capacity, PAD)
    head_rows = pl.ds(0, capacity)
    heads = PART // HD
    mine_columns = pl.ds(part * PART, PART)

    @pl.when(step == 0)
    def _():
        slot_row = lax.broadcasted_iota(jnp.int32, (1, capacity), 1)
        group = group_row[...]
        for start in range(0, capacity, CHUNK):
            slot = lax.broadcasted_iota(jnp.int32, (CHUNK, 1), 0) + start
            live = live_of(slot, counts, read, block_rows)
            keys = group_col[pl.ds(start, CHUNK), :]
            seen = live & (keys <= group) & ((keys % 2 == 0) | (keys == group))
            seen = seen | (slot == slot_row)
            mask[pl.ds(start, CHUNK), :] = jnp.where(seen, 0.0, NEG)
        head = lax.broadcasted_iota(jnp.int32, (8, PART), 0)
        column = lax.broadcasted_iota(jnp.int32, (8, PART), 1)
        select = jnp.where(column // HD == head, 1.0, 0.0).astype(BF16)
        for start in range(0, capacity, CHUNK):
            rows = pl.ds(start, CHUNK)
            product = grad[rows, mine_columns].astype(F32) * mixed[rows, mine_columns].astype(F32)
            high = product.astype(BF16)
            low = (product - high.astype(F32)).astype(BF16)
            delta[:, rows] = nt(select, high) + nt(select, low)

        live_row = live_of(slot_row, counts, read, block_rows)
        mine = own_head(heads)
        query = qkv[0, tail_rows, mine_columns].astype(F32)[:RD] * SCALE
        query = jnp.where(mine, tiled(query, heads), 0.0).astype(BF16)
        upper = grad[tail_rows, mine_columns].astype(F32)[:RD]
        upper = jnp.where(mine, tiled(upper, heads), 0.0)
        result = tiled(mixed[tail_rows, mine_columns].astype(F32)[:RD], heads)
        row_delta = jnp.sum(upper * result, axis=1, keepdims=True)
        upper = upper.astype(BF16)
        logs = lse_read[pl.ds(part * heads * RD, heads * RD), 0:1]
        far = nt(query, qkv[1, head_rows, mine_columns]) + tiled(visible_readout(group_row, live_row), heads)
        near = nt(query, qkv[1, tail_rows, mine_columns]) + tiled(visible_between(read), heads)
        far = jnp.exp(far - logs)
        near = jnp.exp(near - logs)
        far_grad = (far * (nt(upper, qkv[2, head_rows, mine_columns]) - row_delta)).astype(BF16)
        near_grad = (near * (nt(upper, qkv[2, tail_rows, mine_columns]) - row_delta)).astype(BF16)
        query_grad = nn(far_grad, qkv[1, head_rows, mine_columns]) + nn(near_grad, qkv[1, tail_rows, mine_columns])
        tails[0] = fold_heads(query_grad, mine) * SCALE
        tails[1] = tn(near_grad, query)
        tails[2] = tn(near.astype(BF16), upper)
        key_more[...] = tn(far_grad, query)
        value_more[...] = tn(far.astype(BF16), upper)

    lane = lax.broadcasted_iota(jnp.int32, (1, LANES), 1)
    columns = pl.ds(pl.multiple_of(step * LANES, LANES), LANES)
    here = pl.ds(pl.multiple_of(part * PART + step * LANES, LANES), LANES)
    query = (qkv[0, head_rows, here] * SCALE).astype(BF16)
    upper = grad[head_rows, here]
    query_grad = jnp.zeros((capacity, LANES), F32)
    for start in range(0, capacity, CHUNK):
        rows = pl.ds(start, CHUNK)
        all_keys = qkv[1, rows, here]
        all_values = qkv[2, rows, here]
        key_parts = []
        value_parts = []
        for head in range(2):
            own = lane // HD == head
            keys = jnp.where(own, all_keys, jnp.zeros_like(all_keys))
            values = jnp.where(own, all_values, jnp.zeros_like(all_values))
            logs = lse[pl.ds(part * heads + 2 * step + head, 1), :]
            row_delta = delta[pl.ds(2 * step + head, 1), :]
            probs = jnp.exp(nt(keys, query) + mask[rows, :] - logs)
            score_grad = (probs * (nt(values, upper) - row_delta)).astype(BF16)
            value_parts.append(nn(probs.astype(BF16), upper))
            key_parts.append(nn(score_grad, query))
            query_grad = query_grad + tn(score_grad, keys)
        key_grad = jnp.where(lane < HD, key_parts[0], key_parts[1]) + key_more[rows, columns]
        value_grad = jnp.where(lane < HD, value_parts[0], value_parts[1]) + value_more[rows, columns]
        out[1, rows, :] = key_grad.astype(BF16)
        out[2, rows, :] = value_grad.astype(BF16)
    out[0, head_rows, :] = (query_grad * SCALE).astype(BF16)
    for part in range(3):
        out[part, tail_rows, :] = tails[part, :, columns].astype(BF16)


def attend_back(
    qkv, mixed, grad, lse, lse_read, counts, read, group_row, group_col, block_rows, part,
    deps=()
):
    total = qkv.shape[1]
    capacity = total - PAD
    pairs = PART // LANES
    return call(
        functools.partial(attend_back_kernel, block_rows, part),
        struct((3, total, PART), BF16),
        deps,
        grid=(pairs,),
        in_specs=[VMEM, VMEM, VMEM, VMEM, VMEM, SMEM, SMEM, VMEM, VMEM],
        out_specs=pl.BlockSpec((3, total, LANES), lambda j: (0, 0, j)),
        scratch_shapes=[
            pltpu.VMEM((capacity, capacity), F32),
            pltpu.VMEM((8, capacity), F32),
            pltpu.VMEM((capacity, PART), F32),
            pltpu.VMEM((capacity, PART), F32),
            pltpu.VMEM((3, PAD, PART), F32),
        ],
        cost=cost(15),
    )(qkv, mixed, grad, lse, lse_read, counts, read, group_row, group_col)


def out_kernel(ids, mixed, w0, w1, w2, w3, stream, gain, bias, after, normed, buffer, sem):
    fetch(ids, (w0, w1, w2, w3), 3, buffer, sem)
    fetched(buffer, sem)
    for start, size in chunks(mixed.shape[0]):
        rows = pl.ds(start, size)
        value = stream[rows, :] + nn(mixed[rows, :], buffer[...])
        after[rows, :] = value
        xhat, _ = normalise(value)
        normed[rows, :] = (xhat * line(gain) + line(bias)).astype(BF16)


def out_project(ids, mixed, weights, stream, gain, bias, deps=()):
    total = mixed.shape[0]
    return call(
        out_kernel,
        (struct((total, D), F32), struct((total, D), BF16)),
        deps,
        in_specs=[SMEM, VMEM, ANY, ANY, ANY, ANY, VMEM, VMEM, VMEM],
        out_specs=(VMEM, VMEM),
        scratch_shapes=[pltpu.VMEM((D, D), BF16), pltpu.SemaphoreType.DMA],
        cost=cost(6.4),
    )(ids, mixed, *weights, stream, gain, bias)


def out_back_kernel(
    ids, inner, after, branch, gain, w0, w1, w2, w3, grad, grad_low, mixed_grad, sums, buffer, sem
):
    fetch(ids, (w0, w1, w2, w3), 3, buffer, sem)
    fetched(buffer, sem)
    gain_sum = jnp.zeros((1, D), F32)
    bias_sum = jnp.zeros((1, D), F32)
    for start, size in chunks(inner.shape[0]):
        rows = pl.ds(start, size)
        upstream = inner[rows, :]
        xhat, rstd = normalise(after[rows, :])
        gain_sum = gain_sum + jnp.sum(upstream * xhat, axis=0, keepdims=True)
        bias_sum = bias_sum + jnp.sum(upstream, axis=0, keepdims=True)
        total = branch[rows, :].astype(F32) + norm_input_grad(xhat, rstd, line(gain), upstream)
        grad[rows, :] = total
        low = total.astype(BF16)
        grad_low[rows, :] = low
        mixed_grad[rows, :] = nt(low, buffer[...]).astype(BF16)
    sums[0:1, :] = gain_sum
    sums[1:2, :] = bias_sum


def out_back(ids, inner, after, branch, gain, weights, deps=()):
    total = inner.shape[0]
    return call(
        out_back_kernel,
        (
            struct((total, D), F32),
            struct((total, D), BF16),
            struct((total, D), BF16),
            struct((2, D), F32),
        ),
        deps,
        in_specs=[SMEM, VMEM, VMEM, VMEM, VMEM, ANY, ANY, ANY, ANY],
        out_specs=(VMEM, VMEM, VMEM, VMEM),
        scratch_shapes=[pltpu.VMEM((D, D), BF16), pltpu.SemaphoreType.DMA],
        cost=cost(8.5),
    )(ids, inner, after, branch, gain, *weights)


def prepare_kernel(block_rows, cotangent, counts, read, branch, bias_grad):
    total, slots = branch.shape[0], cotangent.shape[0]
    index = lax.broadcasted_iota(jnp.int32, (total, 1), 0)
    live = jnp.where(live_of(index, counts, read, block_rows), 1.0, 0.0)
    upstream = cotangent[...].astype(F32) * live[:slots]
    bias_grad[...] = jnp.sum(upstream, axis=0, keepdims=True)
    upstream = jnp.concatenate([upstream, jnp.zeros((total - slots, D), F32)], axis=0)
    branch[...] = upstream.astype(BF16)


def prepare(cotangent, counts, read, block_rows, total):
    return call(
        functools.partial(prepare_kernel, block_rows),
        (struct((total, D), BF16), struct((1, D), F32)),
        in_specs=[VMEM, SMEM, SMEM],
        out_specs=(VMEM, VMEM),
        cost=cost(3),
    )(cotangent, counts, read)


def mlp_kernel(
    block_rows,
    ks,
    first,
    last,
    slots,
    *refs,
):
    nk = len(ks)
    ids, counts, read, normed, branch, up_bias, down_bias, total_in, inner_in, sums_in = refs[:10]
    weights = refs[10 : 10 + 2 * nk]
    active, hidden_grad, total, inner, sums = refs[10 + 2 * nk : 15 + 2 * nk]
    up, down, sem = refs[-3:]
    step = pl.program_id(0)
    index = step // (D // FB)
    part = step % (D // FB)
    length = normed.shape[0]

    @pl.when(step == 0)
    def _():
        for i in range(nk):
            fetch_array(ids, weights[2 * i], up.at[i], sem.at[i, 0])
            fetch_array(ids, weights[2 * i + 1], down.at[i], sem.at[i, 1], True)
        sums[...] = sums_in[...]
        if first:
            total[...] = total_in[...] + line(down_bias)
            inner[...] = jnp.zeros_like(inner)
        else:
            total[...] = total_in[...]
            inner[...] = inner_in[...]

    @pl.when(part == 0)
    def _():
        fetched(up.at[index], sem.at[index, 0])
        fetched(down.at[index], sem.at[index, 1])

    columns = pl.ds(pl.multiple_of(part * FB, FB), FB)
    rank = ids[0] ^ ks[0]
    for i in range(1, nk):
        rank = jnp.where(index == i, ids[0] ^ ks[i], rank)
    up_part = up[index, :, columns]
    down_part = down[index, columns, :]
    shift = up_bias[pl.ds(rank, 1), columns]
    bias_sum = jnp.zeros((1, FB), F32)
    for start, size in chunks(length):
        rows = pl.ds(start, size)
        hidden = nn(normed[rows, :], up_part) + shift
        factor = (2.0 / jnp.pi) ** 0.5
        square = hidden * hidden
        bent = jnp.tanh(hidden * (factor + (factor * 0.044715) * square))
        half = 0.5 * (1.0 + bent)
        act = (hidden * half).astype(BF16)
        slope = half + (0.5 * hidden) * (1.0 - bent * bent) * (
            factor + (3.0 * factor * 0.044715) * square
        )
        back = (nt(branch[rows, :], down_part) * slope).astype(BF16)
        bias_sum = bias_sum + jnp.sum(back.astype(F32), axis=0, keepdims=True)
        active[0, rows, :] = act
        hidden_grad[0, rows, :] = back
        total[rows, :] += nn(act, down_part)
        inner[rows, :] += nt(back, up_part)
    sums[pl.ds(rank, 1), columns] = bias_sum

    if last:

        @pl.when(step == pl.num_programs(0) - 1)
        def _():
            at = lax.broadcasted_iota(jnp.int32, (length, 1), 0)
            live = jnp.where(live_of(at, counts, read, block_rows), 1.0, 0.0)
            total[...] = total[...] * live


def mlp(ids, ks, counts, read, normed, branch, up_bias, down_bias, state, weights, block_rows, slots, first, last, deps=()):
    total = normed.shape[0]
    nk = len(ks)
    per = D // FB
    whole = pl.BlockSpec((total, D), lambda j: (0, 0))
    vectors = pl.BlockSpec((4, D), lambda j: (0, 0))
    block = pl.BlockSpec((1, total, FB), lambda j: (j // per, 0, j % per))
    flat = [w for pair in weights for w in pair]
    return call(
        functools.partial(mlp_kernel, block_rows, ks, first, last, slots),
        (
            struct((nk, total, D), BF16),
            struct((nk, total, D), BF16),
            struct((total, D), F32),
            struct((total, D), F32),
            struct((4, D), F32),
        ),
        deps,
        grid=(nk * per,),
        in_specs=[SMEM, SMEM, SMEM, whole, whole, vectors, VMEM, whole, whole, vectors]
        + [ANY] * (2 * nk),
        out_specs=(block, block, whole, whole, vectors),
        scratch_shapes=[
            pltpu.VMEM((nk, D, D), BF16),
            pltpu.VMEM((nk, D, D), BF16),
            pltpu.SemaphoreType.DMA((nk, 2)),
        ],
        cost=cost(20),
    )(ids, counts, read, normed, branch, up_bias, down_bias, *state, *flat)


def put_rows(ids, value, first_row, places, store):
    rows = D // places
    for i in range(value.shape[0] // rows):
        bits = ids[1] ^ (first_row // rows + i)
        store(place_of(bits) if places > 1 else 0, value[i * rows : (i + 1) * rows])


def product_rows(ids, left, right, places, store):
    block = D // 2 if places > 1 else D
    for start in range(0, D, block):
        value = tn(left[:, start : start + block], right[...])
        put_rows(ids, value, start, places, store)


def to_give_kernel(places, count, ids, *refs):
    lefts, rights, out = refs[:count], refs[count : 2 * count], refs[2 * count]
    for i in range(count):

        def store(place, rows, i=i):
            out[i, pl.ds(place, 1)] = rows.astype(BF16)[None]

        product_rows(ids, lefts[i], rights[i], places, store)


def to_keep_kernel(places, y_first, ids, left0, right0, left2, right2, got0, got2, keep, give):
    half = max(places // 2, 1)
    for x, (left, right) in enumerate(((left0, right0), (left2, right2))):

        def store(place, rows, x=x):
            got = (got0, got2)[x]
            summed = (rows + got[pl.ds(place, 1)][0].astype(F32)).astype(BF16)[None]
            y, z = place // half, place % half
            if y_first:

                @pl.when(y == 0)
                def _():
                    keep[x, pl.ds(z, 1)] = summed

                @pl.when(y == 1)
                def _():
                    give[x, pl.ds(z, 1)] = summed
            else:
                (give if x else keep)[y, pl.ds(z, 1)] = summed

        product_rows(ids, left, right, places, store)


def column_spec(total):
    return pl.BlockSpec((total, D), lambda i: (0, 0))


def act_spec(total, index):
    return pl.BlockSpec((None, total, D), lambda i: (index, 0, 0))


def give_products(ids, pairs, specs, places, deps=()):
    count = len(pairs)
    total = pairs[0][0].shape[-2]
    rows = D // places
    return call(
        functools.partial(to_give_kernel, places, count),
        struct((count, places, rows, D), BF16),
        deps,
        grid=(1,),
        in_specs=[SMEM] + [s[0] for s in specs] + [s[1] for s in specs],
        out_specs=pl.BlockSpec((count, places, rows, D), lambda i: (0, 0, 0, 0)),
        cost=cost(6.5),
    )(ids, *[p[0] for p in pairs], *[p[1] for p in pairs])


def keep_products(ids, pairs, specs, got, index, places, y_first, deps=()):
    total = pairs[0][0].shape[-2]
    rows = D // places
    half = struct((2, max(places // 2, 1), rows, D), BF16)
    half_spec = pl.BlockSpec((2, max(places // 2, 1), rows, D), lambda i: (0, 0, 0, 0))
    return call(
        functools.partial(to_keep_kernel, places, y_first),
        (half, half),
        deps,
        grid=(1,),
        in_specs=[
            SMEM,
            specs[0][0],
            specs[0][1],
            specs[1][0],
            specs[1][1],
            pl.BlockSpec((None, places, rows, D), lambda i: (index, 0, 0, 0)),
            pl.BlockSpec((None, places, rows, D), lambda i: (index, 0, 0, 0)),
        ],
        out_specs=(half_spec, half_spec),
        cost=cost(8),
    )(ids, pairs[0][0], pairs[0][1], pairs[1][0], pairs[1][1], *got)


def first_fetch(ids, k, part, normed, mixed, grads, attn_grad, left, right, sem):
    rank = ids[0] ^ k

    @pl.when(rank < 3)
    def _():
        pltpu.make_async_copy(normed, left, sem.at[0]).start()
        pltpu.make_async_copy(grads.at[rank], right, sem.at[1]).start()

    @pl.when(rank == 3)
    def _():
        pltpu.make_async_copy(mixed, left, sem.at[0]).start()
        pltpu.make_async_copy(attn_grad.at[:, pl.ds(part * PART, PART)], right, sem.at[1]).start()


def first_give_kernel(places, part, ids, normed, mixed, grads, attn_grad, out, left, right, sem):
    ks = (1, 3)
    sources = (normed, mixed, grads, attn_grad)
    for i, k in enumerate(ks):
        first_fetch(ids, k, part, *sources, left.at[i], right.at[i], sem.at[i])
    for i, k in enumerate(ks):
        fetched(left.at[i], sem.at[i, 0])
        fetched(right.at[i], sem.at[i, 1])

        def store(place, rows, i=i):
            out[i, pl.ds(place, 1)] = rows.astype(BF16)[None]

        product_rows(ids, left.at[i], right.at[i], places, store)


def first_scratch(total):
    return [
        pltpu.VMEM((2, total, D), BF16),
        pltpu.VMEM((2, total, PART), BF16),
        pltpu.SemaphoreType.DMA((2, 2)),
    ]


def first_give(ids, part, normed, mixed, grads, attn_grad, places, deps=()):
    total = normed.shape[0]
    return call(
        functools.partial(first_give_kernel, places, part),
        struct((2, places, D // places, PART), BF16),
        deps,
        in_specs=[SMEM, ANY, ANY, ANY, ANY],
        out_specs=VMEM,
        scratch_shapes=first_scratch(total),
        cost=cost(5),
    )(ids, normed, mixed, grads, attn_grad)


def first_keep_kernel(places, part, y_first, ids, normed, mixed, grads, attn_grad, got, *refs):
    keep, give, left, right, sem = refs[-5:]
    sources = (normed, mixed, grads, attn_grad)
    for i, k in enumerate((0, 2)):
        first_fetch(ids, k, part, *sources, left.at[i], right.at[i], sem.at[i])
    for i in range(2):
        fetched(left.at[i], sem.at[i, 0])
        fetched(right.at[i], sem.at[i, 1])
    if len(refs) > 5:
        before = refs[0]
        give[:, :, :, :PART] = before[...]
        give = give.at[:, :, :, pl.ds(PART, PART)]
    to_keep_kernel(
        places, y_first, ids, left.at[0], right.at[0], left.at[1], right.at[1], got.at[0], got.at[1],
        keep, give
    )


def first_keep(
    ids, part, normed, mixed, grads, attn_grad, got, places, y_first, deps=(), before=None
):
    total = normed.shape[0]
    half = struct((2, max(places // 2, 1), D // places, PART), BF16)
    return call(
        functools.partial(first_keep_kernel, places, part, y_first),
        (half, half if before is None else struct(half.shape[:3] + (D,), BF16)),
        deps,
        in_specs=[SMEM, ANY, ANY, ANY, ANY, VMEM] + [VMEM] * (before is not None),
        out_specs=(VMEM, VMEM),
        scratch_shapes=first_scratch(total),
        cost=cost(6),
    )(ids, normed, mixed, grads, attn_grad, got, *([] if before is None else [before]))


def qkv_back_kernel(capacity, ids, grads0, grads1, *refs):
    stream, gain, after_grad, embedded, readout, sums, buffer, sem = refs[4:]
    for r in range(3):
        fetch(ids, refs[:4], r, buffer.at[r], sem.at[r])
    for r in range(3):
        fetched(buffer.at[r], sem.at[r])
    gain_sum = jnp.zeros((1, D), F32)
    bias_sum = jnp.zeros((1, D), F32)
    for start, size in chunks(stream.shape[0]):
        rows = pl.ds(start, size)
        upstream = jnp.zeros((size, D), F32)
        for r in range(3):
            grad = jnp.concatenate([grads0[r, rows, :], grads1[r, rows, :]], axis=1)
            upstream = upstream + nt(grad, buffer[r])
        xhat, rstd = normalise(stream[rows, :])
        gain_sum = gain_sum + jnp.sum(upstream * xhat, axis=0, keepdims=True)
        bias_sum = bias_sum + jnp.sum(upstream, axis=0, keepdims=True)
        total = after_grad[rows, :] + norm_input_grad(xhat, rstd, line(gain), upstream)
        inside = min(size, capacity - start)
        embedded[pl.ds(start, inside), :] = total[:inside].astype(BF16)
        if start + size > capacity:
            readout[...] = total[capacity - start : capacity - start + RD]
    sums[0:1, :] = gain_sum
    sums[1:2, :] = bias_sum


def qkv_back(ids, grads, weights, stream, gain, after_grad, deps=()):
    total = stream.shape[0]
    capacity = total - PAD
    return call(
        functools.partial(qkv_back_kernel, capacity),
        (struct((capacity, D), BF16), struct((RD, D), F32), struct((2, D), F32)),
        deps,
        in_specs=[SMEM, VMEM, VMEM] + [ANY] * 4 + [VMEM, VMEM, VMEM],
        out_specs=(VMEM, VMEM, VMEM),
        scratch_shapes=[pltpu.VMEM((3, D, D), BF16), pltpu.SemaphoreType.DMA((3,))],
        cost=cost(10),
    )(ids, *grads, *weights, stream, gain, after_grad)


def stem_back_kernel(cut, places, ids, raw, embedded, *refs):
    keep, give = refs[-4:-2], refs[-2:]
    rows = D // places // 2
    small = [part[...] for part in refs[:-4]]
    sums = [
        jnp.sum(embedded[part, :].astype(F32), axis=0, keepdims=True)
        for part in (slice(0, cut), slice(cut, None))
    ]
    small = jnp.concatenate(sums + small, axis=0)
    small = jnp.concatenate([small, jnp.zeros((SMALL - small.shape[0], D), F32)], axis=0)
    for stem, part in enumerate((slice(0, cut), slice(cut, None))):
        value = tn(raw[part, :], embedded[part, :])
        mine = (ids[0] & 1) == stem
        for i in range(2 * places):
            place = place_of(ids[1] ^ (i // 2))
            x = (i % 2) ^ (ids[0] >> 1)
            more = jnp.zeros((8, D), F32)
            if stem == 0 and 8 * i < SMALL:
                more = small[8 * i : 8 * i + 8]
            piece = jnp.concatenate([value[i * rows : (i + 1) * rows], more], axis=0)
            piece = piece.astype(BF16)[None]

            for side in range(2):

                @pl.when(mine & (x == side))
                def _():
                    keep[side][pl.ds(place, 1)] = piece

                @pl.when(jnp.logical_not(mine) & (x == side))
                def _():
                    give[side][pl.ds(place, 1)] = piece


def stem_back_plain_kernel(cut, raw, embedded, *refs):
    keep, give, out = refs[-3:]
    sums = [
        jnp.sum(embedded[part, :].astype(F32), axis=0, keepdims=True)
        for part in (slice(0, cut), slice(cut, None))
    ]
    small = jnp.concatenate(sums + [part[...] for part in refs[:-3]], axis=0)
    out[...] = jnp.concatenate([small, jnp.zeros((SMALL - small.shape[0], D), F32)], axis=0)
    keep[0] = tn(raw[:cut, :], embedded[:cut, :]).astype(BF16)
    give[0] = tn(raw[cut:, :], embedded[cut:, :]).astype(BF16)


def stem_back(ids, raw, embedded, small, places, deps=()):
    capacity = raw.shape[0]
    cut = 3 * capacity // 4
    if places == 1:
        return call(
            functools.partial(stem_back_plain_kernel, cut),
            (struct((1, D, D), BF16), struct((1, D, D), BF16), struct((SMALL, D), F32)),
            deps,
            in_specs=[VMEM, VMEM] + [VMEM] * len(small),
            out_specs=(VMEM, VMEM, VMEM),
            cost=cost(6),
        )(raw, embedded, *small)
    shape = (places, D // (2 * places) + 8, D)
    return call(
        functools.partial(stem_back_kernel, cut, places),
        (struct(shape, BF16),) * 4,
        deps,
        in_specs=[SMEM, VMEM, VMEM] + [VMEM] * len(small),
        out_specs=(VMEM,) * 4,
        cost=cost(6),
    )(ids, raw, embedded, *small)


def stem_out_kernel(ids, own, other, patch, lang, small):
    rows = own.shape[1] - 8
    for i in range(own.shape[0]):
        shard = ids[1] ^ place_bits(((i >> 2) & 1) * 4 + (i & 3), 8)
        x = (i >> 3) ^ (ids[0] >> 1)
        slot = shard * 2 + x
        at = pl.ds(pl.multiple_of(slot * rows, 16), rows)
        mine, theirs = own[i].astype(F32), other[i].astype(F32)
        first = (ids[0] & 1) == 0
        pieces = jnp.where(first, mine, theirs), jnp.where(first, theirs, mine)
        patch[at, :] = pieces[0][:rows]
        lang[at, :] = pieces[1][:rows]

        @pl.when(slot * 8 < SMALL)
        def _():
            small[pl.ds(pl.multiple_of(slot * 8, 8), 8), :] = pieces[0][rows:]


def stem_out(ids, own, other):
    return call(
        stem_out_kernel,
        (struct((D, D), F32), struct((D, D), F32), struct((SMALL, D), F32)),
        in_specs=[SMEM, VMEM, VMEM],
        out_specs=(VMEM, VMEM, VMEM),
        cost=cost(4.4),
    )(ids, own, other)


def raw_kernel(image, grad, wp, wl, out):
    @pl.when(image[0] != 0)
    def _():
        out[...] = nt(grad[...], wp[...])

    @pl.when(image[0] == 0)
    def _():
        out[...] = nt(grad[...], wl[...])


def raw_back(image, grad, wp, wl, deps=()):
    return call(
        raw_kernel,
        struct(grad.shape, F32),
        deps,
        in_specs=[SMEM, VMEM, VMEM, VMEM],
        out_specs=VMEM,
        cost=cost(4.6),
    )(image, grad, wp, wl)


def first_out_kernel(ids, k0, k2, k13, qkv, out, ranks):
    ranks[0], ranks[2], ranks[1], ranks[3] = k0[...], k2[...], k13[0], k13[1]
    for r in range(3):
        qkv[:, r * D : (r + 1) * D] = ranks[pl.ds(ids[0] ^ r, 1)][0].astype(F32)
    out[...] = ranks[pl.ds(ids[0] ^ 3, 1)][0].astype(F32)


def first_out(ids, k0, k2, k13):
    rows = k0.shape[0]
    return call(
        first_out_kernel,
        (struct((rows, 3 * D), F32), struct((rows, D), F32)),
        in_specs=[SMEM, VMEM, VMEM, VMEM],
        out_specs=(VMEM, VMEM),
        scratch_shapes=[pltpu.VMEM((4, rows, D), BF16)],
        cost=cost(2.3),
    )(ids, k0, k2, k13)


def mlp_out_kernel(places, ids, k0, k2, k13, up, down, ranks):
    ranks[0], ranks[2], ranks[1], ranks[3] = k0[...], k2[...], k13[0], k13[1]
    rows, unit = k0.shape[1], D // places
    for r in range(4):
        both = ranks[pl.ds(ids[0] ^ r, 1)][0]
        value = both[0].astype(F32)
        for s in range(places):
            start = (4 * s + r) * unit
            up[:, start : start + unit] = value[:, s * unit : (s + 1) * unit]
        down[r * rows : (r + 1) * rows, :] = both[1].astype(F32)


def mlp_out(ids, k0, k2, k13, places):
    rows = k0.shape[1]
    return call(
        functools.partial(mlp_out_kernel, places),
        (struct((rows, 4 * D), F32), struct((4 * rows, D), F32)),
        in_specs=[SMEM, VMEM, VMEM, VMEM],
        out_specs=(VMEM, VMEM),
        scratch_shapes=[pltpu.VMEM((4, 2, rows, D), BF16)],
        cost=cost(3.1),
    )(ids, k0, k2, k13)


class Grid:
    def __init__(self, mods, reps):
        self.mods, self.reps = mods, reps
        self.mod, self.rep = lax.axis_index("mod"), lax.axis_index("rep")

    def swap(self, value, mod=0, rep=0):
        pairs = [
            (m * self.reps + r, (m ^ mod) * self.reps + (r ^ rep))
            for m in range(self.mods)
            for r in range(self.reps)
        ]
        return lax.ppermute(value, AXES, pairs)


CORE, X, Y, Z0, Z1 = {"rep": 1}, {"rep": 2}, {"mod": 1}, {"mod": 2}, {"mod": 4}
Z01, XY = {"mod": 6}, {"rep": 2, "mod": 1}


def tie(value, *deps):
    return lax.optimization_barrier((value,) + deps)[0]


def joined(*parts):
    return jnp.concatenate(parts, axis=0)


def gather_z(grid, piece):
    parts = [piece] + [grid.swap(piece, **bit) for bit in (Z0, Z1, Z01)]
    return jnp.stack(parts)


def double_z(grid, piece):
    value = jnp.stack([piece, grid.swap(piece, **Z0)])
    return joined(value, grid.swap(value, **Z1))


def halve_z(grid, value):
    value = value[:2] + grid.swap(value[2:], **Z1)
    return value[0] + grid.swap(value[1], **Z0)


def reduce_z(grid, parts):
    total = parts[0]
    for part, bit in zip(parts[1:], (Z0, Z1, Z01)):
        total = total + grid.swap(part, **bit)
    return total


def per_device(
    raw_rows,
    recv_counts,
    slot_groups,
    read_counts,
    patch_convolution_weight,
    patch_stem_bias_vector,
    language_projection_weight,
    language_bias_vector,
    readout_table,
    attn_gain,
    attn_bias,
    qkv_weight,
    out_weight,
    mlp_gain,
    mlp_bias,
    up_weight,
    up_bias,
    down_weight,
    down_bias,
    out_cotangent,
):
    mods, reps = lax.axis_size("mod"), lax.axis_size("rep")
    fast = mods == 8 and reps == 4
    places = mods if fast else 1
    grid = Grid(mods, reps)
    block_rows = raw_rows.shape[1]
    capacity = mods * block_rows
    total = capacity + PAD
    slots = out_cotangent.shape[1]
    units = up_bias.shape[0] // (4 * mods)
    image = (grid.mod < 3 * mods // 4).astype(jnp.int32).reshape(1)
    rank = grid.rep if fast else jnp.zeros((), jnp.int32)
    ids = jnp.stack([rank, grid.mod if fast else jnp.zeros((), jnp.int32)]).astype(jnp.int32)
    group_row = slot_groups
    group_col = slot_groups.reshape(capacity, 1)
    marks = (recv_counts, read_counts, group_row, group_col)

    by_rank = lambda w: w.reshape(w.shape[0], -1, 4, units).transpose(2, 0, 1, 3).reshape(4, -1, D)
    up_bias_rows = up_bias.reshape(-1, 4, units).transpose(1, 0, 2).reshape(4, D)

    if fast:
        piece = lax.dynamic_slice_in_dim(
            jnp.concatenate([qkv_weight, out_weight], axis=1), rank * D, D, 1
        )
        quarter = down_weight.shape[0] // 4
        piece_up = lax.dynamic_index_in_dim(
            up_weight.reshape(-1, mods, 4, units), rank, 2, keepdims=False
        ).reshape(-1, D)
        piece_down = lax.dynamic_slice_in_dim(down_weight, rank * quarter, quarter, 0)
        first_z = gather_z(grid, piece)
        first_y = grid.swap(first_z, **Y)
        first_x = grid.swap(first_z, **X)
        up_z = gather_z(grid, tie(piece_up, first_z))
        raw_rows = tie(raw_rows, first_y, up_z)
    received = lax.all_to_all(raw_rows, "mod", split_axis=0, concat_axis=0, tiled=True)
    rows = received.reshape(capacity, D)
    branch, down_bias_grad = prepare(out_cotangent[0], recv_counts, read_counts, block_rows, total)
    if fast:
        first0 = joined(first_z, first_y)
        first2 = joined(first_x, grid.swap(first_y, **X))
        first1 = grid.swap(first0, **CORE)
        first3 = grid.swap(first2, **CORE)
        first = (first0, first1, first2, first3)
        down0 = lax.all_gather(piece_down, "mod", axis=0)
        piece_down = lax.dynamic_slice_in_dim(down_weight, (rank ^ 2) * quarter, quarter, 0)
        down2 = lax.all_gather(piece_down, "mod", axis=0)
    else:
        whole = lambda w: lax.all_gather(w, "mod", axis=0, tiled=True)
        every = jnp.concatenate([whole(qkv_weight), whole(out_weight)], axis=1)
        first = tuple(every[None, :, r * D : (r + 1) * D] for r in range(4))
        every = by_rank(whole(up_weight))
        up0, up1, up2, up3 = (every[r : r + 1] for r in range(4))
        every = whole(down_weight).reshape(mods, 4, units, D).transpose(1, 0, 2, 3)
        every = every.reshape(4, D, D)
        down0, down1, down2, down3 = (every[r : r + 1] for r in range(4))

    stream, normed = stems(
        rows,
        patch_convolution_weight,
        patch_stem_bias_vector,
        language_projection_weight,
        language_bias_vector,
        readout_table,
        attn_gain,
        attn_bias,
    )
    if fast:
        up0 = joined(up_z, grid.swap(tie(up_z, first_y), **Y))
    qkv = project_qkv(ids, normed, first)
    deps = ()
    mixed, lse, lse_read = attend(qkv, *marks, block_rows, deps)
    deps = ()
    if fast:
        down1 = grid.swap(tie(down0, up_z), **CORE)
        up2 = grid.swap(tie(up0, first1, first3), **X)
        deps = (up0, down1)
    after, normed2 = out_project(ids, mixed, first, stream, mlp_gain, mlp_bias, deps)
    deps = ()
    if fast:
        up1 = grid.swap(up0, **CORE)
        down3 = grid.swap(tie(down2, mixed), **CORE)
    sums = jnp.zeros((4, D), F32)
    step = lambda ks, state, weights, first_call, last_call, deps: mlp(
        ids, ks, recv_counts, read_counts, normed2, branch, up_bias_rows, down_bias, state,
        weights, block_rows, slots, first_call, last_call, deps,
    )
    active01, hidden01, outer, inner, sums = step(
        (0, 1), (after, after, sums), ((up0, down0), (up1, down1)), True, False, deps
    )
    spec = column_spec(total)
    at = [act_spec(total, i) for i in range(2)]
    deps = ()
    if fast:
        up3 = grid.swap(tie(up2, inner), **CORE)
    give1 = give_products(
        ids, [(normed2, hidden01), (active01, branch)], [(spec, at[1]), (at[1], spec)], places
    )
    active23, hidden23, outer, inner, sums = step(
        (2, 3), (outer, inner, sums), ((up2, down2), (up3, down3)), False, True, (give1,)
    )
    layer_out = outer[:slots].astype(BF16)[None]
    give3 = give_products(
        ids, [(normed2, hidden23), (active23, branch)], [(spec, at[1]), (at[1], spec)], places
    )
    if fast:
        got1, got3 = grid.swap(give1, **CORE), grid.swap(give3, **CORE)
    else:
        got1, got3 = jnp.zeros_like(give1), jnp.zeros_like(give3)
    after_grad, attn_grad, mixed_grad, mlp_sums = out_back(
        ids, inner, after, branch, mlp_gain, first, (give3,)
    )
    keep_down, give_down = keep_products(
        ids, [(active01, branch), (active23, branch)], [(at[0], spec)] * 2, (got1, got3), 1,
        places, False, (attn_grad,)
    )
    keep_up, give_up = keep_products(
        ids, [(normed2, hidden01), (normed2, hidden23)], [(spec, at[0])] * 2, (got1, got3), 0,
        places, True, (keep_down,)
    )
    grads_a = attend_back(
        qkv, mixed, mixed_grad, lse, lse_read, *marks, block_rows, 0, (keep_up,)
    )
    first_a13 = first_give(ids, 0, normed, mixed, grads_a, attn_grad, places)
    deps = (first_a13,)
    if fast:
        got = grid.swap(give_down, **X)
        down_y = (keep_down[0] + got[0], keep_down[1] + got[1])
        got = grid.swap(give_up, **Y)
        up_x = (keep_up[0] + got[0], keep_up[1] + got[1])
        got_a = grid.swap(first_a13, **CORE)
    else:
        got_a = jnp.zeros_like(first_a13)
    grads_b = attend_back(
        qkv, mixed, mixed_grad, lse, lse_read, *marks, block_rows, 1, deps
    )
    first_b13 = first_give(ids, 1, normed, mixed, grads_b, attn_grad, places)
    keep_a, give_a = first_keep(
        ids, 0, normed, mixed, grads_a, attn_grad, got_a, places, False, (first_b13,)
    )
    got_b = grid.swap(first_b13, **CORE) if fast else jnp.zeros_like(first_b13)
    deps = (keep_a,)
    if fast:
        got_up = grid.swap(tie(up_x[1], grads_a), **X)
        got_down = grid.swap(tie(down_y[1], grads_a), **Y)
        both = jnp.stack([up_x[0] + got_up, down_y[0] + got_down], axis=1)
        deps = deps + (both,)
    keep_b, give_b = first_keep(
        ids, 1, normed, mixed, grads_b, attn_grad, got_b, places, False, deps, give_a
    )
    embedded_grad, readout_grad, attn_sums = qkv_back(
        ids, (grads_a, grads_b), first, stream, attn_gain, after_grad, (keep_b,)
    )
    returned = lax.all_to_all(
        embedded_grad.reshape(raw_rows.shape), "mod", split_axis=0, concat_axis=0, tiled=True
    )
    small = (attn_sums, mlp_sums, down_bias_grad, sums, readout_grad)
    stem_parts = stem_back(ids, rows, embedded_grad, small, places)

    if fast:
        together = lambda *values: lax.optimization_barrier(values)
        got_z = grid.swap(both[2:], **Z1)
        got_x = grid.swap(give_b, **X)
        got = [grid.swap(give, **CORE) for give in stem_parts[2:]]
        parts = [
            stem_parts[x][4 * y : 4 * y + 4] + got[x][4 * y : 4 * y + 4]
            for x in range(2)
            for y in range(2)
        ]
        own = jnp.concatenate([keep_a[0], keep_b[0]], axis=2) + got_x[0]
        away = jnp.concatenate([keep_a[1], keep_b[1]], axis=2) + got_x[1]
        both = both[:2] + got_z
        *parts, own, away, both = together(*parts, own, away, both)
        got = [grid.swap(part, **bit) for part, bit in zip(parts[1:], (Y, X, XY))]
        parts = [parts[0][i] + got[0][i] + got[1][i] + got[2][i] for i in range(4)]
        *parts, away, own, both = together(*parts, away, own, both)
        got_both = grid.swap(both[1], **Z0)
        got_y = grid.swap(away, **Y)
        piece = reduce_z(grid, parts)
        last = own + got_y
        both = both[0] + got_both
        piece, last, both = together(piece, last, both)
        both_x = grid.swap(both, **X)
        got_z = grid.swap(last[2:], **Z1)
        piece = gather_z(grid, piece)
        last = last[:2] + got_z
        raw_grad = raw_back(
            image,
            returned.reshape(capacity, D),
            patch_convolution_weight,
            language_projection_weight,
        )
        piece, last, layer_out, both_x = together(piece, last, layer_out, both_x)
        both_core = grid.swap(jnp.stack([both, both_x]), **CORE)
        got_z = grid.swap(last[1], **Z0)
        piece = joined(piece, *[grid.swap(piece, **bit) for bit in (Y, X, XY)])
        last = last[0] + got_z
        piece, last, both_core, raw_grad = together(piece, last, both_core, raw_grad)
        up_sum, down_sum = mlp_out(ids, both, both_x, both_core, places)
        last_x = grid.swap(last, **X)
        theirs = grid.swap(piece, **CORE)
        theirs, last_x, up_sum = together(theirs, last_x, up_sum)
        last_core = grid.swap(jnp.stack([last, last_x]), **CORE)
        patch_sum, lang_sum, small = stem_out(ids, piece, theirs)
        qkv_sum, out_sum = first_out(ids, last, last_x, last_core)
    else:
        reduced = lambda v: lax.psum(
            lax.psum_scatter(v, "mod", scatter_dimension=0, tiled=True), "rep"
        ).astype(F32)
        every = []
        for keep, other, give in ((keep_a, first_a13, give_a), (keep_b, first_b13, give_b[..., PART:])):
            every.append(jnp.stack([keep[0, 0], other[0, 0], give[0, 0], other[1, 0]], axis=1))
        every = reduced(jnp.concatenate(every, axis=2).reshape(D, -1))
        qkv_sum, out_sum = every[:, : 3 * D], every[:, 3 * D :]
        every = jnp.stack([keep_up[0, 0], give1[0, 0], keep_up[1, 0], give3[0, 0]])
        every = every.reshape(4, D, mods, units).transpose(1, 2, 0, 3).reshape(D, -1)
        up_sum = reduced(every)
        every = jnp.stack([keep_down[0, 0], give1[1, 0], give_down[0, 0], give3[1, 0]])
        every = every.reshape(4, mods, units, D).transpose(1, 0, 2, 3).reshape(-1, D)
        down_sum = reduced(every)
        stem_keep, stem_give, small = stem_parts
        small = lax.psum(small, AXES)
        patch_sum = lax.psum(stem_keep[0].astype(F32), AXES)
        lang_sum = lax.psum(stem_give[0].astype(F32), AXES)
        raw_grad = raw_back(
            image,
            returned.reshape(capacity, D),
            patch_convolution_weight,
            language_projection_weight,
        )
    raw_grad = raw_grad.reshape(raw_rows.shape)
    up_bias_sum = small[7:11].reshape(4, -1, units).transpose(1, 0, 2).reshape(-1)
    return (
        layer_out,
        raw_grad,
        patch_sum,
        small[0],
        lang_sum,
        small[1],
        small[11 : 11 + RD],
        small[2],
        small[3],
        qkv_sum,
        out_sum,
        small[4],
        small[5],
        up_sum,
        up_bias_sum,
        down_sum,
        small[6],
    )


def solution(mesh):
    both, rows, rep = P("mod", "rep", None), P("mod", None), P()
    pair = P("mod", "rep")
    return jax.shard_map(
        per_device,
        mesh=mesh,
        in_specs=(both, pair, pair, pair)
        + (rep,) * 7
        + (rows, rows, rep, rep, rows, rep, rows, rep, both),
        out_specs=(both, both)
        + (rep,) * 7
        + (rows, rows, rep, rep, rows, rep, rows, rep),
        check_vma=False,
    )
```

```python
import functools

import jax
import jax.numpy as jnp
from jax import lax
from jax.experimental import pallas as pl
from jax.experimental.pallas import tpu as pltpu
from jax.sharding import PartitionSpec as P

D = 768
HEADS = 12
HD = 64
RPS = 4
RD = 8
PAD = 16
PART = D // 2
SMALL = 24
LANES = 128
CHUNK = 384
FB = 768
EPS = 1e-6
NEG = -1e30
F32 = jnp.float32
BF16 = jnp.bfloat16
AXES = ("mod", "rep")
SCALE = HD ** (-0.5)
VMEM = pl.BlockSpec(memory_space=pltpu.VMEM)
SMEM = pl.BlockSpec(memory_space=pltpu.SMEM)
ANY = pl.BlockSpec(memory_space=pl.ANY)


def nn(left, right):
    return lax.dot_general(left, right, (((1,), (0,)), ((), ())), preferred_element_type=F32)


def nt(left, right):
    return lax.dot_general(left, right, (((1,), (1,)), ((), ())), preferred_element_type=F32)


def tn(left, right):
    return lax.dot_general(left, right, (((0,), (0,)), ((), ())), preferred_element_type=F32)


def line(vector):
    return vector[...].reshape(1, -1)


def chunks(rows):
    count = rows // CHUNK
    return [
        (i * CHUNK, (rows - i * CHUNK) if i == count - 1 else CHUNK) for i in range(count)
    ]


def normalise(rows):
    mean = jnp.mean(rows, axis=-1, keepdims=True)
    centred = rows - mean
    var = jnp.mean(centred * centred, axis=-1, keepdims=True)
    rstd = lax.rsqrt(var + EPS)
    return centred * rstd, rstd


def norm_input_grad(xhat, rstd, gain, upstream):
    scaled = upstream * gain
    first = jnp.mean(scaled, axis=-1, keepdims=True)
    second = jnp.mean(scaled * xhat, axis=-1, keepdims=True)
    return rstd * (scaled - first - xhat * second)


def call(kernel, out_shape, deps=(), **kw):
    limit = kw.pop("vmem", 16)
    estimate = kw.pop("cost", None)
    in_specs = kw.pop("in_specs")
    count, more = len(in_specs), len(deps)

    def body(*refs):
        kernel(*refs[:count], *refs[count + more :])

    built = pl.pallas_call(
        body,
        out_shape=out_shape,
        in_specs=list(in_specs) + [ANY] * more,
        cost_estimate=estimate,
        compiler_params=pltpu.CompilerParams(vmem_limit_bytes=limit * 1024 * 1024),
        **kw,
    )
    return lambda *args: built(*args, *deps)


def cost(us):
    return pl.CostEstimate(flops=int(us * 1.15e9), bytes_accessed=1 << 20, transcendentals=0)


def struct(shape, dtype):
    return jax.ShapeDtypeStruct(shape, dtype)


def live_of(index, counts, read, block_rows):
    groups_n = counts.shape[1]
    capacity = groups_n * block_rows
    live = index < 0
    for s in range(groups_n):
        live = live | ((index >= s * block_rows) & (index < s * block_rows + counts[0, s]))
    slot = index - capacity
    return live | ((slot >= 0) & (slot < RD) & (slot % RPS < read[0, 0]))


def place_bits(place, places):
    if places == 1:
        return 0
    return (place >> 2) + 2 * (place & 3)


def place_of(bits):
    return ((bits & 1) << 2) | (bits >> 1)


def fetch(ids, arrays, want, target, sem):
    places, rows = arrays[0].shape[0], arrays[0].shape[1]
    for k in range(4):

        @pl.when((ids[0] ^ k) == want)
        def _():
            fetch_array(ids, arrays[k], target, sem)


def fetch_array(ids, array, target, sem, in_order=False):
    places, rows = array.shape[0], array.shape[1]
    for place in range(places):
        shard = place if in_order else ids[1] ^ place_bits(place, places)
        start = shard * rows if in_order else pl.multiple_of(shard * rows, 16)
        pltpu.make_async_copy(array.at[place], target.at[pl.ds(start, rows), :], sem).start()


def fetched(target, sem):
    pltpu.make_async_copy(target, target, sem).wait()


def stem_kernel(cut, raw, wp, bp, wl, bl, table, gain, bias, stream, normed):
    capacity = raw.shape[0]
    step = capacity // 4
    for start in range(0, capacity, step):
        weight, shift = (wp, bp) if start < cut else (wl, bl)
        rows = pl.ds(start, step)
        embedded = (nn(raw[rows, :], weight[...]) + line(shift)).astype(BF16).astype(F32)
        stream[rows, :] = embedded
        xhat, _ = normalise(embedded)
        normed[rows, :] = (xhat * line(gain) + line(bias)).astype(BF16)
    tail = jnp.concatenate([table[...], jnp.zeros((PAD - RD, D), F32)], axis=0)
    stream[pl.ds(capacity, PAD), :] = tail
    xhat, _ = normalise(tail)
    normed[pl.ds(capacity, PAD), :] = (xhat * line(gain) + line(bias)).astype(BF16)


def stems(raw, wp, bp, wl, bl, table, gain, bias):
    capacity = raw.shape[0]
    total = capacity + PAD
    return call(
        functools.partial(stem_kernel, 3 * capacity // 4),
        (struct((total, D), F32), struct((total, D), BF16)),
        in_specs=[VMEM] * 8,
        out_specs=(VMEM, VMEM),
        cost=cost(5),
    )(raw, wp, bp, wl, bl, table, gain, bias)


def qkv_kernel(ids, rows, w0, w1, w2, w3, out, buffer, sem):
    for r in range(3):
        fetch(ids, (w0, w1, w2, w3), r, buffer.at[r], sem.at[r])
    for r in range(3):
        fetched(buffer.at[r], sem.at[r])
        for start, size in chunks(rows.shape[0]):
            out[r, pl.ds(start, size), :] = nn(rows[pl.ds(start, size), :], buffer[r]).astype(BF16)


def project_qkv(ids, normed, weights, deps=()):
    total = normed.shape[0]
    return call(
        qkv_kernel,
        struct((3, total, D), BF16),
        deps,
        in_specs=[SMEM, VMEM, ANY, ANY, ANY, ANY],
        out_specs=VMEM,
        scratch_shapes=[pltpu.VMEM((3, D, D), BF16), pltpu.SemaphoreType.DMA((3,))],
        cost=cost(7),
    )(ids, normed, *weights)


def visible_readout(group_row, live_row):
    capacity = group_row.shape[1]
    query = lax.broadcasted_iota(jnp.int32, (RD, capacity), 0)
    group = 2 * (query // RPS + 1) + 1
    keys = group_row[...]
    seen = live_row & (keys <= group) & ((keys % 2 == 0) | (keys == group))
    return jnp.where(seen, 0.0, NEG)


def visible_between(read):
    query = lax.broadcasted_iota(jnp.int32, (RD, PAD), 0)
    key = lax.broadcasted_iota(jnp.int32, (RD, PAD), 1)
    live = (key < RD) & (key % RPS < read[0, 0])
    seen = (query == key) | (live & (query // RPS == key // RPS))
    return jnp.where(seen, 0.0, NEG)


def tiled(rows, heads):
    return jnp.concatenate([rows] * heads, axis=0)


def own_head(heads):
    row = lax.broadcasted_iota(jnp.int32, (heads * RD, heads * HD), 0) // RD
    lane = lax.broadcasted_iota(jnp.int32, (heads * RD, heads * HD), 1) // HD
    return row == lane


def fold_heads(stack, mine):
    kept = jnp.where(mine, stack, 0.0)
    total = kept[:RD]
    for start in range(RD, stack.shape[0], RD):
        total = total + kept[start : start + RD]
    return jnp.concatenate([total, jnp.zeros((PAD - RD, stack.shape[1]), F32)], axis=0)


def attend_kernel(
    block_rows, qkv, counts, read, group_row, group_col, mixed, lse, lse_read, mask, lse_cols, tail
):
    step = pl.program_id(0)
    capacity = group_row.shape[1]

    @pl.when(step == 0)
    def _():
        slot_row = lax.broadcasted_iota(jnp.int32, (1, capacity), 1)
        live_row = live_of(slot_row, counts, read, block_rows)
        keys = group_row[...]
        for start in range(0, capacity, CHUNK):
            query = lax.broadcasted_iota(jnp.int32, (CHUNK, capacity), 0) + start
            group = group_col[pl.ds(start, CHUNK), :]
            seen = live_row & (keys <= group) & ((keys % 2 == 0) | (keys == group))
            seen = seen | (query == slot_row)
            mask[pl.ds(start, CHUNK), :] = jnp.where(seen, 0.0, NEG)
        lse_cols[...] = jnp.zeros_like(lse_cols)
        mine = own_head(HEADS)
        tail_rows = pl.ds(capacity, PAD)
        head_rows = pl.ds(0, capacity)
        query = qkv[0, tail_rows, :].astype(F32)[:RD] * SCALE
        query = jnp.where(mine, tiled(query, HEADS), 0.0).astype(BF16)
        far = nt(query, qkv[1, head_rows, :]) + tiled(visible_readout(group_row, live_row), HEADS)
        near = nt(query, qkv[1, tail_rows, :]) + tiled(visible_between(read), HEADS)
        peak = jnp.maximum(
            jnp.max(far, axis=1, keepdims=True), jnp.max(near, axis=1, keepdims=True)
        )
        far = jnp.exp(far - peak)
        near = jnp.exp(near - peak)
        total = jnp.sum(far, axis=1, keepdims=True) + jnp.sum(near, axis=1, keepdims=True)
        out = nn(far.astype(BF16), qkv[2, head_rows, :]) + nn(
            near.astype(BF16), qkv[2, tail_rows, :]
        )
        tail[...] = fold_heads(out / total, mine)
        lse_read[...] = jnp.broadcast_to(peak + jnp.log(total), lse_read.shape)

    lane = lax.broadcasted_iota(jnp.int32, (1, LANES), 1)
    columns = pl.ds(pl.multiple_of(step * LANES, LANES), LANES)
    keys = qkv[1, pl.ds(0, capacity), columns]
    values = qkv[2, pl.ds(0, capacity), columns]
    for start in range(0, capacity, CHUNK):
        rows = pl.ds(start, CHUNK)
        query = qkv[0, rows, columns] * SCALE
        outs = []
        logs = lse_cols[rows, :]
        for head in range(2):
            chosen = jnp.where(lane // HD == head, query, jnp.zeros_like(query))
            scores = nt(chosen.astype(BF16), keys) + mask[rows, :]
            peak = jnp.max(scores, axis=1, keepdims=True)
            weight = jnp.exp(scores - peak)
            total = jnp.sum(weight, axis=1, keepdims=True)
            outs.append(nn(weight.astype(BF16), values) / total)
            logs = jnp.where(lane == 2 * step + head, peak + jnp.log(total), logs)
        mixed[rows, :] = jnp.where(lane < HD, outs[0], outs[1]).astype(BF16)
        lse_cols[rows, :] = logs
    mixed[pl.ds(capacity, PAD), :] = tail[:, columns].astype(BF16)

    @pl.when(step == pl.num_programs(0) - 1)
    def _():
        lse[...] = lse_cols[...].T[: lse.shape[0], :]


def attend(qkv, counts, read, group_row, group_col, block_rows, deps=()):
    total = qkv.shape[1]
    capacity = total - PAD
    pairs = HEADS // 2
    return call(
        functools.partial(attend_kernel, block_rows),
        (
            struct((total, D), BF16),
            struct((16, capacity), F32),
            struct((HEADS * RD, LANES), F32),
        ),
        deps,
        grid=(pairs,),
        in_specs=[VMEM, SMEM, SMEM, VMEM, VMEM],
        out_specs=(pl.BlockSpec((total, LANES), lambda j: (0, j)), VMEM, VMEM),
        scratch_shapes=[
            pltpu.VMEM((capacity, capacity), F32),
            pltpu.VMEM((capacity, LANES), F32),
            pltpu.VMEM((PAD, D), F32),
        ],
        cost=cost(21),
    )(qkv, counts, read, group_row, group_col)


def attend_back_kernel(
    block_rows,
    part,
    qkv,
    mixed,
    grad,
    lse,
    lse_read,
    counts,
    read,
    group_row,
    group_col,
    out,
    mask,
    delta,
    key_more,
    value_more,
    tails,
):
    step = pl.program_id(0)
    capacity = group_row.shape[1]
    tail_rows = pl.ds(capacity, PAD)
    head_rows = pl.ds(0, capacity)
    heads = PART // HD
    mine_columns = pl.ds(part * PART, PART)

    @pl.when(step == 0)
    def _():
        slot_row = lax.broadcasted_iota(jnp.int32, (1, capacity), 1)
        group = group_row[...]
        for start in range(0, capacity, CHUNK):
            slot = lax.broadcasted_iota(jnp.int32, (CHUNK, 1), 0) + start
            live = live_of(slot, counts, read, block_rows)
            keys = group_col[pl.ds(start, CHUNK), :]
            seen = live & (keys <= group) & ((keys % 2 == 0) | (keys == group))
            seen = seen | (slot == slot_row)
            mask[pl.ds(start, CHUNK), :] = jnp.where(seen, 0.0, NEG)
        head = lax.broadcasted_iota(jnp.int32, (8, PART), 0)
        column = lax.broadcasted_iota(jnp.int32, (8, PART), 1)
        select = jnp.where(column // HD == head, 1.0, 0.0).astype(BF16)
        for start in range(0, capacity, CHUNK):
            rows = pl.ds(start, CHUNK)
            product = grad[rows, mine_columns].astype(F32) * mixed[rows, mine_columns].astype(F32)
            high = product.astype(BF16)
            low = (product - high.astype(F32)).astype(BF16)
            delta[:, rows] = nt(select, high) + nt(select, low)

        live_row = live_of(slot_row, counts, read, block_rows)
        mine = own_head(heads)
        query = qkv[0, tail_rows, mine_columns].astype(F32)[:RD] * SCALE
        query = jnp.where(mine, tiled(query, heads), 0.0).astype(BF16)
        upper = grad[tail_rows, mine_columns].astype(F32)[:RD]
        upper = jnp.where(mine, tiled(upper, heads), 0.0)
        result = tiled(mixed[tail_rows, mine_columns].astype(F32)[:RD], heads)
        row_delta = jnp.sum(upper * result, axis=1, keepdims=True)
        upper = upper.astype(BF16)
        logs = lse_read[pl.ds(part * heads * RD, heads * RD), 0:1]
        far = nt(query, qkv[1, head_rows, mine_columns]) + tiled(visible_readout(group_row, live_row), heads)
        near = nt(query, qkv[1, tail_rows, mine_columns]) + tiled(visible_between(read), heads)
        far = jnp.exp(far - logs)
        near = jnp.exp(near - logs)
        far_grad = (far * (nt(upper, qkv[2, head_rows, mine_columns]) - row_delta)).astype(BF16)
        near_grad = (near * (nt(upper, qkv[2, tail_rows, mine_columns]) - row_delta)).astype(BF16)
        query_grad = nn(far_grad, qkv[1, head_rows, mine_columns]) + nn(near_grad, qkv[1, tail_rows, mine_columns])
        tails[0] = fold_heads(query_grad, mine) * SCALE
        tails[1] = tn(near_grad, query)
        tails[2] = tn(near.astype(BF16), upper)
        key_more[...] = tn(far_grad, query)
        value_more[...] = tn(far.astype(BF16), upper)

    lane = lax.broadcasted_iota(jnp.int32, (1, LANES), 1)
    columns = pl.ds(pl.multiple_of(step * LANES, LANES), LANES)
    here = pl.ds(pl.multiple_of(part * PART + step * LANES, LANES), LANES)
    query = (qkv[0, head_rows, here] * SCALE).astype(BF16)
    upper = grad[head_rows, here]
    query_grad = jnp.zeros((capacity, LANES), F32)
    for start in range(0, capacity, CHUNK):
        rows = pl.ds(start, CHUNK)
        all_keys = qkv[1, rows, here]
        all_values = qkv[2, rows, here]
        key_parts = []
        value_parts = []
        for head in range(2):
            own = lane // HD == head
            keys = jnp.where(own, all_keys, jnp.zeros_like(all_keys))
            values = jnp.where(own, all_values, jnp.zeros_like(all_values))
            logs = lse[pl.ds(part * heads + 2 * step + head, 1), :]
            row_delta = delta[pl.ds(2 * step + head, 1), :]
            probs = jnp.exp(nt(keys, query) + mask[rows, :] - logs)
            score_grad = (probs * (nt(values, upper) - row_delta)).astype(BF16)
            value_parts.append(nn(probs.astype(BF16), upper))
            key_parts.append(nn(score_grad, query))
            query_grad = query_grad + tn(score_grad, keys)
        key_grad = jnp.where(lane < HD, key_parts[0], key_parts[1]) + key_more[rows, columns]
        value_grad = jnp.where(lane < HD, value_parts[0], value_parts[1]) + value_more[rows, columns]
        out[1, rows, :] = key_grad.astype(BF16)
        out[2, rows, :] = value_grad.astype(BF16)
    out[0, head_rows, :] = (query_grad * SCALE).astype(BF16)
    for part in range(3):
        out[part, tail_rows, :] = tails[part, :, columns].astype(BF16)


def attend_back(
    qkv, mixed, grad, lse, lse_read, counts, read, group_row, group_col, block_rows, part,
    deps=()
):
    total = qkv.shape[1]
    capacity = total - PAD
    pairs = PART // LANES
    return call(
        functools.partial(attend_back_kernel, block_rows, part),
        struct((3, total, PART), BF16),
        deps,
        grid=(pairs,),
        in_specs=[VMEM, VMEM, VMEM, VMEM, VMEM, SMEM, SMEM, VMEM, VMEM],
        out_specs=pl.BlockSpec((3, total, LANES), lambda j: (0, 0, j)),
        scratch_shapes=[
            pltpu.VMEM((capacity, capacity), F32),
            pltpu.VMEM((8, capacity), F32),
            pltpu.VMEM((capacity, PART), F32),
            pltpu.VMEM((capacity, PART), F32),
            pltpu.VMEM((3, PAD, PART), F32),
        ],
        cost=cost(15),
    )(qkv, mixed, grad, lse, lse_read, counts, read, group_row, group_col)


def out_kernel(ids, mixed, w0, w1, w2, w3, stream, gain, bias, after, normed, buffer, sem):
    fetch(ids, (w0, w1, w2, w3), 3, buffer, sem)
    fetched(buffer, sem)
    for start, size in chunks(mixed.shape[0]):
        rows = pl.ds(start, size)
        value = stream[rows, :] + nn(mixed[rows, :], buffer[...])
        after[rows, :] = value
        xhat, _ = normalise(value)
        normed[rows, :] = (xhat * line(gain) + line(bias)).astype(BF16)


def out_project(ids, mixed, weights, stream, gain, bias, deps=()):
    total = mixed.shape[0]
    return call(
        out_kernel,
        (struct((total, D), F32), struct((total, D), BF16)),
        deps,
        in_specs=[SMEM, VMEM, ANY, ANY, ANY, ANY, VMEM, VMEM, VMEM],
        out_specs=(VMEM, VMEM),
        scratch_shapes=[pltpu.VMEM((D, D), BF16), pltpu.SemaphoreType.DMA],
        cost=cost(6.4),
    )(ids, mixed, *weights, stream, gain, bias)


def out_back_kernel(
    ids, inner, after, branch, gain, w0, w1, w2, w3, grad, grad_low, mixed_grad, sums, buffer, sem
):
    fetch(ids, (w0, w1, w2, w3), 3, buffer, sem)
    fetched(buffer, sem)
    gain_sum = jnp.zeros((1, D), F32)
    bias_sum = jnp.zeros((1, D), F32)
    for start, size in chunks(inner.shape[0]):
        rows = pl.ds(start, size)
        upstream = inner[rows, :]
        xhat, rstd = normalise(after[rows, :])
        gain_sum = gain_sum + jnp.sum(upstream * xhat, axis=0, keepdims=True)
        bias_sum = bias_sum + jnp.sum(upstream, axis=0, keepdims=True)
        total = branch[rows, :].astype(F32) + norm_input_grad(xhat, rstd, line(gain), upstream)
        grad[rows, :] = total
        low = total.astype(BF16)
        grad_low[rows, :] = low
        mixed_grad[rows, :] = nt(low, buffer[...]).astype(BF16)
    sums[0:1, :] = gain_sum
    sums[1:2, :] = bias_sum


def out_back(ids, inner, after, branch, gain, weights, deps=()):
    total = inner.shape[0]
    return call(
        out_back_kernel,
        (
            struct((total, D), F32),
            struct((total, D), BF16),
            struct((total, D), BF16),
            struct((2, D), F32),
        ),
        deps,
        in_specs=[SMEM, VMEM, VMEM, VMEM, VMEM, ANY, ANY, ANY, ANY],
        out_specs=(VMEM, VMEM, VMEM, VMEM),
        scratch_shapes=[pltpu.VMEM((D, D), BF16), pltpu.SemaphoreType.DMA],
        cost=cost(8.5),
    )(ids, inner, after, branch, gain, *weights)


def prepare_kernel(block_rows, cotangent, counts, read, branch, bias_grad):
    total, slots = branch.shape[0], cotangent.shape[0]
    index = lax.broadcasted_iota(jnp.int32, (total, 1), 0)
    live = jnp.where(live_of(index, counts, read, block_rows), 1.0, 0.0)
    upstream = cotangent[...].astype(F32) * live[:slots]
    bias_grad[...] = jnp.sum(upstream, axis=0, keepdims=True)
    upstream = jnp.concatenate([upstream, jnp.zeros((total - slots, D), F32)], axis=0)
    branch[...] = upstream.astype(BF16)


def prepare(cotangent, counts, read, block_rows, total):
    return call(
        functools.partial(prepare_kernel, block_rows),
        (struct((total, D), BF16), struct((1, D), F32)),
        in_specs=[VMEM, SMEM, SMEM],
        out_specs=(VMEM, VMEM),
        cost=cost(3),
    )(cotangent, counts, read)


def mlp_kernel(
    block_rows,
    ks,
    first,
    last,
    slots,
    *refs,
):
    nk = len(ks)
    ids, counts, read, normed, branch, up_bias, down_bias, total_in, inner_in, sums_in = refs[:10]
    weights = refs[10 : 10 + 2 * nk]
    active, hidden_grad, total, inner, sums = refs[10 + 2 * nk : 15 + 2 * nk]
    up, down, sem = refs[-3:]
    step = pl.program_id(0)
    index = step // (D // FB)
    part = step % (D // FB)
    length = normed.shape[0]

    @pl.when(step == 0)
    def _():
        for i in range(nk):
            fetch_array(ids, weights[2 * i], up.at[i], sem.at[i, 0])
            fetch_array(ids, weights[2 * i + 1], down.at[i], sem.at[i, 1], True)
        sums[...] = sums_in[...]
        if first:
            total[...] = total_in[...] + line(down_bias)
            inner[...] = jnp.zeros_like(inner)
        else:
            total[...] = total_in[...]
            inner[...] = inner_in[...]

    @pl.when(part == 0)
    def _():
        fetched(up.at[index], sem.at[index, 0])
        fetched(down.at[index], sem.at[index, 1])

    columns = pl.ds(pl.multiple_of(part * FB, FB), FB)
    rank = ids[0] ^ ks[0]
    for i in range(1, nk):
        rank = jnp.where(index == i, ids[0] ^ ks[i], rank)
    up_part = up[index, :, columns]
    down_part = down[index, columns, :]
    shift = up_bias[pl.ds(rank, 1), columns]
    bias_sum = jnp.zeros((1, FB), F32)
    for start, size in chunks(length):
        rows = pl.ds(start, size)
        hidden = nn(normed[rows, :], up_part) + shift
        factor = (2.0 / jnp.pi) ** 0.5
        square = hidden * hidden
        bent = jnp.tanh(hidden * (factor + (factor * 0.044715) * square))
        half = 0.5 * (1.0 + bent)
        act = (hidden * half).astype(BF16)
        slope = half + (0.5 * hidden) * (1.0 - bent * bent) * (
            factor + (3.0 * factor * 0.044715) * square
        )
        back = (nt(branch[rows, :], down_part) * slope).astype(BF16)
        bias_sum = bias_sum + jnp.sum(back.astype(F32), axis=0, keepdims=True)
        active[0, rows, :] = act
        hidden_grad[0, rows, :] = back
        total[rows, :] += nn(act, down_part)
        inner[rows, :] += nt(back, up_part)
    sums[pl.ds(rank, 1), columns] = bias_sum

    if last:

        @pl.when(step == pl.num_programs(0) - 1)
        def _():
            at = lax.broadcasted_iota(jnp.int32, (length, 1), 0)
            live = jnp.where(live_of(at, counts, read, block_rows), 1.0, 0.0)
            total[...] = total[...] * live


def mlp(ids, ks, counts, read, normed, branch, up_bias, down_bias, state, weights, block_rows, slots, first, last, deps=()):
    total = normed.shape[0]
    nk = len(ks)
    per = D // FB
    whole = pl.BlockSpec((total, D), lambda j: (0, 0))
    vectors = pl.BlockSpec((4, D), lambda j: (0, 0))
    block = pl.BlockSpec((1, total, FB), lambda j: (j // per, 0, j % per))
    flat = [w for pair in weights for w in pair]
    return call(
        functools.partial(mlp_kernel, block_rows, ks, first, last, slots),
        (
            struct((nk, total, D), BF16),
            struct((nk, total, D), BF16),
            struct((total, D), F32),
            struct((total, D), F32),
            struct((4, D), F32),
        ),
        deps,
        grid=(nk * per,),
        in_specs=[SMEM, SMEM, SMEM, whole, whole, vectors, VMEM, whole, whole, vectors]
        + [ANY] * (2 * nk),
        out_specs=(block, block, whole, whole, vectors),
        scratch_shapes=[
            pltpu.VMEM((nk, D, D), BF16),
            pltpu.VMEM((nk, D, D), BF16),
            pltpu.SemaphoreType.DMA((nk, 2)),
        ],
        cost=cost(20),
    )(ids, counts, read, normed, branch, up_bias, down_bias, *state, *flat)


def put_rows(ids, value, first_row, places, store):
    rows = D // places
    for i in range(value.shape[0] // rows):
        bits = ids[1] ^ (first_row // rows + i)
        store(place_of(bits) if places > 1 else 0, value[i * rows : (i + 1) * rows])


def product_rows(ids, left, right, places, store):
    block = D // 2 if places > 1 else D
    for start in range(0, D, block):
        value = tn(left[:, start : start + block], right[...])
        put_rows(ids, value, start, places, store)


def to_give_kernel(places, count, ids, *refs):
    lefts, rights, out = refs[:count], refs[count : 2 * count], refs[2 * count]
    for i in range(count):

        def store(place, rows, i=i):
            out[i, pl.ds(place, 1)] = rows.astype(BF16)[None]

        product_rows(ids, lefts[i], rights[i], places, store)


def to_keep_kernel(places, y_first, ids, left0, right0, left2, right2, got0, got2, keep, give):
    half = max(places // 2, 1)
    for x, (left, right) in enumerate(((left0, right0), (left2, right2))):

        def store(place, rows, x=x):
            got = (got0, got2)[x]
            summed = (rows + got[pl.ds(place, 1)][0].astype(F32)).astype(BF16)[None]
            y, z = place // half, place % half
            if y_first:

                @pl.when(y == 0)
                def _():
                    keep[x, pl.ds(z, 1)] = summed

                @pl.when(y == 1)
                def _():
                    give[x, pl.ds(z, 1)] = summed
            else:
                (give if x else keep)[y, pl.ds(z, 1)] = summed

        product_rows(ids, left, right, places, store)


def column_spec(total):
    return pl.BlockSpec((total, D), lambda i: (0, 0))


def act_spec(total, index):
    return pl.BlockSpec((None, total, D), lambda i: (index, 0, 0))


def give_products(ids, pairs, specs, places, deps=()):
    count = len(pairs)
    total = pairs[0][0].shape[-2]
    rows = D // places
    return call(
        functools.partial(to_give_kernel, places, count),
        struct((count, places, rows, D), BF16),
        deps,
        grid=(1,),
        in_specs=[SMEM] + [s[0] for s in specs] + [s[1] for s in specs],
        out_specs=pl.BlockSpec((count, places, rows, D), lambda i: (0, 0, 0, 0)),
        cost=cost(6.5),
    )(ids, *[p[0] for p in pairs], *[p[1] for p in pairs])


def keep_products(ids, pairs, specs, got, index, places, y_first, deps=()):
    total = pairs[0][0].shape[-2]
    rows = D // places
    half = struct((2, max(places // 2, 1), rows, D), BF16)
    half_spec = pl.BlockSpec((2, max(places // 2, 1), rows, D), lambda i: (0, 0, 0, 0))
    return call(
        functools.partial(to_keep_kernel, places, y_first),
        (half, half),
        deps,
        grid=(1,),
        in_specs=[
            SMEM,
            specs[0][0],
            specs[0][1],
            specs[1][0],
            specs[1][1],
            pl.BlockSpec((None, places, rows, D), lambda i: (index, 0, 0, 0)),
            pl.BlockSpec((None, places, rows, D), lambda i: (index, 0, 0, 0)),
        ],
        out_specs=(half_spec, half_spec),
        cost=cost(8),
    )(ids, pairs[0][0], pairs[0][1], pairs[1][0], pairs[1][1], *got)


def first_fetch(ids, k, part, normed, mixed, grads, attn_grad, left, right, sem):
    rank = ids[0] ^ k

    @pl.when(rank < 3)
    def _():
        pltpu.make_async_copy(normed, left, sem.at[0]).start()
        pltpu.make_async_copy(grads.at[rank], right, sem.at[1]).start()

    @pl.when(rank == 3)
    def _():
        pltpu.make_async_copy(mixed, left, sem.at[0]).start()
        pltpu.make_async_copy(attn_grad.at[:, pl.ds(part * PART, PART)], right, sem.at[1]).start()


def first_give_kernel(places, part, ids, normed, mixed, grads, attn_grad, out, left, right, sem):
    ks = (1, 3)
    sources = (normed, mixed, grads, attn_grad)
    for i, k in enumerate(ks):
        first_fetch(ids, k, part, *sources, left.at[i], right.at[i], sem.at[i])
    for i, k in enumerate(ks):
        fetched(left.at[i], sem.at[i, 0])
        fetched(right.at[i], sem.at[i, 1])

        def store(place, rows, i=i):
            out[i, pl.ds(place, 1)] = rows.astype(BF16)[None]

        product_rows(ids, left.at[i], right.at[i], places, store)


def first_scratch(total):
    return [
        pltpu.VMEM((2, total, D), BF16),
        pltpu.VMEM((2, total, PART), BF16),
        pltpu.SemaphoreType.DMA((2, 2)),
    ]


def first_give(ids, part, normed, mixed, grads, attn_grad, places, deps=()):
    total = normed.shape[0]
    return call(
        functools.partial(first_give_kernel, places, part),
        struct((2, places, D // places, PART), BF16),
        deps,
        in_specs=[SMEM, ANY, ANY, ANY, ANY],
        out_specs=VMEM,
        scratch_shapes=first_scratch(total),
        cost=cost(5),
    )(ids, normed, mixed, grads, attn_grad)


def first_keep_kernel(places, part, y_first, ids, normed, mixed, grads, attn_grad, got, *refs):
    keep, give, left, right, sem = refs[-5:]
    sources = (normed, mixed, grads, attn_grad)
    for i, k in enumerate((0, 2)):
        first_fetch(ids, k, part, *sources, left.at[i], right.at[i], sem.at[i])
    for i in range(2):
        fetched(left.at[i], sem.at[i, 0])
        fetched(right.at[i], sem.at[i, 1])
    if len(refs) > 5:
        before = refs[0]
        give[:, :, :, :PART] = before[...]
        give = give.at[:, :, :, pl.ds(PART, PART)]
    to_keep_kernel(
        places, y_first, ids, left.at[0], right.at[0], left.at[1], right.at[1], got.at[0], got.at[1],
        keep, give
    )


def first_keep(
    ids, part, normed, mixed, grads, attn_grad, got, places, y_first, deps=(), before=None
):
    total = normed.shape[0]
    half = struct((2, max(places // 2, 1), D // places, PART), BF16)
    return call(
        functools.partial(first_keep_kernel, places, part, y_first),
        (half, half if before is None else struct(half.shape[:3] + (D,), BF16)),
        deps,
        in_specs=[SMEM, ANY, ANY, ANY, ANY, VMEM] + [VMEM] * (before is not None),
        out_specs=(VMEM, VMEM),
        scratch_shapes=first_scratch(total),
        cost=cost(6),
    )(ids, normed, mixed, grads, attn_grad, got, *([] if before is None else [before]))


def qkv_back_kernel(capacity, ids, grads0, grads1, *refs):
    stream, gain, after_grad, embedded, readout, sums, buffer, sem = refs[4:]
    for r in range(3):
        fetch(ids, refs[:4], r, buffer.at[r], sem.at[r])
    for r in range(3):
        fetched(buffer.at[r], sem.at[r])
    gain_sum = jnp.zeros((1, D), F32)
    bias_sum = jnp.zeros((1, D), F32)
    for start, size in chunks(stream.shape[0]):
        rows = pl.ds(start, size)
        upstream = jnp.zeros((size, D), F32)
        for r in range(3):
            grad = jnp.concatenate([grads0[r, rows, :], grads1[r, rows, :]], axis=1)
            upstream = upstream + nt(grad, buffer[r])
        xhat, rstd = normalise(stream[rows, :])
        gain_sum = gain_sum + jnp.sum(upstream * xhat, axis=0, keepdims=True)
        bias_sum = bias_sum + jnp.sum(upstream, axis=0, keepdims=True)
        total = after_grad[rows, :] + norm_input_grad(xhat, rstd, line(gain), upstream)
        inside = min(size, capacity - start)
        embedded[pl.ds(start, inside), :] = total[:inside].astype(BF16)
        if start + size > capacity:
            readout[...] = total[capacity - start : capacity - start + RD]
    sums[0:1, :] = gain_sum
    sums[1:2, :] = bias_sum


def qkv_back(ids, grads, weights, stream, gain, after_grad, deps=()):
    total = stream.shape[0]
    capacity = total - PAD
    return call(
        functools.partial(qkv_back_kernel, capacity),
        (struct((capacity, D), BF16), struct((RD, D), F32), struct((2, D), F32)),
        deps,
        in_specs=[SMEM, VMEM, VMEM] + [ANY] * 4 + [VMEM, VMEM, VMEM],
        out_specs=(VMEM, VMEM, VMEM),
        scratch_shapes=[pltpu.VMEM((3, D, D), BF16), pltpu.SemaphoreType.DMA((3,))],
        cost=cost(10),
    )(ids, *grads, *weights, stream, gain, after_grad)


def stem_back_kernel(cut, places, ids, raw, embedded, *refs):
    keep, give = refs[-4:-2], refs[-2:]
    rows = D // places // 2
    small = [part[...] for part in refs[:-4]]
    sums = [
        jnp.sum(embedded[part, :].astype(F32), axis=0, keepdims=True)
        for part in (slice(0, cut), slice(cut, None))
    ]
    small = jnp.concatenate(sums + small, axis=0)
    small = jnp.concatenate([small, jnp.zeros((SMALL - small.shape[0], D), F32)], axis=0)
    for stem, part in enumerate((slice(0, cut), slice(cut, None))):
        value = tn(raw[part, :], embedded[part, :])
        mine = (ids[0] & 1) == stem
        for i in range(2 * places):
            place = place_of(ids[1] ^ (i // 2))
            x = (i % 2) ^ (ids[0] >> 1)
            more = jnp.zeros((8, D), F32)
            if stem == 0 and 8 * i < SMALL:
                more = small[8 * i : 8 * i + 8]
            piece = jnp.concatenate([value[i * rows : (i + 1) * rows], more], axis=0)
            piece = piece.astype(BF16)[None]

            for side in range(2):

                @pl.when(mine & (x == side))
                def _():
                    keep[side][pl.ds(place, 1)] = piece

                @pl.when(jnp.logical_not(mine) & (x == side))
                def _():
                    give[side][pl.ds(place, 1)] = piece


def stem_back_plain_kernel(cut, raw, embedded, *refs):
    keep, give, out = refs[-3:]
    sums = [
        jnp.sum(embedded[part, :].astype(F32), axis=0, keepdims=True)
        for part in (slice(0, cut), slice(cut, None))
    ]
    small = jnp.concatenate(sums + [part[...] for part in refs[:-3]], axis=0)
    out[...] = jnp.concatenate([small, jnp.zeros((SMALL - small.shape[0], D), F32)], axis=0)
    keep[0] = tn(raw[:cut, :], embedded[:cut, :]).astype(BF16)
    give[0] = tn(raw[cut:, :], embedded[cut:, :]).astype(BF16)


def stem_back(ids, raw, embedded, small, places, deps=()):
    capacity = raw.shape[0]
    cut = 3 * capacity // 4
    if places == 1:
        return call(
            functools.partial(stem_back_plain_kernel, cut),
            (struct((1, D, D), BF16), struct((1, D, D), BF16), struct((SMALL, D), F32)),
            deps,
            in_specs=[VMEM, VMEM] + [VMEM] * len(small),
            out_specs=(VMEM, VMEM, VMEM),
            cost=cost(6),
        )(raw, embedded, *small)
    shape = (places, D // (2 * places) + 8, D)
    return call(
        functools.partial(stem_back_kernel, cut, places),
        (struct(shape, BF16),) * 4,
        deps,
        in_specs=[SMEM, VMEM, VMEM] + [VMEM] * len(small),
        out_specs=(VMEM,) * 4,
        cost=cost(6),
    )(ids, raw, embedded, *small)


def stem_out_kernel(ids, own, other, patch, lang, small):
    rows = own.shape[1] - 8
    for i in range(own.shape[0]):
        shard = ids[1] ^ place_bits(((i >> 2) & 1) * 4 + (i & 3), 8)
        x = (i >> 3) ^ (ids[0] >> 1)
        slot = shard * 2 + x
        at = pl.ds(pl.multiple_of(slot * rows, 16), rows)
        mine, theirs = own[i].astype(F32), other[i].astype(F32)
        first = (ids[0] & 1) == 0
        pieces = jnp.where(first, mine, theirs), jnp.where(first, theirs, mine)
        patch[at, :] = pieces[0][:rows]
        lang[at, :] = pieces[1][:rows]

        @pl.when(slot * 8 < SMALL)
        def _():
            small[pl.ds(pl.multiple_of(slot * 8, 8), 8), :] = pieces[0][rows:]


def stem_out(ids, own, other):
    return call(
        stem_out_kernel,
        (struct((D, D), F32), struct((D, D), F32), struct((SMALL, D), F32)),
        in_specs=[SMEM, VMEM, VMEM],
        out_specs=(VMEM, VMEM, VMEM),
        cost=cost(4.4),
    )(ids, own, other)


def raw_kernel(image, grad, wp, wl, out):
    @pl.when(image[0] != 0)
    def _():
        out[...] = nt(grad[...], wp[...])

    @pl.when(image[0] == 0)
    def _():
        out[...] = nt(grad[...], wl[...])


def raw_back(image, grad, wp, wl, deps=()):
    return call(
        raw_kernel,
        struct(grad.shape, F32),
        deps,
        in_specs=[SMEM, VMEM, VMEM, VMEM],
        out_specs=VMEM,
        cost=cost(4.6),
    )(image, grad, wp, wl)


def first_out_kernel(ids, k0, k2, k13, qkv, out, ranks):
    ranks[0], ranks[2], ranks[1], ranks[3] = k0[...], k2[...], k13[0], k13[1]
    for r in range(3):
        qkv[:, r * D : (r + 1) * D] = ranks[pl.ds(ids[0] ^ r, 1)][0].astype(F32)
    out[...] = ranks[pl.ds(ids[0] ^ 3, 1)][0].astype(F32)


def first_out(ids, k0, k2, k13):
    rows = k0.shape[0]
    return call(
        first_out_kernel,
        (struct((rows, 3 * D), F32), struct((rows, D), F32)),
        in_specs=[SMEM, VMEM, VMEM, VMEM],
        out_specs=(VMEM, VMEM),
        scratch_shapes=[pltpu.VMEM((4, rows, D), BF16)],
        cost=cost(2.3),
    )(ids, k0, k2, k13)


def mlp_out_kernel(places, ids, k0, k2, k13, up, down, ranks):
    ranks[0], ranks[2], ranks[1], ranks[3] = k0[...], k2[...], k13[0], k13[1]
    rows, unit = k0.shape[1], D // places
    for r in range(4):
        both = ranks[pl.ds(ids[0] ^ r, 1)][0]
        value = both[0].astype(F32)
        for s in range(places):
            start = (4 * s + r) * unit
            up[:, start : start + unit] = value[:, s * unit : (s + 1) * unit]
        down[r * rows : (r + 1) * rows, :] = both[1].astype(F32)


def mlp_out(ids, k0, k2, k13, places):
    rows = k0.shape[1]
    return call(
        functools.partial(mlp_out_kernel, places),
        (struct((rows, 4 * D), F32), struct((4 * rows, D), F32)),
        in_specs=[SMEM, VMEM, VMEM, VMEM],
        out_specs=(VMEM, VMEM),
        scratch_shapes=[pltpu.VMEM((4, 2, rows, D), BF16)],
        cost=cost(3.1),
    )(ids, k0, k2, k13)


class Grid:
    def __init__(self, mods, reps):
        self.mods, self.reps = mods, reps
        self.mod, self.rep = lax.axis_index("mod"), lax.axis_index("rep")

    def swap(self, value, mod=0, rep=0):
        pairs = [
            (m * self.reps + r, (m ^ mod) * self.reps + (r ^ rep))
            for m in range(self.mods)
            for r in range(self.reps)
        ]
        return lax.ppermute(value, AXES, pairs)


CORE, X, Y, Z0, Z1 = {"rep": 1}, {"rep": 2}, {"mod": 1}, {"mod": 2}, {"mod": 4}
Z01, XY = {"mod": 6}, {"rep": 2, "mod": 1}


def tie(value, *deps):
    return lax.optimization_barrier((value,) + deps)[0]


def joined(*parts):
    return jnp.concatenate(parts, axis=0)


def gather_z(grid, piece):
    parts = [piece] + [grid.swap(piece, **bit) for bit in (Z0, Z1, Z01)]
    return jnp.stack(parts)


def double_z(grid, piece):
    value = jnp.stack([piece, grid.swap(piece, **Z0)])
    return joined(value, grid.swap(value, **Z1))


def halve_z(grid, value):
    value = value[:2] + grid.swap(value[2:], **Z1)
    return value[0] + grid.swap(value[1], **Z0)


def reduce_z(grid, parts):
    total = parts[0]
    for part, bit in zip(parts[1:], (Z0, Z1, Z01)):
        total = total + grid.swap(part, **bit)
    return total


def per_device(
    raw_rows,
    recv_counts,
    slot_groups,
    read_counts,
    patch_convolution_weight,
    patch_stem_bias_vector,
    language_projection_weight,
    language_bias_vector,
    readout_table,
    attn_gain,
    attn_bias,
    qkv_weight,
    out_weight,
    mlp_gain,
    mlp_bias,
    up_weight,
    up_bias,
    down_weight,
    down_bias,
    out_cotangent,
):
    mods, reps = lax.axis_size("mod"), lax.axis_size("rep")
    fast = mods == 8 and reps == 4
    places = mods if fast else 1
    grid = Grid(mods, reps)
    block_rows = raw_rows.shape[1]
    capacity = mods * block_rows
    total = capacity + PAD
    slots = out_cotangent.shape[1]
    units = up_bias.shape[0] // (4 * mods)
    image = (grid.mod < 3 * mods // 4).astype(jnp.int32).reshape(1)
    rank = grid.rep if fast else jnp.zeros((), jnp.int32)
    ids = jnp.stack([rank, grid.mod if fast else jnp.zeros((), jnp.int32)]).astype(jnp.int32)
    group_row = slot_groups
    group_col = slot_groups.reshape(capacity, 1)
    marks = (recv_counts, read_counts, group_row, group_col)

    by_rank = lambda w: w.reshape(w.shape[0], -1, 4, units).transpose(2, 0, 1, 3).reshape(4, -1, D)
    up_bias_rows = up_bias.reshape(-1, 4, units).transpose(1, 0, 2).reshape(4, D)

    if fast:
        piece = lax.dynamic_slice_in_dim(
            jnp.concatenate([qkv_weight, out_weight], axis=1), rank * D, D, 1
        )
        quarter = down_weight.shape[0] // 4
        piece_up = lax.dynamic_index_in_dim(
            up_weight.reshape(-1, mods, 4, units), rank, 2, keepdims=False
        ).reshape(-1, D)
        piece_down = lax.dynamic_slice_in_dim(down_weight, rank * quarter, quarter, 0)
        first_z = gather_z(grid, piece)
        first_y = grid.swap(first_z, **Y)
        first_x = grid.swap(first_z, **X)
        up_z = gather_z(grid, tie(piece_up, first_z))
        raw_rows = tie(raw_rows, first_y)
    received = lax.all_to_all(raw_rows, "mod", split_axis=0, concat_axis=0, tiled=True)
    rows = received.reshape(capacity, D)
    branch, down_bias_grad = prepare(out_cotangent[0], recv_counts, read_counts, block_rows, total)
    if fast:
        first0 = joined(first_z, first_y)
        first2 = joined(first_x, grid.swap(first_y, **X))
        first1 = grid.swap(first0, **CORE)
        first3 = grid.swap(first2, **CORE)
        first = (first0, first1, first2, first3)
        down0 = lax.all_gather(piece_down, "mod", axis=0)
        piece_down = lax.dynamic_slice_in_dim(down_weight, (rank ^ 2) * quarter, quarter, 0)
        down2 = lax.all_gather(piece_down, "mod", axis=0)
    else:
        whole = lambda w: lax.all_gather(w, "mod", axis=0, tiled=True)
        every = jnp.concatenate([whole(qkv_weight), whole(out_weight)], axis=1)
        first = tuple(every[None, :, r * D : (r + 1) * D] for r in range(4))
        every = by_rank(whole(up_weight))
        up0, up1, up2, up3 = (every[r : r + 1] for r in range(4))
        every = whole(down_weight).reshape(mods, 4, units, D).transpose(1, 0, 2, 3)
        every = every.reshape(4, D, D)
        down0, down1, down2, down3 = (every[r : r + 1] for r in range(4))

    stream, normed = stems(
        rows,
        patch_convolution_weight,
        patch_stem_bias_vector,
        language_projection_weight,
        language_bias_vector,
        readout_table,
        attn_gain,
        attn_bias,
    )
    if fast:
        up0 = joined(up_z, grid.swap(tie(up_z, first_y), **Y))
    qkv = project_qkv(ids, normed, first)
    deps = ()
    mixed, lse, lse_read = attend(qkv, *marks, block_rows, deps)
    deps = ()
    if fast:
        down1 = grid.swap(tie(down0, up_z), **CORE)
        up2 = grid.swap(tie(up0, first1, first3), **X)
        deps = (up0, down1)
    after, normed2 = out_project(ids, mixed, first, stream, mlp_gain, mlp_bias, deps)
    deps = ()
    if fast:
        up1 = grid.swap(up0, **CORE)
        down3 = grid.swap(tie(down2, mixed), **CORE)
    sums = jnp.zeros((4, D), F32)
    step = lambda ks, state, weights, first_call, last_call, deps: mlp(
        ids, ks, recv_counts, read_counts, normed2, branch, up_bias_rows, down_bias, state,
        weights, block_rows, slots, first_call, last_call, deps,
    )
    active01, hidden01, outer, inner, sums = step(
        (0, 1), (after, after, sums), ((up0, down0), (up1, down1)), True, False, deps
    )
    spec = column_spec(total)
    at = [act_spec(total, i) for i in range(2)]
    deps = ()
    if fast:
        up3 = grid.swap(tie(up2, inner), **CORE)
    give1 = give_products(
        ids, [(normed2, hidden01), (active01, branch)], [(spec, at[1]), (at[1], spec)], places
    )
    active23, hidden23, outer, inner, sums = step(
        (2, 3), (outer, inner, sums), ((up2, down2), (up3, down3)), False, True, (give1,)
    )
    layer_out = outer[:slots].astype(BF16)[None]
    give3 = give_products(
        ids, [(normed2, hidden23), (active23, branch)], [(spec, at[1]), (at[1], spec)], places
    )
    if fast:
        got1, got3 = grid.swap(give1, **CORE), grid.swap(give3, **CORE)
    else:
        got1, got3 = jnp.zeros_like(give1), jnp.zeros_like(give3)
    after_grad, attn_grad, mixed_grad, mlp_sums = out_back(
        ids, inner, after, branch, mlp_gain, first, (give3,)
    )
    keep_down, give_down = keep_products(
        ids, [(active01, branch), (active23, branch)], [(at[0], spec)] * 2, (got1, got3), 1,
        places, False, (attn_grad,)
    )
    keep_up, give_up = keep_products(
        ids, [(normed2, hidden01), (normed2, hidden23)], [(spec, at[0])] * 2, (got1, got3), 0,
        places, True, (keep_down,)
    )
    grads_a = attend_back(
        qkv, mixed, mixed_grad, lse, lse_read, *marks, block_rows, 0, (keep_up,)
    )
    first_a13 = first_give(ids, 0, normed, mixed, grads_a, attn_grad, places)
    deps = (first_a13,)
    if fast:
        got = grid.swap(give_down, **X)
        down_y = (keep_down[0] + got[0], keep_down[1] + got[1])
        got = grid.swap(give_up, **Y)
        up_x = (keep_up[0] + got[0], keep_up[1] + got[1])
        got_a = grid.swap(first_a13, **CORE)
    else:
        got_a = jnp.zeros_like(first_a13)
    grads_b = attend_back(
        qkv, mixed, mixed_grad, lse, lse_read, *marks, block_rows, 1, deps
    )
    first_b13 = first_give(ids, 1, normed, mixed, grads_b, attn_grad, places)
    keep_a, give_a = first_keep(
        ids, 0, normed, mixed, grads_a, attn_grad, got_a, places, False, (first_b13,)
    )
    got_b = grid.swap(first_b13, **CORE) if fast else jnp.zeros_like(first_b13)
    deps = (keep_a,)
    if fast:
        got_up = grid.swap(tie(up_x[1], grads_a), **X)
        got_down = grid.swap(tie(down_y[1], grads_a), **Y)
        both = jnp.stack([up_x[0] + got_up, down_y[0] + got_down], axis=1)
        deps = deps + (both,)
    keep_b, give_b = first_keep(
        ids, 1, normed, mixed, grads_b, attn_grad, got_b, places, False, deps, give_a
    )
    embedded_grad, readout_grad, attn_sums = qkv_back(
        ids, (grads_a, grads_b), first, stream, attn_gain, after_grad, (keep_b,)
    )
    returned = lax.all_to_all(
        embedded_grad.reshape(raw_rows.shape), "mod", split_axis=0, concat_axis=0, tiled=True
    )
    small = (attn_sums, mlp_sums, down_bias_grad, sums, readout_grad)
    stem_parts = stem_back(ids, rows, embedded_grad, small, places)

    if fast:
        together = lambda *values: lax.optimization_barrier(values)
        got_z = grid.swap(both[2:], **Z1)
        got_x = grid.swap(give_b, **X)
        got = [grid.swap(give, **CORE) for give in stem_parts[2:]]
        parts = [
            stem_parts[x][4 * y : 4 * y + 4] + got[x][4 * y : 4 * y + 4]
            for x in range(2)
            for y in range(2)
        ]
        own = jnp.concatenate([keep_a[0], keep_b[0]], axis=2) + got_x[0]
        away = jnp.concatenate([keep_a[1], keep_b[1]], axis=2) + got_x[1]
        both = both[:2] + got_z
        *parts, own, away, both = together(*parts, own, away, both)
        got = [grid.swap(part, **bit) for part, bit in zip(parts[1:], (Y, X, XY))]
        parts = [parts[0][i] + got[0][i] + got[1][i] + got[2][i] for i in range(4)]
        *parts, away, own, both = together(*parts, away, own, both)
        got_both = grid.swap(both[1], **Z0)
        got_y = grid.swap(away, **Y)
        piece = reduce_z(grid, parts)
        last = own + got_y
        both = both[0] + got_both
        piece, last, both = together(piece, last, both)
        both_x = grid.swap(both, **X)
        got_z = grid.swap(last[2:], **Z1)
        piece = gather_z(grid, piece)
        last = last[:2] + got_z
        raw_grad = raw_back(
            image,
            returned.reshape(capacity, D),
            patch_convolution_weight,
            language_projection_weight,
        )
        piece, last, layer_out, both_x = together(piece, last, layer_out, both_x)
        both_core = grid.swap(jnp.stack([both, both_x]), **CORE)
        got_z = grid.swap(last[1], **Z0)
        piece = joined(piece, *[grid.swap(piece, **bit) for bit in (Y, X, XY)])
        last = last[0] + got_z
        piece, last, both_core, raw_grad = together(piece, last, both_core, raw_grad)
        up_sum, down_sum = mlp_out(ids, both, both_x, both_core, places)
        last_x = grid.swap(last, **X)
        theirs = grid.swap(piece, **CORE)
        theirs, last_x, up_sum = together(theirs, last_x, up_sum)
        last_core = grid.swap(jnp.stack([last, last_x]), **CORE)
        patch_sum, lang_sum, small = stem_out(ids, piece, theirs)
        qkv_sum, out_sum = first_out(ids, last, last_x, last_core)
    else:
        reduced = lambda v: lax.psum(
            lax.psum_scatter(v, "mod", scatter_dimension=0, tiled=True), "rep"
        ).astype(F32)
        every = []
        for keep, other, give in ((keep_a, first_a13, give_a), (keep_b, first_b13, give_b[..., PART:])):
            every.append(jnp.stack([keep[0, 0], other[0, 0], give[0, 0], other[1, 0]], axis=1))
        every = reduced(jnp.concatenate(every, axis=2).reshape(D, -1))
        qkv_sum, out_sum = every[:, : 3 * D], every[:, 3 * D :]
        every = jnp.stack([keep_up[0, 0], give1[0, 0], keep_up[1, 0], give3[0, 0]])
        every = every.reshape(4, D, mods, units).transpose(1, 2, 0, 3).reshape(D, -1)
        up_sum = reduced(every)
        every = jnp.stack([keep_down[0, 0], give1[1, 0], give_down[0, 0], give3[1, 0]])
        every = every.reshape(4, mods, units, D).transpose(1, 0, 2, 3).reshape(-1, D)
        down_sum = reduced(every)
        stem_keep, stem_give, small = stem_parts
        small = lax.psum(small, AXES)
        patch_sum = lax.psum(stem_keep[0].astype(F32), AXES)
        lang_sum = lax.psum(stem_give[0].astype(F32), AXES)
        raw_grad = raw_back(
            image,
            returned.reshape(capacity, D),
            patch_convolution_weight,
            language_projection_weight,
        )
    raw_grad = raw_grad.reshape(raw_rows.shape)
    up_bias_sum = small[7:11].reshape(4, -1, units).transpose(1, 0, 2).reshape(-1)
    return (
        layer_out,
        raw_grad,
        patch_sum,
        small[0],
        lang_sum,
        small[1],
        small[11 : 11 + RD],
        small[2],
        small[3],
        qkv_sum,
        out_sum,
        small[4],
        small[5],
        up_sum,
        up_bias_sum,
        down_sum,
        small[6],
    )


def solution(mesh):
    both, rows, rep = P("mod", "rep", None), P("mod", None), P()
    pair = P("mod", "rep")
    return jax.shard_map(
        per_device,
        mesh=mesh,
        in_specs=(both, pair, pair, pair)
        + (rep,) * 7
        + (rows, rows, rep, rep, rows, rep, rows, rep, both),
        out_specs=(both, both)
        + (rep,) * 7
        + (rows, rows, rep, rep, rows, rep, rows, rep),
        check_vma=False,
    )
```
